32 devices in a mesh: lat: 4 (over z), lon: 8 (over y, x, core).
Axes of the slice: x: 2, y: 2, z: 4, core: 2. Of those that a mesh axis runs over, the one named last changes fastest.
Arguments:
- state_field: bfloat16 [96, 512, 640], P('lat', 'lon'), may hold values from -6 to 6
- filters: float32 [96, 5, 5, 9], P('lat'), may hold values from -0.9 to 0.9
- band_edges: int32 [96, 2], P('lat'), may hold values from 0 to 96, as said below
- basis_mask: int32 [96, 5], P('lat'), may hold values 0 or 1
- weights_one: float32 [5, 640], replicated, may hold values from -2.5 to 2.5
- weights_two: float32 [5, 640], replicated, may hold values from -2.5 to 2.5
Outputs:
- mixed_field: bfloat16 [96, 512, 640], P('lat', 'lon')
The draws below stay inside these ranges and needn't reach their ends.
Inputs may be any that keep to these rules, and one draw needn't show every extreme that they name: For each row y, max(y - 2, 0) <= band_edges[y,0] <= max(y - 1, 0) and min(y + 2, 96) <= band_edges[y,1] <= min(y + 3, 96); some row's band spans from y - 2 to y + 3.
All inputs are finite; a program needn't handle non-finite values. No bound on the sum of `basis_mask` on one device may be relied on, other than what follows from the above.
Results may differ from the reference program's by a relative error of at most 0.0049.
Values may be sent and summed in bfloat16 or wider, within the bound.
No kernel may reach another device: no remote copies, remote signals or barrier semaphores. Data moves between devices by JAX's collectives and lax.ppermute only.
A program may use at most 64 MiB of HBM per device.

```python
import jax
import jax.numpy as jnp
from jax import lax

CHANNELS = 640
BASES = 5
LAT_REACH = 2
LON_REACH = 4
NLAT = 96
NLON = 512


def draw_band_edges(key, part):
    base = jax.random.fold_in(key, 11)
    key_below, key_above, key_full = jax.random.split(base, 3)
    latitude = jnp.arange(NLAT, dtype=jnp.int32)
    below = jax.random.randint(key_below, (NLAT,), 1, LAT_REACH + 1, dtype=jnp.int32)
    above = jax.random.randint(key_above, (NLAT,), 1, LAT_REACH + 1, dtype=jnp.int32)
    chosen = jax.random.randint(key_full, (), LAT_REACH, NLAT - LAT_REACH, dtype=jnp.int32)
    picked = latitude == chosen
    below = jnp.where(picked, LAT_REACH, below)
    above = jnp.where(picked, LAT_REACH, above)
    start_row = jnp.maximum(latitude - below, 0)
    end_row = jnp.minimum(latitude + 1 + above, NLAT)
    return jnp.stack([start_row, end_row], axis=1).astype(jnp.int32)


def place_ends(result, stream_key, smallest, top_value):
    longest = result.shape.index(max(result.shape))
    spots = []
    for shift in (0, 1):
        where = [jax.random.randint(jax.random.fold_in(stream_key, axis), (), 0, length) for axis, length in enumerate(result.shape)]
        where[longest] = (where[longest] + shift) % result.shape[longest]
        spots.append(tuple(where))
    return result.at[spots[0]].set(smallest).at[spots[1]].set(top_value)


def block_scale(own_key, shape, shards, least, top_value):
    loudness = 1.0
    for axis_at, shards_of in shards:
        heights = jax.random.uniform(jax.random.fold_in(jax.random.fold_in(own_key, 6), axis_at), (shards_of,), jnp.float32, least / len(shards), top_value / len(shards))
        loudness = loudness * jnp.repeat(jnp.exp(heights), shape[axis_at] // shards_of).reshape((-1,) + (1,) * (len(shape) - 1 - axis_at))
    return loudness


def gaussian(rng, dims, deviation, reach, shards=(), held_as=jnp.bfloat16):
    result = deviation * jax.random.normal(rng, dims, jnp.float32)
    if shards:
        result = result * block_scale(rng, dims, shards, -0.22, 0.18)
    return jnp.clip(result, -reach, reach).astype(held_as)


def setup_inputs(seed: int = 0) -> dict:
    key_of = jax.random.split(jax.random.key(seed), 7)
    return {
        "state_field": gaussian(key_of[0], (NLAT, NLON, CHANNELS), 1.0, 6.0, ((0, 4), (1, 8))),
        "filters": gaussian(key_of[1], (NLAT, BASES, 2 * LAT_REACH + 1, 2 * LON_REACH + 1), 0.15, 0.9, ((0, 4),), jnp.float32),
        "band_edges": draw_band_edges(jax.random.fold_in(key_of[6], 71), 0),
        "basis_mask": place_ends((jax.random.randint(key_of[3], (NLAT, BASES), 0, 5) < 4).astype(jnp.int32), jax.random.fold_in(key_of[3], 1), 0, 1),
        "weights_one": gaussian(key_of[4], (BASES, CHANNELS), BASES ** -0.5, 2.5, (), jnp.float32),
        "weights_two": gaussian(key_of[5], (BASES, CHANNELS), BASES ** -0.5, 2.5, (), jnp.float32),
    }


def build_filter(filters, band_edges, basis_mask):
    latitude = jnp.arange(filters.shape[0], dtype=jnp.int32)
    source = latitude[:, None] + jnp.arange(2 * LAT_REACH + 1, dtype=jnp.int32)[None, :] - LAT_REACH
    inside = (source >= band_edges[:, 0:1]) & (source < band_edges[:, 1:2])
    return filters * inside.astype(filters.dtype)[:, None, :, None] * basis_mask.astype(filters.dtype)[:, :, None, None]


def convolve(field_in, kernel, weights):
    coefficients = jnp.einsum("ykdm,kc->ydmc", kernel, weights, precision=lax.Precision.HIGHEST)
    padded = jnp.pad(field_in.astype(jnp.float32), ((LAT_REACH, LAT_REACH), (0, 0), (0, 0)))

    def one_row(latitude):
        window = lax.dynamic_slice_in_dim(padded, latitude, 2 * LAT_REACH + 1, 0)
        row_coef = lax.dynamic_index_in_dim(coefficients, latitude, 0, keepdims=False)
        running = jnp.zeros(window.shape[1:], jnp.float32)
        for offset in range(2 * LAT_REACH + 1):
            for lon_lag in range(2 * LON_REACH + 1):
                running = running + row_coef[offset, lon_lag][None, :] * jnp.roll(window[offset], LON_REACH - lon_lag, axis=0)
        return running

    return lax.map(one_row, jnp.arange(NLAT, dtype=jnp.int32))


def reference(state_field, filters, band_edges, basis_mask, weights_one, weights_two):
    kernel = build_filter(filters, band_edges, basis_mask)
    hidden = jax.nn.gelu(convolve(state_field, kernel, weights_one), approximate=False).astype(jnp.bfloat16)
    return convolve(hidden, kernel, weights_two).astype(jnp.bfloat16)
```

```python
import functools

import jax
import jax.numpy as jnp
from jax import lax
from jax.experimental import pallas as pl
from jax.experimental.pallas import tpu as pltpu
from jax.sharding import PartitionSpec as P

LAT_REACH = 2
LON_REACH = 4
CELLS = 8
WINDOW = CELLS + 2 * LON_REACH
LANES = 128
BANDS = 2 * LAT_REACH + 1

ERF_SERIES = (
    1.5957685368174537,
    0.2906731929485398,
    -0.0010568544789619305,
    -0.007074993444558666,
    0.0020347241919514126,
    -0.00027398798106634774,
    1.4859691157006145e-05,
)


def shift_pair(axis, wrap):
    peers = lax.axis_size(axis)
    up = [(i, (i + 1) % peers) for i in range(peers if wrap else peers - 1)]
    return up, [(j, i) for i, j in up]


def masked_filter(filters, band_edges, basis_mask):
    rows = filters.shape[0]
    latitude = lax.axis_index("lat") * rows + jnp.arange(rows, dtype=jnp.int32)
    source = latitude[:, None] + jnp.arange(BANDS, dtype=jnp.int32)[None, :] - LAT_REACH
    inside = (source >= band_edges[:, 0:1]) & (source < band_edges[:, 1:2])
    keep = inside[:, None, :] & (basis_mask != 0)[:, :, None]
    return jnp.where(keep[..., None], filters, 0.0)


def band_rows(kernel):
    rows, bases, bands, lags = kernel.shape
    spaced = jnp.pad(kernel, ((0, 0), (0, 0), (0, 0), (0, WINDOW - lags)))
    spaced = spaced.reshape(rows, bases, bands * WINDOW)
    return jnp.pad(spaced, ((0, 0), (0, 8 - bases), (0, 2 * LANES - bands * WINDOW)))


def erf_gelu(half):
    square = half * half
    series = jnp.full_like(square, ERF_SERIES[-1])
    for term in ERF_SERIES[-2::-1]:
        series = series * square + term
    return half + half * jnp.tanh(half * series)


def block_kernel(
    block, x_ref, low_ref, high_ref, left_ref, right_ref, band_ref, one_ref, two_ref,
    out_ref, toeplitz, rim_toeplitz, extended, hidden,
):
    rows, cells = x_ref.shape[0], x_ref.shape[1]
    bases = one_ref.shape[0]
    group = bases * CELLS
    reach = 2 * LAT_REACH
    blocks = rows // block
    depth = (block + reach) * WINDOW
    rim_rows = LAT_REACH + reach

    def toeplitz_rows(row, place):
        parts = []
        for basis in range(bases):
            line = jnp.broadcast_to(band_ref[row, basis : basis + 1, :], (CELLS, 2 * LANES))
            parts.append(pltpu.roll(line, place * WINDOW, 1, stride=1, stride_axis=0))
        return parts

    @pl.when(pl.program_id(0) == 0)
    def _():
        for row in range(0, rows, 2):
            inner = row % block
            parts = toeplitz_rows(row + LAT_REACH, inner) + toeplitz_rows(row + LAT_REACH + 1, inner + 1)
            toeplitz[row * group : (row + 2) * group, :] = jnp.concatenate(parts, 0).astype(jnp.bfloat16)
        for side in range(2):
            row = side * (rows + LAT_REACH)
            place = side * rim_rows
            parts = toeplitz_rows(row, place) + toeplitz_rows(row + 1, place + 1)
            at = side * LAT_REACH * group
            rim_toeplitz[at : at + LAT_REACH * group, :] = jnp.concatenate(parts, 0).astype(jnp.bfloat16)

    f32 = jnp.float32
    extended[reach : reach + rows, CELLS : CELLS + cells, :] = x_ref[...].astype(f32)
    extended[:reach, CELLS : CELLS + cells, :] = low_ref[...].astype(f32)
    extended[reach + rows :, CELLS : CELLS + cells, :] = high_ref[...].astype(f32)
    extended[:, :CELLS, :] = left_ref[...].astype(f32)
    extended[:, CELLS + cells :, :] = right_ref[...].astype(f32)

    def pair_lanes(value):
        return jnp.concatenate([value, value], axis=-1)

    one = [pair_lanes(one_ref[k : k + 1, :]) * 0.5 for k in range(bases)]
    two = [pair_lanes(two_ref[k : k + 1, :]) for k in range(bases)]

    def window(ref, spans, at):
        tall = [ref[a:b, at : at + WINDOW, :].astype(jnp.bfloat16) for a, b in spans]
        tall = tall[0] if len(tall) == 1 else jnp.concatenate(tall, 0)
        return tall.reshape(tall.shape[0] * WINDOW, LANES)

    def product(matrix, ref, spans, at, weights):
        wide = jnp.concatenate([window(ref, spans, a) for a in at], axis=1)
        result = jnp.dot(matrix, wide, preferred_element_type=f32)
        result = result.reshape(result.shape[0] // group, bases, CELLS, wide.shape[1])
        total = result[:, 0] * weights[0][:, : wide.shape[1]]
        for k in range(1, bases):
            total = total + result[:, k] * weights[k][:, : wide.shape[1]]
        return total

    columns = cells // CELLS + 1
    for first in range(0, columns, 2):
        at = [c * CELLS for c in range(first, min(first + 2, columns))]
        for part in range(blocks + 1):
            if part < blocks:
                matrix = toeplitz[part * block * group : (part + 1) * block * group, :depth]
                start = LAT_REACH + part * block
                spans = [(start, start + block + reach)]
            else:
                matrix = rim_toeplitz[:, : 2 * rim_rows * WINDOW]
                spans = [(0, rim_rows), (rows + 2 * reach - rim_rows, rows + 2 * reach)]
            value = erf_gelu(product(matrix, extended, spans, at, one))
            for i, a in enumerate(at):
                piece = value[:, :, i * LANES : (i + 1) * LANES]
                if part < blocks:
                    hidden[start : start + block, a : a + CELLS, :] = piece
                else:
                    hidden[:LAT_REACH, a : a + CELLS, :] = piece[:LAT_REACH]
                    hidden[rows + LAT_REACH :, a : a + CELLS, :] = piece[LAT_REACH:]
    for first in range(0, cells // CELLS, 2):
        at = [first * CELLS, (first + 1) * CELLS]
        for part in range(blocks):
            matrix = toeplitz[part * block * group : (part + 1) * block * group, :depth]
            start = part * block
            value = product(matrix, hidden, [(start, start + block + reach)], at, two)
            value = jnp.concatenate([value[:, :, :LANES], value[:, :, LANES:]], axis=1)
            out_ref[start : start + block, at[0] : at[0] + 2 * CELLS, :] = value.astype(out_ref.dtype)


def per_device(state_field, filters, band_edges, basis_mask, weights_one, weights_two):
    rows, cells, channels = state_field.shape
    bases = filters.shape[1]
    reach = 2 * LAT_REACH
    group = bases * CELLS
    block = max(
        b for b in range(2, rows + 1, 2) if rows % b == 0 and (b + reach) * WINDOW <= 2 * LANES
    )

    north, south = shift_pair("lat", False)
    east, west = shift_pair("lon", True)
    low = lax.ppermute(state_field[-reach:], "lat", north)
    high = lax.ppermute(state_field[:reach], "lat", south)
    kernel = masked_filter(filters, band_edges, basis_mask).astype(jnp.bfloat16)
    kernel_low = lax.ppermute(kernel[-LAT_REACH:], "lat", north)
    kernel_high = lax.ppermute(kernel[:LAT_REACH], "lat", south)
    bands = band_rows(jnp.concatenate([kernel_low, kernel, kernel_high], 0).astype(jnp.float32))

    width = 2 * LON_REACH
    left = jnp.concatenate([low[:, -width:], state_field[:, -width:], high[:, -width:]], 0)
    right = jnp.concatenate([low[:, :width], state_field[:, :width], high[:, :width]], 0)
    left = lax.ppermute(left, "lon", east)
    right = lax.ppermute(right, "lon", west)

    def chunked(array):
        lead = array.shape[:-1]
        return pl.BlockSpec(lead + (LANES,), lambda c: (0,) * len(lead) + (c,))

    operands = (state_field, low, high, left, right)
    flops = 2 * (rows * 2 + 2 * reach) * (cells + CELLS) * bases * (block + reach) * WINDOW * channels
    return pl.pallas_call(
        functools.partial(block_kernel, block),
        grid=(channels // LANES,),
        out_shape=jax.ShapeDtypeStruct(state_field.shape, jnp.bfloat16),
        in_specs=[chunked(a) for a in operands]
        + [pl.BlockSpec(bands.shape, lambda c: (0, 0, 0)), chunked(weights_one), chunked(weights_two)],
        out_specs=chunked(state_field),
        scratch_shapes=[
            pltpu.VMEM((rows * group, 2 * LANES), jnp.bfloat16),
            pltpu.VMEM((2 * LAT_REACH * group, 2 * LANES), jnp.bfloat16),
            pltpu.VMEM((rows + 2 * reach, cells + 2 * CELLS, LANES), jnp.float32),
            pltpu.VMEM((rows + reach, cells + CELLS, LANES), jnp.float32),
        ],
        compiler_params=pltpu.CompilerParams(vmem_limit_bytes=48 * 1024 * 1024),
        cost_estimate=pl.CostEstimate(flops=flops, bytes_accessed=4 * state_field.size, transcendentals=0),
    )(*operands, bands, weights_one, weights_two)


def solution(mesh):
    placed = (
        P("lat", "lon", None),
        P("lat", None, None, None),
        P("lat", None),
        P("lat", None),
        P(),
        P(),
    )
    return jax.shard_map(
        per_device, mesh=mesh, in_specs=placed, out_specs=P("lat", "lon", None), check_vma=False
    )
```

```python
import functools

import jax
import jax.numpy as jnp
from jax import lax
from jax.experimental import pallas as pl
from jax.experimental.pallas import tpu as pltpu
from jax.sharding import PartitionSpec as P

LAT_REACH = 2
LON_REACH = 4
REACH = 2 * LAT_REACH
CELLS = 8
WINDOW = CELLS + 2 * LON_REACH
LANES = 128
DEPTH = 2 * LANES
BANDS = 2 * LAT_REACH + 1
VMEM_BYTES = 56 * 1024 * 1024

ERF_SERIES = (
    1.5956562720156744,
    0.2917503271976864,
    -0.003995570947534282,
    -0.003914369984884403,
    0.0005729703632347449,
)


def erf_gelu(half):
    square = half * half
    series = ERF_SERIES[-1] * square + ERF_SERIES[-2]
    for term in ERF_SERIES[-3::-1]:
        series = series * square + term
    return half + half * jnp.tanh(half * series)


def swaps(peers, second, wrap):
    pairs = [(i, i + 1) for i in range(1 if second else 0, peers - 1, 2)]
    if second and wrap:
        pairs.append((peers - 1, 0))
    return pairs + [(j, i) for i, j in pairs]


def masked_filter(filters, band_edges, basis_mask):
    rows = filters.shape[0]
    latitude = lax.axis_index("lat") * rows + jnp.arange(rows, dtype=jnp.int32)
    source = latitude[:, None] + jnp.arange(BANDS, dtype=jnp.int32)[None, :] - LAT_REACH
    inside = (source >= band_edges[:, 0:1]) & (source < band_edges[:, 1:2])
    keep = inside[:, None, :] & (basis_mask != 0)[:, :, None]
    return jnp.where(keep[..., None], filters, 0.0).astype(jnp.bfloat16)


def band_rows(kernel):
    rows, bases, bands, lags = kernel.shape
    spaced = jnp.pad(kernel.astype(jnp.float32), ((0, 0), (0, 0), (0, 0), (0, WINDOW - lags)))
    spaced = spaced.reshape(rows, bases, bands * WINDOW)
    return jnp.pad(spaced, ((0, 0), (0, 8 - bases), (0, DEPTH - bands * WINDOW)))


def fill_toeplitz(toeplitz, band_ref, bases, places):
    group = bases * CELLS
    for row in range(0, len(places), 2):
        parts = []
        for r in (row, row + 1):
            for basis in range(bases):
                line = jnp.broadcast_to(band_ref[r, basis : basis + 1, :], (CELLS, DEPTH))
                parts.append(pltpu.roll(line, places[r] * WINDOW, 1, stride=1, stride_axis=0))
        toeplitz[row * group : (row + 2) * group, :] = jnp.concatenate(parts, 0).astype(jnp.bfloat16)


def pairs_of(items):
    return [items[i : i + 2] for i in range(0, len(items), 2)]


def lane_weights(ref, scale=1.0):
    bases, channels = ref.shape
    return [
        [ref[k : k + 1, c * LANES : (c + 1) * LANES] * scale for k in range(bases)]
        for c in range(channels // LANES)
    ]


def product(matrix, windows, weights):
    wide = [w.astype(jnp.bfloat16).reshape(DEPTH, LANES) for w in windows]
    result = jnp.dot(matrix, jnp.concatenate(wide, 1), preferred_element_type=jnp.float32)
    bases = len(weights[0])
    result = result.reshape(-1, bases, CELLS, len(windows) * LANES)
    total = None
    for k in range(bases):
        term = result[:, k] * jnp.concatenate([w[k] for w in weights], 1)
        total = term if total is None else total + term
    return [total[:, :, i * LANES : (i + 1) * LANES] for i in range(len(windows))]


def inner_kernel(
    block, x_ref, band_ref, one_ref, two_ref, toeplitz, edge_rows, edge_cells, out_ref, field, hidden
):
    rows, cells, channels = x_ref.shape
    bases = one_ref.shape[0]
    group = bases * CELLS
    chunks = channels // LANES
    fill_toeplitz(toeplitz, band_ref, bases, [r % block for r in range(rows)])
    one, two = lane_weights(one_ref, 0.5), lane_weights(two_ref)

    for c in range(chunks):
        lanes = slice(c * LANES, (c + 1) * LANES)
        field[c, LAT_REACH : LAT_REACH + rows] = x_ref[:, :, lanes].astype(jnp.float32)
        field[c, :LAT_REACH] = jnp.zeros((LAT_REACH, cells, LANES), jnp.float32)
        field[c, LAT_REACH + rows :] = jnp.zeros((LAT_REACH, cells, LANES), jnp.float32)

    windows = (cells - WINDOW) // CELLS + 1
    for start in range(0, rows, block):
        low = max(start, LAT_REACH)
        high = min(start + block, rows - LAT_REACH)
        for items in pairs_of([(c, w) for c in range(chunks) for w in range(windows)]):
            values = product(
                toeplitz[low * group : high * group, :],
                [field[c, start : start + block + REACH, w * CELLS : w * CELLS + WINDOW] for c, w in items],
                [one[c] for c, w in items],
            )
            for (c, w), value in zip(items, values):
                hidden[c, low : high, w * CELLS : (w + 1) * CELLS] = erf_gelu(value)
    for c in range(chunks):
        lanes = slice(c * LANES, (c + 1) * LANES)
        hidden[c, :LAT_REACH] = jnp.zeros((LAT_REACH,) + hidden.shape[2:], jnp.float32)
        hidden[c, rows - LAT_REACH :] = jnp.zeros((LAT_REACH,) + hidden.shape[2:], jnp.float32)
        span = windows * CELLS
        for i in range(2):
            at = LAT_REACH if i == 0 else rows - REACH - LAT_REACH
            edge_rows[i * REACH : (i + 1) * REACH, :span, lanes] = hidden[c, at : at + REACH].astype(jnp.bfloat16)
            edge_rows[i * REACH : (i + 1) * REACH, span:, lanes] = jnp.zeros((REACH, CELLS, LANES), jnp.bfloat16)
        edge = jnp.concatenate([hidden[c, :, :CELLS], hidden[c, :, span - CELLS :]], axis=1)
        edge_cells[:, :, lanes] = edge.astype(jnp.bfloat16)

    for start in range(0, rows, block):
        low = max(start, REACH)
        high = min(start + block, rows - REACH)
        first = min(max(start - LAT_REACH, 0), rows - block - REACH)
        shift = start - LAT_REACH - first
        for c in range(chunks):
            lanes = slice(c * LANES, (c + 1) * LANES)
            for pair in pairs_of(list(range(windows - 1))):
                tall = []
                for w in pair:
                    at = slice(w * CELLS, w * CELLS + WINDOW)
                    if shift < 0:
                        zero = jnp.zeros((-shift, WINDOW, LANES), jnp.float32)
                        tall.append(jnp.concatenate([zero, hidden[c, : block + REACH + shift, at]], 0))
                    elif shift > 0:
                        zero = jnp.zeros((shift, WINDOW, LANES), jnp.float32)
                        tall.append(jnp.concatenate([hidden[c, rows - block - REACH + shift :, at], zero], 0))
                    else:
                        tall.append(hidden[c, first : first + block + REACH, at])
                values = product(toeplitz[low * group : high * group, :], tall, [two[c]] * 2)
                value = jnp.concatenate(values, 1).astype(out_ref.dtype)
                out_ref[low - REACH : high - REACH, pair[0] * CELLS : (pair[0] + 2) * CELLS, lanes] = value


def rim_kernel(
    block, place_ref, x_ref, lat_a, lat_b, lon_a, lon_b, corner_a, corner_b, edge_rows, edge_cells, inner_ref,
    toeplitz, rim_band, wide_band, one_ref, two_ref, out_ref, rim_toeplitz, wide_toeplitz, field, hidden,
):
    rows, cells, channels = x_ref.shape
    bases = one_ref.shape[0]
    group = bases * CELLS
    chunks = channels // LANES
    f32, bf16 = jnp.float32, jnp.bfloat16
    tall = rows + 2 * REACH
    places = list(range(REACH)) + [2 * REACH + r for r in range(REACH)]
    fill_toeplitz(rim_toeplitz, rim_band, bases, places)
    fill_toeplitz(wide_toeplitz, wide_band, bases, places)
    one, two = lane_weights(one_ref, 0.5), lane_weights(two_ref)
    lat_odd, lon_odd = place_ref[0] == 1, place_ref[1] == 1

    def fill_lat(low, high):
        for c in range(chunks):
            lanes = slice(c * LANES, (c + 1) * LANES)
            for ref, at in ((low, 0), (high, REACH + rows)):
                part = ref[: REACH * cells, lanes].reshape(REACH, cells, LANES)
                field[c, at : at + REACH, CELLS : CELLS + cells] = part.astype(f32)

    def fill_lon(left, right, left_corner, right_corner, lat_low):
        for c in range(chunks):
            lanes = slice(c * LANES, (c + 1) * LANES)
            for ref, corner, at in ((left, left_corner, 0), (right, right_corner, CELLS + cells)):
                span = slice(at, at + CELLS)
                field[c, REACH : REACH + rows, span] = ref[:, :, lanes].astype(f32)
                field[c, :REACH, span] = corner[lat_low * REACH : (lat_low + 1) * REACH, :, lanes].astype(f32)
                other = 1 - lat_low
                field[c, REACH + rows :, span] = corner[other * REACH : (other + 1) * REACH, :, lanes].astype(f32)

    @pl.when(lat_odd)
    def _():
        fill_lat(lat_a, lat_b)

    @pl.when(jnp.logical_not(lat_odd))
    def _():
        fill_lat(lat_b, lat_a)

    for lat_low in range(2):
        for lon_is_odd in range(2):
            def fill(lat_low=lat_low, lon_is_odd=lon_is_odd):
                if lon_is_odd:
                    fill_lon(lon_a, lon_b, corner_a, corner_b, lat_low)
                else:
                    fill_lon(lon_b, lon_a, corner_b, corner_a, lat_low)

            pl.when((lat_odd if lat_low == 0 else jnp.logical_not(lat_odd))
                    & (lon_odd if lon_is_odd else jnp.logical_not(lon_odd)))(fill)

    for c in range(chunks):
        lanes = slice(c * LANES, (c + 1) * LANES)
        own = x_ref[:, :, lanes].astype(f32)
        field[c, REACH : 2 * REACH, CELLS : CELLS + cells] = own[:REACH]
        field[c, rows : rows + REACH, CELLS : CELLS + cells] = own[rows - REACH :]
        field[c, 2 * REACH : rows, CELLS : 2 * CELLS] = own[REACH : rows - REACH, :CELLS]
        field[c, 2 * REACH : rows, cells : CELLS + cells] = own[REACH : rows - REACH, cells - CELLS :]
        span = cells - CELLS
        for i, at in ((0, 2 * LAT_REACH), (1, rows - REACH)):
            part = edge_rows[i * REACH : (i + 1) * REACH, :, lanes].astype(f32)
            hidden[c, at : at + REACH, CELLS : CELLS + span] = part[:, :span]
        part = edge_cells[REACH + LAT_REACH : rows - REACH - LAT_REACH, :, lanes].astype(f32)
        at = slice(2 * REACH, rows - REACH)
        hidden[c, at, CELLS : 2 * CELLS] = part[:, :CELLS]
        hidden[c, at, cells - CELLS : cells] = part[:, CELLS:]

    def rims(ref, c, at):
        span = slice(at, at + WINDOW)
        last = ref.shape[1] - 2 * REACH
        return jnp.concatenate([ref[c, : 2 * REACH, span], ref[c, last:, span]], 0)

    columns = cells // CELLS + 1
    for items in pairs_of([(c, w) for c in range(chunks) for w in range(columns)]):
        values = product(rim_toeplitz[...], [rims(field, c, w * CELLS) for c, w in items], [one[c] for c, w in items])
        for (c, w), value in zip(items, values):
            value = erf_gelu(value)
            hidden[c, :REACH, w * CELLS : (w + 1) * CELLS] = value[:REACH]
            hidden[c, rows:, w * CELLS : (w + 1) * CELLS] = value[REACH:]
    sides = (0, cells)
    for c in range(chunks):
        for start in range(0, rows, block):
            low = max(start, LAT_REACH)
            high = min(start + block, rows - LAT_REACH)
            at = slice(start + LAT_REACH, start + LAT_REACH + block + REACH)
            values = product(
                toeplitz[low * group : high * group, :], [field[c, at, s : s + WINDOW] for s in sides], [one[c]] * 2
            )
            for s, value in zip(sides, values):
                hidden[c, low + LAT_REACH : high + LAT_REACH, s : s + CELLS] = erf_gelu(value)

    for c in range(chunks):
        lanes = slice(c * LANES, (c + 1) * LANES)
        for pair in pairs_of([w * CELLS for w in range(columns - 1)]):
            values = product(wide_toeplitz[...], [rims(hidden, c, s) for s in pair], [two[c]] * 2)
            value = jnp.concatenate(values, 1).astype(out_ref.dtype)
            out_ref[:REACH, pair[0] : pair[0] + 2 * CELLS, lanes] = value[:REACH]
            out_ref[rows - REACH :, pair[0] : pair[0] + 2 * CELLS, lanes] = value[REACH:]
        for start in range(0, rows, block):
            low = max(start, REACH)
            high = min(start + block, rows - REACH)
            at = slice(start, start + block + REACH)
            sides = (0, cells - CELLS)
            values = product(
                toeplitz[low * group : high * group, :], [hidden[c, at, s : s + WINDOW] for s in sides], [two[c]] * 2
            )
            inner = inner_ref[low - REACH : high - REACH, :, lanes].astype(f32)
            whole = jnp.concatenate([values[0], inner, values[1]], 1)
            out_ref[low:high, :, lanes] = whole.astype(out_ref.dtype)


def per_device(state_field, filters, band_edges, basis_mask, weights_one, weights_two):
    rows, cells, channels = state_field.shape
    bases = filters.shape[1]
    group = bases * CELLS
    chunks = channels // LANES
    width = 2 * LON_REACH
    block = max(b for b in range(2, rows + 1, 2) if rows % b == 0 and (b + REACH) * WINDOW <= DEPTH)
    bf16 = jnp.bfloat16
    lat_peers, lon_peers = lax.axis_size("lat"), lax.axis_size("lon")
    lat_odd, lon_odd = lax.axis_index("lat") % 2, lax.axis_index("lon") % 2

    kernel = masked_filter(filters, band_edges, basis_mask)
    tags = bases * BANDS * filters.shape[3] * LAT_REACH

    def lat_send(leading, second):
        start = jnp.where(leading, 0, rows - REACH)
        edge = lax.dynamic_slice_in_dim(state_field, start, REACH, 0).reshape(REACH * cells, channels)
        tag = jnp.where(leading, kernel[:LAT_REACH], kernel[rows - LAT_REACH :]).reshape(1, tags)
        tag = jnp.pad(tag, ((0, 15), (0, channels - tags)))
        return lax.ppermute(jnp.concatenate([edge, tag], 0), "lat", swaps(lat_peers, second, False))

    def lon_send(values, leading, second):
        start = jnp.where(leading, 0, cells - width)
        edge = lax.dynamic_slice_in_dim(values, start, width, 1)
        return lax.ppermute(edge, "lon", swaps(lon_peers, second, True))

    lat_a = lat_send(lat_odd == 1, False)
    lat_b = lat_send(lat_odd == 0, True)
    lon_b = lon_send(state_field, lon_odd == 0, True)
    lon_a = lon_send(state_field, lon_odd == 1, False)

    own_band = band_rows(kernel)
    vmem = pl.BlockSpec(memory_space=pltpu.VMEM)
    spread = cells - 2 * CELLS
    flops = 2 * (2 * rows - 3 * REACH) * (cells - 2 * CELLS) * bases * DEPTH * channels
    toeplitz, edge_rows, edge_cells, inner = pl.pallas_call(
        functools.partial(inner_kernel, block),
        out_shape=(
            jax.ShapeDtypeStruct((rows * group, DEPTH), bf16),
            jax.ShapeDtypeStruct((2 * REACH, cells, channels), bf16),
            jax.ShapeDtypeStruct((rows, 2 * CELLS, channels), bf16),
            jax.ShapeDtypeStruct((rows - 2 * REACH, spread, channels), bf16),
        ),
        in_specs=[vmem] * 4,
        out_specs=(vmem,) * 4,
        scratch_shapes=[
            pltpu.VMEM((chunks, rows + REACH, cells, LANES), jnp.float32),
            pltpu.VMEM((chunks, rows, cells - CELLS, LANES), jnp.float32),
        ],
        compiler_params=pltpu.CompilerParams(vmem_limit_bytes=VMEM_BYTES),
        cost_estimate=pl.CostEstimate(flops=flops, bytes_accessed=4 * state_field.size, transcendentals=0),
        name="inner",
    )(state_field, own_band, weights_one, weights_two)

    def rows_of(received):
        return received[: REACH * cells].reshape(REACH, cells, channels)

    def tag_of(received):
        tag = received[REACH * cells, :tags]
        return tag.reshape(LAT_REACH, bases, BANDS, filters.shape[3])

    joined = jnp.concatenate([rows_of(lat_a), rows_of(lat_b)], 0)
    corner_b = lon_send(joined, lon_odd == 0, True)
    corner_a = lon_send(joined, lon_odd == 1, False)
    tag_a, tag_b = tag_of(lat_a), tag_of(lat_b)
    tag_low = jnp.where(lat_odd == 1, tag_a, tag_b)
    tag_high = jnp.where(lat_odd == 1, tag_b, tag_a)
    edge = REACH - LAT_REACH
    rim_band = band_rows(jnp.concatenate([tag_low, kernel[:edge], kernel[rows - edge :], tag_high], 0))
    wide_band = jnp.concatenate([own_band[:REACH], own_band[rows - REACH :]], 0)
    place = jnp.stack([lat_odd, lon_odd]).astype(jnp.int32)
    return pl.pallas_call(
        functools.partial(rim_kernel, block),
        out_shape=jax.ShapeDtypeStruct(state_field.shape, bf16),
        in_specs=[pl.BlockSpec(memory_space=pltpu.SMEM)] + [vmem] * 15,
        out_specs=vmem,
        scratch_shapes=[
            pltpu.VMEM((2 * REACH * group, DEPTH), bf16),
            pltpu.VMEM((2 * REACH * group, DEPTH), bf16),
            pltpu.VMEM((chunks, rows + 2 * REACH, cells + 2 * CELLS, LANES), jnp.float32),
            pltpu.VMEM((chunks, rows + REACH, cells + CELLS, LANES), jnp.float32),
        ],
        compiler_params=pltpu.CompilerParams(vmem_limit_bytes=VMEM_BYTES),
        cost_estimate=pl.CostEstimate(flops=flops, bytes_accessed=4 * state_field.size, transcendentals=0),
        name="rim",
    )(
        place, state_field, lat_a, lat_b, lon_a, lon_b, corner_a, corner_b, edge_rows, edge_cells, inner,
        toeplitz, rim_band, wide_band, weights_one, weights_two,
    )


def solution(mesh):
    placed = (
        P("lat", "lon", None),
        P("lat", None, None, None),
        P("lat", None),
        P("lat", None),
        P(),
        P(),
    )
    return jax.shard_map(
        per_device, mesh=mesh, in_specs=placed, out_specs=P("lat", "lon", None), check_vma=False
    )
```

```python
import functools

import jax
import jax.numpy as jnp
from jax import lax
from jax.experimental import pallas as pl
from jax.experimental.pallas import tpu as pltpu
from jax.sharding import PartitionSpec as P

LAT_REACH = 2
LON_REACH = 4
REACH = 2 * LAT_REACH
BANDS = 2 * LAT_REACH + 1
CELLS = 8
WINDOW = CELLS + 2 * LON_REACH
LANES = 128
DEPTH = 2 * LANES
TILE = 16
VMEM_BYTES = 56 * 1024 * 1024
F32, BF16 = jnp.float32, jnp.bfloat16

ERF_SERIES = (
    1.5956562720156744,
    0.2917503271976864,
    -0.003995570947534282,
    -0.003914369984884403,
    0.0005729703632347449,
)


def erf_gelu(half):
    square = half * half
    series = ERF_SERIES[-1] * square + ERF_SERIES[-2]
    for term in ERF_SERIES[-3::-1]:
        series = series * square + term
    return half + half * jnp.tanh(half * series)


def swaps(peers, second, wrap):
    pairs = [(i, i + 1) for i in range(1 if second else 0, peers - 1, 2)]
    if second and wrap:
        pairs.append((peers - 1, 0))
    return pairs + [(j, i) for i, j in pairs]


def pairs_of(items):
    return [items[i : i + 2] for i in range(0, len(items), 2)]


def lanes_of(chunk):
    return slice(chunk * LANES, (chunk + 1) * LANES)


def fill_toeplitz(toeplitz, line_of, rows, bases, place_of):
    group = bases * CELLS
    blank = jnp.zeros((CELLS, DEPTH - LANES), F32)
    for row in range(0, rows, 2):
        parts = []
        for r in (row, row + 1):
            for basis in range(bases):
                line = jnp.broadcast_to(line_of(r, basis), (CELLS, LANES))
                line = jnp.concatenate([line, blank], 1)
                parts.append(pltpu.roll(line, place_of(r) * WINDOW, 1, stride=1, stride_axis=0))
        toeplitz[row * group : (row + 2) * group, :] = jnp.concatenate(parts, 0).astype(BF16)


def lane_weights(ref, scale=1.0):
    bases, channels = ref.shape
    return [[ref[k : k + 1, lanes_of(c)] * scale for k in range(bases)] for c in range(channels // LANES)]


def product(matrix, windows, weights):
    wide = [w.astype(BF16).reshape(DEPTH, LANES) for w in windows]
    result = jnp.dot(matrix, jnp.concatenate(wide, 1), preferred_element_type=F32)
    bases = len(weights[0])
    result = result.reshape(-1, bases, CELLS, len(windows) * LANES)
    total = None
    for k in range(bases):
        term = result[:, k] * jnp.concatenate([w[k] for w in weights], 1)
        total = term if total is None else total + term
    return [total[:, :, i * LANES : (i + 1) * LANES] for i in range(len(windows))]


def prep_kernel(
    place_ref, rows_ref, tiles_ref, filter_ref, edge_ref, mask_ref,
    lat_a, lat_b, lon_a, lon_b, lines, sides, padded, tags, packed, sems,
):
    bases, lags, bands, rows = filter_ref.shape
    groups = lat_a.shape[0] - 1
    lat_odd, lon_odd = place_ref[0], place_ref[1]
    start_a = (1 - lat_odd) * (rows_ref.shape[0] - groups)
    start_b = lat_odd * (rows_ref.shape[0] - groups)
    copies = [
        pltpu.make_async_copy(tiles_ref.at[:, 0], sides.at[0], sems.at[0]),
        pltpu.make_async_copy(tiles_ref.at[:, tiles_ref.shape[1] - 1], sides.at[1], sems.at[1]),
        pltpu.make_async_copy(rows_ref.at[pl.ds(start_a, groups)], lat_a.at[pl.ds(0, groups)], sems.at[2]),
        pltpu.make_async_copy(rows_ref.at[pl.ds(start_b, groups)], lat_b.at[pl.ds(0, groups)], sems.at[3]),
    ]
    for copy in copies:
        copy.start()

    source = place_ref[2] + lax.broadcasted_iota(jnp.int32, (bands, rows), 1) - LAT_REACH
    source = source + lax.broadcasted_iota(jnp.int32, (bands, rows), 0)
    inside = (source >= edge_ref[0:1, :]) & (source < edge_ref[1:2, :])
    padded[...] = jnp.zeros_like(padded)
    for k in range(bases):
        keep = inside & (mask_ref[k : k + 1, :] != 0)
        for m in range(lags):
            padded[k, m * 8 : m * 8 + bands, :rows] = jnp.where(keep, filter_ref[k, m], 0.0)
    at = lax.broadcasted_iota(jnp.int32, (LANES, LANES), 0)
    lane = lax.broadcasted_iota(jnp.int32, (LANES, LANES), 1)
    chosen = (at // 8 == lane % WINDOW) & (at % 8 == lane // WINDOW) & (at % 8 < bands) & (at // 8 < lags)
    chosen = jnp.where(chosen, 1.0, 0.0).astype(BF16)
    tags[...] = jnp.zeros_like(tags)
    for k in range(bases):
        line = jnp.dot(padded[k].T.astype(BF16), chosen, preferred_element_type=F32)
        lines[k] = line[:rows]
        span = slice(k * LAT_REACH, (k + 1) * LAT_REACH)
        tags[0, span] = line[:LAT_REACH]
        tags[1, span] = line[rows - LAT_REACH : rows]
    blank = jnp.zeros((TILE, packed.shape[2] - LANES), BF16)
    first = jnp.concatenate([tags[0].astype(BF16), blank], 1)
    last = jnp.concatenate([tags[1].astype(BF16), blank], 1)
    packed[0] = jnp.where(lat_odd == 1, first, last)
    packed[1] = jnp.where(lat_odd == 1, last, first)
    tag_copies = [
        pltpu.make_async_copy(packed.at[0], lat_a.at[groups], sems.at[4]),
        pltpu.make_async_copy(packed.at[1], lat_b.at[groups], sems.at[5]),
    ]
    for copy in tag_copies:
        copy.start()
    copies[0].wait()
    copies[1].wait()
    leading = sides[0].astype(F32)[:, :CELLS]
    trailing = sides[1].astype(F32)[:, TILE - CELLS :]
    odd = lon_odd == 1
    lon_a[...] = jnp.where(odd, leading, trailing).reshape(lon_a.shape).astype(BF16)
    lon_b[...] = jnp.where(odd, trailing, leading).reshape(lon_b.shape).astype(BF16)
    for copy in copies[2:] + tag_copies:
        copy.wait()


def inner_kernel(
    block, x_ref, lines_ref, one_ref, two_ref, toeplitz_out, rows_out, cells_out, sides_out, out_ref,
    toeplitz, x_buf, field, hidden, edge_rows, edge_cells, sides, result, in_sems, out_sems,
):
    rows, cells, channels = x_ref.shape
    bases = one_ref.shape[0]
    group = bases * CELLS
    chunks = channels // LANES
    copies = [
        pltpu.make_async_copy(x_ref.at[:, :, pl.ds(c * LANES, LANES)], x_buf.at[c], in_sems.at[c])
        for c in range(chunks)
    ]
    for copy in copies:
        copy.start()
    fill_toeplitz(toeplitz, lambda r, k: lines_ref[k, r : r + 1, :], rows, bases, lambda r: r % block)
    pending = [pltpu.make_async_copy(toeplitz, toeplitz_out, out_sems.at[0])]
    pending[0].start()
    one, two = lane_weights(one_ref, 0.5), lane_weights(two_ref)
    starts = range(0, rows, block)
    windows = (cells - WINDOW) // CELLS + 1
    span = windows * CELLS

    def load(c):
        copies[c].wait()
        blank = jnp.zeros((LAT_REACH, cells, LANES), F32)
        field[c, :LAT_REACH] = blank
        field[c, LAT_REACH : LAT_REACH + rows] = x_buf[c].astype(F32)
        field[c, LAT_REACH + rows :] = blank
        blank = jnp.zeros((REACH, span, LANES), F32)
        hidden[c, :REACH] = blank
        hidden[c, rows:] = blank

    def first(items):
        for start in starts:
            low, high = max(start, LAT_REACH), min(start + block, rows - LAT_REACH)
            values = product(
                toeplitz[low * group : high * group, :],
                [field[c, start : start + block + REACH, w * CELLS : w * CELLS + WINDOW] for c, w in items],
                [one[c] for c, w in items],
            )
            for (c, w), value in zip(items, values):
                hidden[c, low + LAT_REACH : high + LAT_REACH, w * CELLS : (w + 1) * CELLS] = erf_gelu(value)

    def second(c):
        at = LAT_REACH + LAT_REACH
        for i, row in enumerate((at, rows - REACH)):
            edge_rows[c, i * REACH : (i + 1) * REACH, :span] = hidden[c, row : row + REACH].astype(BF16)
            edge_rows[c, i * REACH : (i + 1) * REACH, span:] = jnp.zeros((REACH, cells - span, LANES), BF16)
        part = hidden[c, 2 * REACH : rows - REACH]
        edge_cells[c] = jnp.concatenate([part[:, :CELLS], part[:, span - CELLS :]], 1).astype(BF16)
        for start in starts:
            low, high = max(start, REACH), min(start + block, rows - REACH)
            matrix = toeplitz[low * group : high * group, :]
            values = []
            for pair in pairs_of(list(range(windows - 1))):
                tall = [hidden[c, start : start + block + REACH, w * CELLS : w * CELLS + WINDOW] for w in pair]
                values += product(matrix, tall, [two[c]] * len(pair))
            whole = jnp.concatenate(values[1:-1], 1).astype(BF16)
            result[c, low - REACH : high - REACH] = whole
            ends = jnp.concatenate([values[0], values[-1]], 1).astype(BF16)
            sides[c, low - REACH : high - REACH] = ends
        lanes = pl.ds(c * LANES, LANES)
        moves = [
            (edge_rows.at[c], rows_out.at[:, :, lanes]),
            (edge_cells.at[c], cells_out.at[:, :, lanes]),
            (sides.at[c], sides_out.at[:, :, lanes]),
            (result.at[c], out_ref.at[pl.ds(REACH, rows - 2 * REACH), pl.ds(TILE, cells - 2 * TILE), lanes]),
        ]
        for i, (source, target) in enumerate(moves):
            pending.append(pltpu.make_async_copy(source, target, out_sems.at[1 + len(moves) * c + i]))
            pending[-1].start()

    loaded = done = 0
    work = pairs_of([(c, w) for c in range(chunks) for w in range(windows)])
    for i, items in enumerate(work):
        while loaded <= items[-1][0]:
            load(loaded)
            loaded += 1
        first(items)
        upcoming = work[i + 1][0][0] if i + 1 < len(work) else chunks
        while done < upcoming:
            second(done)
            done += 1
    for copy in pending:
        copy.wait()


def rim_kernel(
    block, place_ref, x_ref, lat_a, lat_b, lon_a, lon_b, corner_a, corner_b, rows_in, cells_in, sides_in, toeplitz_in,
    lines_ref, one_ref, two_ref, begun_ref, out_ref,
    toeplitz, rim_toeplitz, wide_toeplitz, own_rows, own_cells, lat_buf, tag_buf, lon_buf, corner_buf,
    rows_buf, cells_buf, sides_buf, field, hidden, rim_out, side_out, first_sems, in_sems, out_sems,
):
    del begun_ref
    rows, cells, channels = x_ref.shape
    bases = one_ref.shape[0]
    group = bases * CELLS
    chunks = channels // LANES
    lat_odd, lon_odd = place_ref[0], place_ref[1]
    edge, wide = REACH * cells, rows * CELLS
    low_a, low_b = 1 - lat_odd, lat_odd
    left_a, left_b = 1 - lon_odd, lon_odd
    early = [
        pltpu.make_async_copy(lat_a.at[pl.ds(edge, TILE), pl.ds(0, LANES)], tag_buf.at[low_a], first_sems.at[0]),
        pltpu.make_async_copy(lat_b.at[pl.ds(edge, TILE), pl.ds(0, LANES)], tag_buf.at[low_b], first_sems.at[1]),
        pltpu.make_async_copy(toeplitz_in, toeplitz, first_sems.at[2]),
    ]
    for copy in early:
        copy.start()
    copies = []
    for c in range(chunks):
        lanes = pl.ds(c * LANES, LANES)
        half = REACH * CELLS
        moves = [
            (lat_a.at[pl.ds(0, edge), lanes], lat_buf.at[c, low_a]),
            (lat_b.at[pl.ds(0, edge), lanes], lat_buf.at[c, low_b]),
            (lon_a.at[:, lanes], lon_buf.at[c, left_a]),
            (lon_b.at[:, lanes], lon_buf.at[c, left_b]),
            (corner_a.at[pl.ds(0, half), lanes], corner_buf.at[c, left_a, low_a]),
            (corner_a.at[pl.ds(half, half), lanes], corner_buf.at[c, left_a, low_b]),
            (corner_b.at[pl.ds(0, half), lanes], corner_buf.at[c, left_b, low_a]),
            (corner_b.at[pl.ds(half, half), lanes], corner_buf.at[c, left_b, low_b]),
            (x_ref.at[pl.ds(0, REACH), :, lanes], own_rows.at[c, 0]),
            (x_ref.at[pl.ds(rows - REACH, REACH), :, lanes], own_rows.at[c, 1]),
            (x_ref.at[pl.ds(REACH, rows - 2 * REACH), pl.ds(0, TILE), lanes], own_cells.at[c, 0]),
            (x_ref.at[pl.ds(REACH, rows - 2 * REACH), pl.ds(cells - TILE, TILE), lanes], own_cells.at[c, 1]),
            (rows_in.at[:, :, lanes], rows_buf.at[c]),
            (cells_in.at[:, :, lanes], cells_buf.at[c]),
            (sides_in.at[:, :, lanes], sides_buf.at[c]),
        ]
        copies.append([pltpu.make_async_copy(s, t, in_sems.at[c, i]) for i, (s, t) in enumerate(moves)])
        for copy in copies[-1]:
            copy.start()

    one, two = lane_weights(one_ref, 0.5), lane_weights(two_ref)
    ends = list(range(REACH)) + list(range(rows - REACH, rows))

    def place_of(r):
        return r if r < REACH else REACH + r

    fill_toeplitz(
        wide_toeplitz, lambda r, k: lines_ref[k, ends[r] : ends[r] + 1, :], 2 * REACH, bases, place_of
    )
    early[0].wait()
    early[1].wait()
    tags = tag_buf[...].astype(F32)

    def rim_line(r, k):
        if r < LAT_REACH:
            return tags[0, k * LAT_REACH + r : k * LAT_REACH + r + 1, :]
        if r >= 2 * REACH - LAT_REACH:
            at = k * LAT_REACH + r - (2 * REACH - LAT_REACH)
            return tags[1, at : at + 1, :]
        at = r - LAT_REACH if r < REACH else rows - LAT_REACH + r - REACH
        return lines_ref[k, at : at + 1, :]

    fill_toeplitz(rim_toeplitz, rim_line, 2 * REACH, bases, place_of)
    early[2].wait()

    def load(c):
        for copy in copies[c]:
            copy.wait()
        for side in range(2):
            at = slice(side * (rows + REACH), side * (rows + REACH) + REACH)
            field[c, at, CELLS : CELLS + cells] = lat_buf[c, side].astype(F32).reshape(REACH, cells, LANES)
            own = slice(REACH + side * (rows - REACH), 2 * REACH + side * (rows - REACH))
            field[c, own, CELLS : CELLS + cells] = own_rows[c, side].astype(F32)
            middle = slice(2 * REACH, rows)
            field[c, middle, CELLS + side * (cells - TILE) : CELLS + TILE + side * (cells - TILE)] = own_cells[
                c, side
            ].astype(F32)
            span = slice(side * (CELLS + cells), side * (CELLS + cells) + CELLS)
            field[c, REACH : REACH + rows, span] = lon_buf[c, side].astype(F32).reshape(rows, CELLS, LANES)
            for end in range(2):
                part = corner_buf[c, side, end].astype(F32).reshape(REACH, CELLS, LANES)
                field[c, end * (rows + REACH) : end * (rows + REACH) + REACH, span] = part
        span = cells - CELLS
        for i, at in enumerate((REACH, rows - REACH)):
            part = rows_buf[c, i * REACH : (i + 1) * REACH].astype(F32)
            hidden[c, at : at + REACH, CELLS : CELLS + span] = part[:, :span]
        part = cells_buf[c].astype(F32)
        at = slice(2 * REACH, rows - REACH)
        hidden[c, at, CELLS : 2 * CELLS] = part[:, :CELLS]
        hidden[c, at, cells - CELLS : cells] = part[:, CELLS:]

    def rims(ref, c, at):
        span = slice(at, at + WINDOW)
        last = ref.shape[1] - 2 * REACH
        return jnp.concatenate([ref[c, : 2 * REACH, span], ref[c, last:, span]], 0)

    columns = cells // CELLS + 1

    def first_rows(items):
        values = product(rim_toeplitz[...], [rims(field, c, w * CELLS) for c, w in items], [one[c] for c, w in items])
        for (c, w), value in zip(items, values):
            value = erf_gelu(value)
            hidden[c, :REACH, w * CELLS : (w + 1) * CELLS] = value[:REACH]
            hidden[c, rows:, w * CELLS : (w + 1) * CELLS] = value[REACH:]

    def first_sides(c):
        for start in range(0, rows, block):
            low, high = max(start, LAT_REACH), min(start + block, rows - LAT_REACH)
            at = slice(start + LAT_REACH, start + LAT_REACH + block + REACH)
            sides = (0, cells)
            tall = [field[c, at, s : s + WINDOW] for s in sides]
            values = product(toeplitz[low * group : high * group, :], tall, [one[c]] * 2)
            for s, value in zip(sides, values):
                hidden[c, low + LAT_REACH : high + LAT_REACH, s : s + CELLS] = erf_gelu(value)

    pending = []

    def second(c):
        lanes = pl.ds(c * LANES, LANES)
        for pair in pairs_of([w * CELLS for w in range(columns - 1)]):
            values = product(wide_toeplitz[...], [rims(hidden, c, s) for s in pair], [two[c]] * 2)
            rim_out[c, :, pair[0] : pair[0] + 2 * CELLS] = jnp.concatenate(values, 1).astype(BF16)
        for start in range(0, rows, block):
            low, high = max(start, REACH), min(start + block, rows - REACH)
            at = slice(start, start + block + REACH)
            tall = [hidden[c, at, s : s + WINDOW] for s in (0, cells - CELLS)]
            values = product(toeplitz[low * group : high * group, :], tall, [two[c]] * 2)
            inner = sides_buf[c, low - REACH : high - REACH].astype(F32)
            side_out[c, 0, low - REACH : high - REACH] = jnp.concatenate([values[0], inner[:, :CELLS]], 1).astype(BF16)
            side_out[c, 1, low - REACH : high - REACH] = jnp.concatenate([inner[:, CELLS:], values[1]], 1).astype(BF16)
        middle = pl.ds(REACH, rows - 2 * REACH)
        moves = [
            (rim_out.at[c, pl.ds(0, REACH)], out_ref.at[pl.ds(0, REACH), :, lanes]),
            (rim_out.at[c, pl.ds(REACH, REACH)], out_ref.at[pl.ds(rows - REACH, REACH), :, lanes]),
            (side_out.at[c, 0], out_ref.at[middle, pl.ds(0, TILE), lanes]),
            (side_out.at[c, 1], out_ref.at[middle, pl.ds(cells - TILE, TILE), lanes]),
        ]
        for i, (source, target) in enumerate(moves):
            pending.append(pltpu.make_async_copy(source, target, out_sems.at[c, i]))
            pending[-1].start()

    loaded = done = 0
    work = pairs_of([(c, w) for c in range(chunks) for w in range(columns)])
    for i, items in enumerate(work):
        while loaded <= items[-1][0]:
            load(loaded)
            first_sides(loaded)
            loaded += 1
        first_rows(items)
        upcoming = work[i + 1][0][0] if i + 1 < len(work) else chunks
        while done < upcoming:
            second(done)
            done += 1
    for copy in pending:
        copy.wait()


def per_device(state_field, filters, band_edges, basis_mask, weights_one, weights_two):
    rows, cells, channels = state_field.shape
    bases = filters.shape[1]
    group = bases * CELLS
    chunks = channels // LANES
    tiles = cells // TILE
    edge = REACH * cells
    block = max(b for b in range(2, rows + 1, 2) if rows % b == 0 and (b + REACH) * WINDOW <= DEPTH)
    lat_peers, lon_peers = lax.axis_size("lat"), lax.axis_size("lon")
    lat, lon = lax.axis_index("lat"), lax.axis_index("lon")
    place = jnp.stack([lat % 2, lon % 2, lat * rows]).astype(jnp.int32)

    anywhere = pl.BlockSpec(memory_space=pl.ANY)
    vmem = pl.BlockSpec(memory_space=pltpu.VMEM)
    smem = pl.BlockSpec(memory_space=pltpu.SMEM)
    params = pltpu.CompilerParams(vmem_limit_bytes=VMEM_BYTES)
    dma = pltpu.SemaphoreType.DMA

    def array(*shape, dtype=BF16):
        return jax.ShapeDtypeStruct(shape, dtype)

    def scratch(*shape, dtype=BF16):
        return pltpu.VMEM(shape, dtype)

    groups = REACH * tiles
    lat_a, lat_b, lon_a, lon_b, lines = pl.pallas_call(
        prep_kernel,
        out_shape=(
            array(groups + 1, TILE, channels), array(groups + 1, TILE, channels),
            array(rows * CELLS, channels), array(rows * CELLS, channels),
            array(bases, rows, LANES, dtype=F32),
        ),
        in_specs=[smem, anywhere, anywhere, vmem, vmem, vmem],
        out_specs=(anywhere, anywhere, vmem, vmem, vmem),
        scratch_shapes=[
            scratch(2, rows, TILE, channels), scratch(bases, LANES, LANES, dtype=F32),
            scratch(2, TILE, LANES, dtype=F32), scratch(2, TILE, channels), dma((6,)),
        ],
        compiler_params=params,
        cost_estimate=pl.CostEstimate(flops=0, bytes_accessed=4 * edge * channels, transcendentals=0),
        name="prep",
    )(
        place, state_field.reshape(rows * tiles, TILE, channels), state_field.reshape(rows, tiles, TILE, channels),
        filters.transpose(1, 3, 2, 0), band_edges.T, basis_mask.T,
    )
    lat_a = lax.ppermute(lat_a, "lat", swaps(lat_peers, False, False)).reshape(edge + TILE, channels)
    lat_b = lax.ppermute(lat_b, "lat", swaps(lat_peers, True, False)).reshape(edge + TILE, channels)
    lon_b = lax.ppermute(lon_b, "lon", swaps(lon_peers, True, True))
    lon_a = lax.ppermute(lon_a, "lon", swaps(lon_peers, False, True))

    middle = rows - 2 * REACH
    flops = 2 * (2 * rows - 3 * REACH) * (cells - 2 * CELLS) * bases * DEPTH * channels
    cost = pl.CostEstimate(flops=flops, bytes_accessed=4 * state_field.size, transcendentals=0)
    toeplitz, edge_rows, edge_cells, sides, begun = pl.pallas_call(
        functools.partial(inner_kernel, block),
        out_shape=(
            array(rows * group, DEPTH), array(2 * REACH, cells, channels),
            array(middle - REACH, TILE, channels), array(middle, TILE, channels), array(rows, cells, channels),
        ),
        in_specs=[anywhere, vmem, vmem, vmem],
        out_specs=(anywhere,) * 5,
        scratch_shapes=[
            scratch(rows * group, DEPTH), scratch(chunks, rows, cells, LANES),
            scratch(chunks, rows + REACH, cells, LANES, dtype=F32),
            scratch(chunks, rows + REACH, cells - CELLS, LANES, dtype=F32),
            scratch(chunks, 2 * REACH, cells, LANES), scratch(chunks, middle - REACH, TILE, LANES),
            scratch(chunks, middle, TILE, LANES), scratch(chunks, middle, cells - 2 * TILE, LANES),
            dma((chunks,)), dma((1 + 4 * chunks,)),
        ],
        compiler_params=params,
        cost_estimate=cost,
        name="inner",
    )(state_field, lines, weights_one, weights_two)

    def corner_send(leading, second):
        start = jnp.where(leading, 0, cells - CELLS)
        joined = [v[:edge].reshape(REACH, cells, channels) for v in (lat_a, lat_b)]
        parts = [lax.dynamic_slice_in_dim(v, start, CELLS, 1) for v in joined]
        sent = jnp.concatenate(parts, 0).reshape(2 * REACH * CELLS, channels)
        return lax.ppermute(sent, "lon", swaps(lon_peers, second, True))

    corner_b = corner_send(lon % 2 == 0, True)
    corner_a = corner_send(lon % 2 == 1, False)
    return pl.pallas_call(
        functools.partial(rim_kernel, block),
        out_shape=array(rows, cells, channels),
        in_specs=[smem] + [anywhere] * 11 + [vmem] * 3 + [anywhere],
        out_specs=anywhere,
        input_output_aliases={15: 0},
        scratch_shapes=[
            scratch(rows * group, DEPTH), scratch(2 * REACH * group, DEPTH), scratch(2 * REACH * group, DEPTH),
            scratch(chunks, 2, REACH, cells, LANES), scratch(chunks, 2, middle, TILE, LANES),
            scratch(chunks, 2, edge, LANES), scratch(2, TILE, LANES), scratch(chunks, 2, rows * CELLS, LANES),
            scratch(chunks, 2, 2, REACH * CELLS, LANES), scratch(chunks, 2 * REACH, cells, LANES),
            scratch(chunks, middle - REACH, TILE, LANES), scratch(chunks, middle, TILE, LANES),
            scratch(chunks, rows + 2 * REACH, cells + 2 * CELLS, LANES, dtype=F32),
            scratch(chunks, rows + REACH, cells + CELLS, LANES, dtype=F32),
            scratch(chunks, 2 * REACH, cells, LANES), scratch(chunks, 2, middle, TILE, LANES),
            dma((3,)), dma((chunks, 15)), dma((chunks, 4)),
        ],
        compiler_params=params,
        cost_estimate=cost,
        name="rim",
    )(
        place, state_field, lat_a, lat_b, lon_a, lon_b, corner_a, corner_b, edge_rows, edge_cells, sides,
        toeplitz, lines, weights_one, weights_two, begun,
    )


def solution(mesh):
    placed = (
        P("lat", "lon", None),
        P("lat", None, None, None),
        P("lat", None),
        P("lat", None),
        P(),
        P(),
    )
    return jax.shard_map(
        per_device, mesh=mesh, in_specs=placed, out_specs=P("lat", "lon", None), check_vma=False
    )
```

```python
import functools

import jax
import jax.numpy as jnp
from jax import lax
from jax.experimental import pallas as pl
from jax.experimental.pallas import tpu as pltpu
from jax.sharding import PartitionSpec as P

LAT_REACH = 2
LON_REACH = 4
REACH = 2 * LAT_REACH
BANDS = 2 * LAT_REACH + 1
CELLS = 8
WINDOW = CELLS + 2 * LON_REACH
LANES = 128
DEPTH = 2 * LANES
TILE = 16
VMEM_BYTES = 24 * 1024 * 1024
PIECE = 4
F32, BF16 = jnp.float32, jnp.bfloat16

ERF_SERIES = (
    1.5956562720156744,
    0.2917503271976864,
    -0.003995570947534282,
    -0.003914369984884403,
    0.0005729703632347449,
)


def erf_gelu(half):
    square = half * half
    series = ERF_SERIES[-1] * square + ERF_SERIES[-2]
    for term in ERF_SERIES[-3::-1]:
        series = series * square + term
    return half + half * jnp.tanh(half * series)


def swaps(peers, second, wrap):
    pairs = [(i, i + 1) for i in range(1 if second else 0, peers - 1, 2)]
    if second and wrap:
        pairs.append((peers - 1, 0))
    return pairs + [(j, i) for i, j in pairs]


def pairs_of(items):
    return [items[i : i + 2] for i in range(0, len(items), 2)]


def lanes_of(chunk):
    return slice(chunk * LANES, (chunk + 1) * LANES)


def fill_toeplitz(toeplitz, line_of, rows, bases, place_of):
    group = bases * CELLS
    blank = jnp.zeros((CELLS, DEPTH - LANES), F32)
    for row in range(0, rows, 2):
        parts = []
        for r in (row, row + 1):
            for basis in range(bases):
                line = jnp.broadcast_to(line_of(r, basis), (CELLS, LANES))
                line = jnp.concatenate([line, blank], 1)
                parts.append(pltpu.roll(line, place_of(r) * WINDOW, 1, stride=1, stride_axis=0))
        toeplitz[row * group : (row + 2) * group, :] = jnp.concatenate(parts, 0).astype(BF16)


def lane_weights(ref, scale=1.0):
    bases, channels = ref.shape
    return [[ref[k : k + 1, lanes_of(c)] * scale for k in range(bases)] for c in range(channels // LANES)]


def product(matrix, low, high, windows, weights):
    wide = [w.astype(BF16).reshape(DEPTH, LANES) for w in windows]
    wide = jnp.concatenate(wide, 1)
    bases = len(weights[0])
    group = bases * CELLS
    scales = [jnp.concatenate([w[k] for w in weights], 1) for k in range(bases)]
    pieces = []
    for at in range(low, high, PIECE):
        to = min(at + PIECE, high)
        result = jnp.dot(matrix[at * group : to * group, :], wide, preferred_element_type=F32)
        result = result.reshape(to - at, bases, CELLS, len(windows) * LANES)
        total = result[:, 0] * scales[0]
        for k in range(1, bases):
            total = total + result[:, k] * scales[k]
        pieces.append(total)
    total = jnp.concatenate(pieces, 0) if len(pieces) > 1 else pieces[0]
    return [total[:, :, i * LANES : (i + 1) * LANES] for i in range(len(windows))]


def run_mixed(steps):
    waiting = []
    for first, second in steps:
        share = -(-len(waiting) // max(len(first), 1))
        for unit in first:
            unit()
            for _ in range(min(share, len(waiting))):
                waiting.pop(0)()
        for unit in waiting:
            unit()
        waiting = list(second)
    for unit in waiting:
        unit()


def prep_kernel(
    rows_ref, tiles_ref, filter_in, edge_in, mask_in,
    lat_a, lat_b, lon_a, lon_b, lines, filter_ref, edge_ref, mask_ref, sides, padded, tags, sems,
):
    bases, lags, bands, rows = filter_in.shape
    groups = lat_a.shape[0] - 1
    lat = lax.axis_index("lat")
    lat_odd, lon_odd = lat % 2, lax.axis_index("lon") % 2
    start_a = (1 - lat_odd) * (rows_ref.shape[0] - groups)
    start_b = lat_odd * (rows_ref.shape[0] - groups)
    small = [
        pltpu.make_async_copy(filter_in, filter_ref, sems.at[4]),
        pltpu.make_async_copy(edge_in, edge_ref, sems.at[5]),
        pltpu.make_async_copy(mask_in, mask_ref, sems.at[6]),
    ]
    copies = [
        pltpu.make_async_copy(tiles_ref.at[:, 0], sides.at[0], sems.at[0]),
        pltpu.make_async_copy(tiles_ref.at[:, tiles_ref.shape[1] - 1], sides.at[1], sems.at[1]),
        pltpu.make_async_copy(rows_ref.at[pl.ds(start_a, groups)], lat_a.at[pl.ds(0, groups)], sems.at[2]),
        pltpu.make_async_copy(rows_ref.at[pl.ds(start_b, groups)], lat_b.at[pl.ds(0, groups)], sems.at[3]),
    ]
    for copy in small + copies:
        copy.start()
    padded[...] = jnp.zeros_like(padded)
    tags[...] = jnp.zeros_like(tags)
    at = lax.broadcasted_iota(jnp.int32, (LANES, LANES), 0)
    lane = lax.broadcasted_iota(jnp.int32, (LANES, LANES), 1)
    chosen = (at // 8 == lane % WINDOW) & (at % 8 == lane // WINDOW) & (at % 8 < bands) & (at // 8 < lags)
    chosen = jnp.where(chosen, 1.0, 0.0).astype(BF16)
    for copy in small:
        copy.wait()

    source = lat * rows + lax.broadcasted_iota(jnp.int32, (bands, rows), 1) - LAT_REACH
    source = source + lax.broadcasted_iota(jnp.int32, (bands, rows), 0)
    inside = (source >= edge_ref[0:1, :]) & (source < edge_ref[1:2, :])
    for k in range(bases):
        keep = inside & (mask_ref[k : k + 1, :] != 0)
        for m in range(lags):
            padded[k, m * 8 : m * 8 + bands, :rows] = jnp.where(keep, filter_ref[k, m], 0.0)
    for k in range(bases):
        line = jnp.dot(padded[k].T.astype(BF16), chosen, preferred_element_type=F32)
        lines[k] = line[:rows]
        span = slice(k * LAT_REACH, (k + 1) * LAT_REACH)
        tags[0, span] = line[:LAT_REACH]
        tags[1, span] = line[rows - LAT_REACH : rows]
    blank = jnp.zeros((TILE, lat_a.shape[2] - LANES), F32)
    first = jnp.concatenate([tags[0], blank], 1)
    last = jnp.concatenate([tags[1], blank], 1)
    lat_a[groups] = jnp.where(lat_odd == 1, first, last).astype(BF16)
    lat_b[groups] = jnp.where(lat_odd == 1, last, first).astype(BF16)
    copies[0].wait()
    copies[1].wait()
    leading = sides[0].astype(F32)[:, :CELLS]
    trailing = sides[1].astype(F32)[:, TILE - CELLS :]
    odd = lon_odd == 1
    lon_a[...] = jnp.where(odd, leading, trailing).reshape(lon_a.shape).astype(BF16)
    lon_b[...] = jnp.where(odd, trailing, leading).reshape(lon_b.shape).astype(BF16)
    for copy in copies[2:]:
        copy.wait()


def inner_kernel(
    block, x_ref, lines_ref, one_ref, two_ref, toeplitz, edge_rows, edge_cells, sides, middle, field, hidden, ends
):
    rows, cells, channels = x_ref.shape
    bases = one_ref.shape[0]
    chunks = channels // LANES
    fill_toeplitz(toeplitz, lambda r, k: lines_ref[k, r : r + 1, :], rows, bases, lambda r: r % block)
    one, two = lane_weights(one_ref, 0.5), lane_weights(two_ref)
    starts = range(0, rows, block)
    windows = (cells - WINDOW) // CELLS + 1
    span = windows * CELLS

    def load(c):
        blank = jnp.zeros((LAT_REACH, cells, LANES), F32)
        field[c, :LAT_REACH] = blank
        field[c, LAT_REACH : LAT_REACH + rows] = x_ref[:, :, lanes_of(c)].astype(F32)
        field[c, LAT_REACH + rows :] = blank
        blank = jnp.zeros((REACH, span, LANES), F32)
        hidden[c, :REACH] = blank
        hidden[c, rows:] = blank

    def first(items, start):
        low, high = max(start, LAT_REACH), min(start + block, rows - LAT_REACH)
        tall = [field[c, start : start + block + REACH, w * CELLS : w * CELLS + WINDOW] for c, w in items]
        values = product(toeplitz, low, high, tall, [one[c] for c, w in items])
        for (c, w), value in zip(items, values):
            hidden[c, low + LAT_REACH : high + LAT_REACH, w * CELLS : (w + 1) * CELLS] = erf_gelu(value)

    def second(c, start, pair):
        low, high = max(start, REACH), min(start + block, rows - REACH)
        tall = [hidden[c, start : start + block + REACH, w * CELLS : w * CELLS + WINDOW] for w in pair]
        values = product(toeplitz, low, high, tall, [two[c]] * len(pair))
        at = slice(low - REACH, high - REACH)
        for w, value in zip(pair, values):
            if w in (0, windows - 2):
                ends[c, at, (w > 0) * CELLS : (w > 0) * CELLS + CELLS] = value
        if len(pair) == 2 and pair[0] > 0:
            span = slice((pair[0] - 1) * CELLS, (pair[0] + 1) * CELLS)
            middle[at, span, lanes_of(c)] = jnp.concatenate(values, 1).astype(BF16)

    def export(c):
        for i, row in enumerate((REACH, rows - REACH)):
            part = jnp.concatenate([hidden[c, row : row + REACH], jnp.zeros((REACH, cells - span, LANES), F32)], 1)
            edge_rows[i * REACH : (i + 1) * REACH, :, lanes_of(c)] = part.astype(BF16)
        part = hidden[c, 2 * REACH : rows - REACH]
        edge_cells[:, :, lanes_of(c)] = jnp.concatenate([part[:, :CELLS], part[:, span - CELLS :]], 1).astype(BF16)
        sides[:, :, lanes_of(c)] = ends[c].astype(BF16)

    part = functools.partial
    steps = [([part(load, c)], []) for c in range(chunks)]
    for items in pairs_of([(c, w) for c in range(chunks) for w in range(windows)]):
        steps[items[-1][0]][0].extend(part(first, items, start) for start in starts)
    for c in range(chunks):
        pairs = [[0, windows - 2]] + pairs_of(list(range(1, windows - 2)))
        steps[c][1].extend(part(second, c, start, pair) for start in starts for pair in pairs)
        steps[c][1].append(part(export, c))
    for c in range(chunks - 1, 0, -1):
        if c * windows % 2:
            straddle = steps[c][0][1 : 1 + len(starts)]
            steps[c][0][1 : 1 + len(starts)] = []
            steps[c - 1][0].extend([steps[c][0].pop(0)] + straddle)
    run_mixed(steps)


def ordered(odd, a, b):
    a, b = a.astype(F32), b.astype(F32)
    return jnp.where(odd, a, b), jnp.where(odd, b, a)


def parities():
    return lax.axis_index("lat") % 2 == 1, lax.axis_index("lon") % 2 == 1


def rim_kernel(
    block, x_ref, lat_a, lat_b, lon_a, lon_b, rows_in, cells_in, sides_in, toeplitz, lines_ref, one_ref, two_ref,
    rim_toeplitz, wide_toeplitz, rim_out, side_out, ends, field, hidden,
):
    rows, cells, channels = x_ref.shape
    bases = one_ref.shape[0]
    chunks = channels // LANES
    edge = REACH * cells
    columns = cells // CELLS + 1
    lat_odd, lon_odd = parities()
    one, two = lane_weights(one_ref, 0.5), lane_weights(two_ref)
    kept = list(range(REACH)) + list(range(rows - REACH, rows))

    def place_of(r):
        return r if r < REACH else REACH + r

    tags = ordered(lat_odd, lat_a[edge:, :LANES], lat_b[edge:, :LANES])

    def rim_line(r, k):
        if r < LAT_REACH:
            return tags[0][k * LAT_REACH + r : k * LAT_REACH + r + 1, :]
        if r >= 2 * REACH - LAT_REACH:
            at = k * LAT_REACH + r - (2 * REACH - LAT_REACH)
            return tags[1][at : at + 1, :]
        at = r - LAT_REACH if r < REACH else rows - LAT_REACH + r - REACH
        return lines_ref[k, at : at + 1, :]

    fill_toeplitz(rim_toeplitz, rim_line, 2 * REACH, bases, place_of)
    fill_toeplitz(wide_toeplitz, lambda r, k: lines_ref[k, kept[r] : kept[r] + 1, :], 2 * REACH, bases, place_of)

    def load(c):
        lanes = lanes_of(c)
        lat = ordered(lat_odd, lat_a[:edge, lanes], lat_b[:edge, lanes])
        lon = ordered(lon_odd, lon_a[:, lanes], lon_b[:, lanes])
        inner = slice(REACH, rows - REACH)
        blank = jnp.zeros((REACH, CELLS, LANES), F32)
        for side in range(2):
            at = slice(side * (rows + REACH), side * (rows + REACH) + REACH)
            field[c, at, CELLS : CELLS + cells] = lat[side].reshape(REACH, cells, LANES)
            own = slice(side * (rows - REACH), side * (rows - REACH) + REACH)
            at = slice(own.start + REACH, own.stop + REACH)
            field[c, at, CELLS : CELLS + cells] = x_ref[own, :, lanes].astype(F32)
            own = slice(side * (cells - TILE), side * (cells - TILE) + TILE)
            at = slice(own.start + CELLS, own.stop + CELLS)
            field[c, 2 * REACH : rows, at] = x_ref[inner, own, lanes].astype(F32)
            span = slice(side * (CELLS + cells), side * (CELLS + cells) + CELLS)
            field[c, REACH : REACH + rows, span] = lon[side].reshape(rows, CELLS, LANES)
            for end in range(2):
                at = slice(end * (rows + REACH), end * (rows + REACH) + REACH)
                field[c, at, span] = blank
                hidden[c, end * rows : end * rows + REACH, side * cells : side * cells + CELLS] = blank
        span = cells - CELLS
        for i, at in enumerate((REACH, rows - REACH)):
            part = rows_in[i * REACH : (i + 1) * REACH, :, lanes].astype(F32)
            hidden[c, at : at + REACH, CELLS : CELLS + span] = part[:, :span]
        part = cells_in[:, :, lanes].astype(F32)
        at = slice(2 * REACH, rows - REACH)
        hidden[c, at, CELLS : 2 * CELLS] = part[:, :CELLS]
        hidden[c, at, cells - CELLS : cells] = part[:, CELLS:]

    def rims(ref, c, span):
        last = ref.shape[1] - 2 * REACH
        return jnp.concatenate([ref[c, : 2 * REACH, span], ref[c, last:, span]], 0)

    def first_rows(items):
        tall = [rims(field, c, slice(w * CELLS, w * CELLS + WINDOW)) for c, w in items]
        values = product(rim_toeplitz, 0, 2 * REACH, tall, [one[c] for c, w in items])
        for (c, w), value in zip(items, values):
            value = erf_gelu(value)
            hidden[c, :REACH, w * CELLS : (w + 1) * CELLS] = value[:REACH]
            hidden[c, rows:, w * CELLS : (w + 1) * CELLS] = value[REACH:]

    def first_sides(c, start):
        low, high = max(start, LAT_REACH), min(start + block, rows - LAT_REACH)
        at = slice(start + LAT_REACH, start + LAT_REACH + block + REACH)
        tall = [field[c, at, s : s + WINDOW] for s in (0, cells)]
        values = product(toeplitz, low, high, tall, [one[c]] * 2)
        for s, value in zip((0, cells), values):
            hidden[c, low + LAT_REACH : high + LAT_REACH, s : s + CELLS] = erf_gelu(value)

    def second_rows(c, pair):
        tall = [rims(hidden, c, slice(w * CELLS, w * CELLS + WINDOW)) for w in pair]
        values = product(wide_toeplitz, 0, 2 * REACH, tall, [two[c]] * 2)
        blank = jnp.zeros((2 * REACH, CELLS, LANES), F32)
        if pair == [1, columns - 3]:
            rim_out[:, :TILE, lanes_of(c)] = jnp.concatenate([blank, values[0]], 1).astype(BF16)
            rim_out[:, cells - TILE :, lanes_of(c)] = jnp.concatenate([values[1], blank], 1).astype(BF16)
        else:
            rim_out[:, pair[0] * CELLS : (pair[0] + 2) * CELLS, lanes_of(c)] = jnp.concatenate(values, 1).astype(BF16)

    def second_sides(c, start):
        low, high = max(start, REACH), min(start + block, rows - REACH)
        tall = [hidden[c, start : start + block + REACH, s : s + WINDOW] for s in (0, cells - CELLS)]
        values = product(toeplitz, low, high, tall, [two[c]] * 2)
        at = slice(low - REACH, high - REACH)
        inner = sides_in[at, :, lanes_of(c)].astype(F32)
        side_out[0, at, :, lanes_of(c)] = jnp.concatenate([values[0], inner[:, :CELLS]], 1).astype(BF16)
        side_out[1, at, :, lanes_of(c)] = jnp.concatenate([inner[:, CELLS:], values[1]], 1).astype(BF16)

    def export(c):
        for side in range(2):
            span = slice(side * (cells - CELLS), side * (cells - CELLS) + WINDOW)
            ends[side, :, :, lanes_of(c)] = rims(hidden, c, span).astype(BF16)

    part = functools.partial
    steps = [([part(load, c)], []) for c in range(chunks)]
    items = [(c, w) for c in range(chunks) for w in range(1, columns - 1)]
    for pair in pairs_of(items):
        steps[pair[-1][0]][0].append(part(first_rows, pair))
    for c in range(chunks - 1, 0, -1):
        if c * (columns - 2) % 2:
            steps[c - 1][0].extend([steps[c][0].pop(0), steps[c][0].pop(0)])
    starts = range(0, rows, block)
    for c, (first, second) in enumerate(steps):
        first.extend(part(first_sides, c, start) for start in starts)
        second.extend(
            part(second_rows, c, pair) for pair in [[1, columns - 3]] + pairs_of(list(range(2, columns - 3)))
        )
        second.extend(part(second_sides, c, start) for start in starts)
        second.append(part(export, c))
    run_mixed(steps)


def corner_kernel(
    x_ref, lat_a, lat_b, lon_a, lon_b, corner_a, corner_b, ends, rim_toeplitz, wide_toeplitz, one_ref, two_ref,
    middle, side_out, rim_out, out_ref, corner_out, sems,
):
    rows, cells, channels = x_ref.shape
    chunks = channels // LANES
    edge = REACH * cells
    inner = pl.ds(REACH, rows - 2 * REACH)
    ends_at = (pl.ds(0, REACH), pl.ds(rows - REACH, REACH))
    sides_at = (pl.ds(0, TILE), pl.ds(cells - TILE, TILE))
    span = pl.ds(TILE, cells - 2 * TILE)
    moves = [(middle, out_ref.at[inner, span])]
    for i in range(2):
        moves.append((side_out.at[i], out_ref.at[inner, sides_at[i]]))
        moves.append((rim_out.at[pl.ds(i * REACH, REACH), span], out_ref.at[ends_at[i], span]))
    copies = [pltpu.make_async_copy(source, target, sems.at[i]) for i, (source, target) in enumerate(moves)]
    for copy in copies:
        copy.start()
    lat_odd, lon_odd = parities()
    one, two = lane_weights(one_ref, 0.5), lane_weights(two_ref)

    def first(c):
        lanes = lanes_of(c)
        lat = ordered(lat_odd, lat_a[:edge, lanes], lat_b[:edge, lanes])
        lon = ordered(lon_odd, lon_a[:, lanes], lon_b[:, lanes])
        corner = ordered(lon_odd, corner_a[:, lanes], corner_b[:, lanes])
        tall = []
        for side in range(2):
            own = slice(side * (cells - CELLS), side * (cells - CELLS) + CELLS)
            above = [v.reshape(REACH, cells, LANES)[:, own] for v in lat]
            tiles = slice(side * (cells - TILE), side * (cells - TILE) + TILE)
            half = slice(side * (TILE - CELLS), side * (TILE - CELLS) + CELLS)
            mine = [x_ref[r : r + REACH, tiles, lanes].astype(F32)[:, half] for r in (0, rows - REACH)]
            near = lon[side].reshape(rows, CELLS, LANES)
            far = ordered(lat_odd, corner[side][: REACH * CELLS], corner[side][REACH * CELLS :])
            far = [v.reshape(REACH, CELLS, LANES) for v in far]
            own = jnp.concatenate([above[0], mine[0], mine[1], above[1]], 0)
            other = jnp.concatenate([far[0], near[:REACH], near[rows - REACH :], far[1]], 0)
            tall.append(jnp.concatenate([own, other] if side else [other, own], 1))
        return [erf_gelu(v) for v in product(rim_toeplitz, 0, 2 * REACH, tall, [one[c]] * 2)]

    def second(c, blocks):
        lanes = lanes_of(c)
        tall = []
        for side in range(2):
            near = ends[side, :, :, lanes].astype(F32)
            own = near[:, side * CELLS : side * CELLS + CELLS]
            own = jnp.concatenate([blocks[side][:REACH], own[REACH : 3 * REACH], blocks[side][REACH:]], 0)
            tall.append(jnp.concatenate([near[:, :CELLS], own] if side else [own, near[:, CELLS:]], 1))
        values = product(wide_toeplitz, 0, 2 * REACH, tall, [two[c]] * 2)
        for side in range(2):
            tiles = slice(side * (cells - TILE), side * (cells - TILE) + TILE)
            near = rim_out[:, tiles, lanes].astype(F32)
            near = near[:, : TILE - CELLS] if side else near[:, CELLS:]
            whole = [near, values[side]] if side else [values[side], near]
            corner_out[side, :, :, lanes] = jnp.concatenate(whole, 1).astype(BF16)

    hidden = [first(c) for c in range(chunks)]
    for c in range(chunks):
        second(c, hidden[c])
    last = []
    for side in range(2):
        for end in range(2):
            source = corner_out.at[side, pl.ds(end * REACH, REACH)]
            target = out_ref.at[ends_at[end], sides_at[side]]
            last.append(pltpu.make_async_copy(source, target, sems.at[len(copies) + len(last)]))
            last[-1].start()
    for copy in copies + last:
        copy.wait()


def per_device(state_field, filters, band_edges, basis_mask, weights_one, weights_two):
    rows, cells, channels = state_field.shape
    bases = filters.shape[1]
    group = bases * CELLS
    chunks = channels // LANES
    tiles = cells // TILE
    edge = REACH * cells
    block = max(b for b in range(2, rows + 1, 2) if rows % b == 0 and (b + REACH) * WINDOW <= DEPTH)
    lat_peers, lon_peers = lax.axis_size("lat"), lax.axis_size("lon")
    lon = lax.axis_index("lon")

    anywhere = pl.BlockSpec(memory_space=pl.ANY)
    vmem = pl.BlockSpec(memory_space=pltpu.VMEM)
    params = pltpu.CompilerParams(vmem_limit_bytes=VMEM_BYTES)
    dma = pltpu.SemaphoreType.DMA

    def array(*shape, dtype=BF16):
        return jax.ShapeDtypeStruct(shape, dtype)

    def scratch(*shape, dtype=BF16):
        return pltpu.VMEM(shape, dtype)

    groups = REACH * tiles
    lat_a, lat_b, lon_a, lon_b, lines = pl.pallas_call(
        prep_kernel,
        out_shape=(
            array(groups + 1, TILE, channels), array(groups + 1, TILE, channels),
            array(rows * CELLS, channels), array(rows * CELLS, channels),
            array(bases, rows, LANES, dtype=F32),
        ),
        in_specs=[anywhere] * 5,
        out_specs=(vmem,) * 5,
        scratch_shapes=[
            scratch(bases, filters.shape[3], BANDS, rows, dtype=F32),
            scratch(2, rows, dtype=jnp.int32), scratch(bases, rows, dtype=jnp.int32),
            scratch(2, rows, TILE, channels), scratch(bases, LANES, LANES, dtype=F32),
            scratch(2, TILE, LANES, dtype=F32), dma((7,)),
        ],
        compiler_params=pltpu.CompilerParams(vmem_limit_bytes=60 * 1024 * 1024),
        cost_estimate=pl.CostEstimate(flops=0, bytes_accessed=4 * edge * channels, transcendentals=0),
        name="prep",
    )(
        state_field.reshape(rows * tiles, TILE, channels), state_field.reshape(rows, tiles, TILE, channels),
        filters.transpose(1, 3, 2, 0), band_edges.T, basis_mask.T,
    )
    lat_a = lax.ppermute(lat_a, "lat", swaps(lat_peers, False, False)).reshape(edge + TILE, channels)
    lat_b = lax.ppermute(lat_b, "lat", swaps(lat_peers, True, False)).reshape(edge + TILE, channels)
    lon_b = lax.ppermute(lon_b, "lon", swaps(lon_peers, True, True))
    lon_a = lax.ppermute(lon_a, "lon", swaps(lon_peers, False, True))

    middle = rows - 2 * REACH
    flops = 2 * (2 * rows - 3 * REACH) * (cells - 2 * CELLS) * bases * DEPTH * channels
    cost = pl.CostEstimate(flops=flops, bytes_accessed=4 * state_field.size, transcendentals=0)
    toeplitz, edge_rows, edge_cells, sides, inner = pl.pallas_call(
        functools.partial(inner_kernel, block),
        out_shape=(
            array(rows * group, DEPTH), array(2 * REACH, cells, channels), array(middle - REACH, TILE, channels),
            array(middle, TILE, channels), array(middle, cells - 2 * TILE, channels),
        ),
        in_specs=[vmem] * 4,
        out_specs=(vmem,) * 5,
        scratch_shapes=[
            scratch(chunks, rows + REACH, cells, LANES, dtype=F32),
            scratch(chunks, rows + REACH, cells - CELLS, LANES, dtype=F32),
            scratch(chunks, middle, TILE, LANES, dtype=F32),
        ],
        compiler_params=params,
        cost_estimate=cost,
        name="inner",
    )(state_field, lines, weights_one, weights_two)

    def corner_send(leading, second):
        start = jnp.where(leading, 0, cells - CELLS)
        joined = [v[:edge].reshape(REACH, cells, channels) for v in (lat_a, lat_b)]
        parts = [lax.dynamic_slice_in_dim(v, start, CELLS, 1) for v in joined]
        sent = jnp.concatenate(parts, 0).reshape(2 * REACH * CELLS, channels)
        return lax.ppermute(sent, "lon", swaps(lon_peers, second, True))

    lat_a, lat_b, inner = lax.optimization_barrier((lat_a, lat_b, inner))
    corner_b = corner_send(lon % 2 == 0, True)
    corner_a = corner_send(lon % 2 == 1, False)
    rim_toeplitz, wide_toeplitz, rim_out, side_out, ends = pl.pallas_call(
        functools.partial(rim_kernel, block),
        out_shape=(
            array(2 * REACH * group, DEPTH), array(2 * REACH * group, DEPTH), array(2 * REACH, cells, channels),
            array(2, middle, TILE, channels), array(2, 4 * REACH, WINDOW, channels),
        ),
        in_specs=[vmem] * 12,
        out_specs=(vmem,) * 5,
        scratch_shapes=[
            scratch(chunks, rows + 2 * REACH, cells + 2 * CELLS, LANES, dtype=F32),
            scratch(chunks, rows + REACH, cells + CELLS, LANES, dtype=F32),
        ],
        compiler_params=params,
        cost_estimate=cost,
        name="rim",
    )(
        state_field, lat_a, lat_b, lon_a, lon_b, edge_rows, edge_cells, sides, toeplitz, lines,
        weights_one, weights_two,
    )
    return pl.pallas_call(
        corner_kernel,
        out_shape=array(rows, cells, channels),
        in_specs=[vmem] * 15,
        out_specs=anywhere,
        scratch_shapes=[scratch(2, 2 * REACH, TILE, channels), dma((9,))],
        compiler_params=params,
        cost_estimate=cost,
        name="corner",
    )(
        state_field, lat_a, lat_b, lon_a, lon_b, corner_a, corner_b, ends, rim_toeplitz, wide_toeplitz,
        weights_one, weights_two, inner, side_out, rim_out,
    )


def solution(mesh):
    placed = (
        P("lat", "lon", None),
        P("lat", None, None, None),
        P("lat", None),
        P("lat", None),
        P(),
        P(),
    )
    return jax.shard_map(
        per_device, mesh=mesh, in_specs=placed, out_specs=P("lat", "lon", None), check_vma=False
    )
```

```python
import functools

import jax
import jax.numpy as jnp
from jax import lax
from jax.experimental import pallas as pl
from jax.experimental.pallas import tpu as pltpu
from jax.sharding import PartitionSpec as P

LAT_REACH = 2
LON_REACH = 4
REACH = 2 * LAT_REACH
BANDS = 2 * LAT_REACH + 1
CELLS = 8
WINDOW = CELLS + 2 * LON_REACH
LANES = 128
DEPTH = 2 * LANES
TILE = 16
VMEM_BYTES = 20 * 1024 * 1024
PIECE = 4
F32, BF16 = jnp.float32, jnp.bfloat16

ERF_SERIES = (
    1.5956562720156744,
    0.2917503271976864,
    -0.003995570947534282,
    -0.003914369984884403,
    0.0005729703632347449,
)


def erf_gelu(half):
    square = half * half
    series = ERF_SERIES[-1] * square + ERF_SERIES[-2]
    for term in ERF_SERIES[-3::-1]:
        series = series * square + term
    return half + half * jnp.tanh(half * series)


def swaps(peers, second):
    pairs = [(i, i + 1) for i in range(1 if second else 0, peers - 1, 2)]
    if second:
        pairs.append((peers - 1, 0))
    return pairs + [(j, i) for i, j in pairs]


def lat_swaps(peers, width, second):
    pairs = [(i, i + 1) for i in range(1 if second else 0, peers - 1, 2)]
    pairs += [(j, i) for i, j in pairs]
    alone = set(range(peers)) - {i for i, _ in pairs}
    result = [(i * width + k, j * width + k) for i, j in pairs for k in range(width)]
    return result + [(i * width + k, i * width + (k ^ 1)) for i in sorted(alone) for k in range(width)]


def pairs_of(items):
    return [items[i : i + 2] for i in range(0, len(items), 2)]


def lanes_of(chunk):
    return slice(chunk * LANES, (chunk + 1) * LANES)


def fill_toeplitz(toeplitz, line_of, rows, bases, place_of):
    group = bases * CELLS
    blank = jnp.zeros((CELLS, DEPTH - LANES), F32)
    for row in range(0, rows, 2):
        parts = []
        for r in (row, row + 1):
            for basis in range(bases):
                line = jnp.broadcast_to(line_of(r, basis), (CELLS, LANES))
                line = jnp.concatenate([line, blank], 1)
                parts.append(pltpu.roll(line, place_of(r) * WINDOW, 1, stride=1, stride_axis=0))
        toeplitz[row * group : (row + 2) * group, :] = jnp.concatenate(parts, 0).astype(BF16)


def lane_weights(ref, scale=1.0):
    bases, channels = ref.shape
    return [[ref[k : k + 1, lanes_of(c)] * scale for k in range(bases)] for c in range(channels // LANES)]


def product(matrix, low, high, windows, weights):
    wide = [w.astype(BF16).reshape(DEPTH, LANES) for w in windows]
    wide = jnp.concatenate(wide, 1)
    bases = len(weights[0])
    group = bases * CELLS
    scales = [jnp.concatenate([w[k] for w in weights], 1) for k in range(bases)]
    pieces = []
    for at in range(low, high, PIECE):
        to = min(at + PIECE, high)
        result = jnp.dot(matrix[at * group : to * group, :], wide, preferred_element_type=F32)
        result = result.reshape(to - at, bases, CELLS, len(windows) * LANES)
        total = result[:, 0] * scales[0]
        for k in range(1, bases):
            total = total + result[:, k] * scales[k]
        pieces.append(total)
    total = jnp.concatenate(pieces, 0) if len(pieces) > 1 else pieces[0]
    return [total[:, :, i * LANES : (i + 1) * LANES] for i in range(len(windows))]


def run_mixed(steps):
    waiting = []
    for first, second in steps:
        share = -(-len(waiting) // max(len(first), 1))
        for unit in first:
            unit()
            for _ in range(min(share, len(waiting))):
                waiting.pop(0)()
        for unit in waiting:
            unit()
        waiting = list(second)
    for unit in waiting:
        unit()


def line_choice(lags):
    at = lax.broadcasted_iota(jnp.int32, (LANES, LANES), 0)
    lane = lax.broadcasted_iota(jnp.int32, (LANES, LANES), 1)
    chosen = (at // 8 == lane % WINDOW) & (at % 8 == lane // WINDOW) & (at % 8 < BANDS) & (at // 8 < lags)
    return jnp.where(chosen, 1.0, 0.0).astype(BF16)


def filter_lines(filter_ref, edge_ref, mask_ref, padded, chosen):
    bases, lags, bands, rows = filter_ref.shape
    source = lax.axis_index("lat") * rows + lax.broadcasted_iota(jnp.int32, (bands, rows), 1) - LAT_REACH
    source = source + lax.broadcasted_iota(jnp.int32, (bands, rows), 0)
    inside = (source >= edge_ref[0:1, :]) & (source < edge_ref[1:2, :])
    for k in range(bases):
        keep = inside & (mask_ref[k : k + 1, :] != 0)
        for m in range(lags):
            padded[k, m * 8 : m * 8 + bands, :rows] = jnp.where(keep, filter_ref[k, m], 0.0)
    return [jnp.dot(padded[k].T.astype(BF16), chosen, preferred_element_type=F32) for k in range(bases)]


def prep_kernel(
    rows_ref, tiles_ref, filter_in, edge_in, mask_in,
    lat_a, lat_b, lon_a, lon_b, filter_ref, edge_ref, mask_ref, sides, padded, tags, sems,
):
    bases, lags, bands, rows = filter_in.shape
    groups = lat_a.shape[0] - 1
    lat_odd, lon_odd = lax.axis_index("lat") % 2, lax.axis_index("lon") % 2
    start_a = (1 - lat_odd) * (rows_ref.shape[0] - groups)
    start_b = lat_odd * (rows_ref.shape[0] - groups)
    small = [
        pltpu.make_async_copy(filter_in, filter_ref, sems.at[4]),
        pltpu.make_async_copy(edge_in, edge_ref, sems.at[5]),
        pltpu.make_async_copy(mask_in, mask_ref, sems.at[6]),
    ]
    copies = [
        pltpu.make_async_copy(tiles_ref.at[:, 0], sides.at[0], sems.at[0]),
        pltpu.make_async_copy(tiles_ref.at[:, tiles_ref.shape[1] - 1], sides.at[1], sems.at[1]),
        pltpu.make_async_copy(rows_ref.at[pl.ds(start_a, groups)], lat_a.at[pl.ds(0, groups)], sems.at[2]),
        pltpu.make_async_copy(rows_ref.at[pl.ds(start_b, groups)], lat_b.at[pl.ds(0, groups)], sems.at[3]),
    ]
    for copy in small + copies:
        copy.start()
    padded[...] = jnp.zeros_like(padded)
    tags[...] = jnp.zeros_like(tags)
    chosen = line_choice(lags)
    for copy in small:
        copy.wait()
    for k, line in enumerate(filter_lines(filter_ref, edge_ref, mask_ref, padded, chosen)):
        span = slice(k * LAT_REACH, (k + 1) * LAT_REACH)
        tags[0, span] = line[:LAT_REACH]
        tags[1, span] = line[rows - LAT_REACH : rows]
    blank = jnp.zeros((TILE, lat_a.shape[2] - LANES), F32)
    first = jnp.concatenate([tags[0], blank], 1)
    last = jnp.concatenate([tags[1], blank], 1)
    lat_a[groups] = jnp.where(lat_odd == 1, first, last).astype(BF16)
    lat_b[groups] = jnp.where(lat_odd == 1, last, first).astype(BF16)
    copies[0].wait()
    copies[1].wait()
    leading = sides[0].astype(F32)[:, :CELLS]
    trailing = sides[1].astype(F32)[:, TILE - CELLS :]
    odd = lon_odd == 1
    lon_a[...] = jnp.where(odd, leading, trailing).reshape(lon_a.shape).astype(BF16)
    lon_b[...] = jnp.where(odd, trailing, leading).reshape(lon_b.shape).astype(BF16)
    for copy in copies[2:]:
        copy.wait()


def inner_kernel(
    block, x_ref, filter_ref, edge_ref, mask_ref, one_ref, two_ref,
    toeplitz, lines_ref, edge_rows, edge_cells, sides, middle, padded, field, hidden, ends,
):
    rows, cells, channels = x_ref.shape
    bases = one_ref.shape[0]
    chunks = channels // LANES
    padded[...] = jnp.zeros_like(padded)
    chosen = line_choice(filter_ref.shape[1])
    lines = filter_lines(filter_ref, edge_ref, mask_ref, padded, chosen)
    for k in range(bases):
        lines_ref[k] = lines[k][:rows]
    fill_toeplitz(toeplitz, lambda r, k: lines[k][r : r + 1, :], rows, bases, lambda r: r % block)
    one, two = lane_weights(one_ref, 0.5), lane_weights(two_ref)
    starts = range(0, rows, block)
    windows = (cells - WINDOW) // CELLS + 1
    span = windows * CELLS

    def load(c):
        blank = jnp.zeros((LAT_REACH, cells, LANES), F32)
        field[c, :LAT_REACH] = blank
        field[c, LAT_REACH : LAT_REACH + rows] = x_ref[:, :, lanes_of(c)].astype(F32)
        field[c, LAT_REACH + rows :] = blank
        blank = jnp.zeros((REACH, span, LANES), F32)
        hidden[c, :REACH] = blank
        hidden[c, rows:] = blank

    def first(items, start):
        low, high = max(start, LAT_REACH), min(start + block, rows - LAT_REACH)
        tall = [field[c, start : start + block + REACH, w * CELLS : w * CELLS + WINDOW] for c, w in items]
        values = product(toeplitz, low, high, tall, [one[c] for c, w in items])
        for (c, w), value in zip(items, values):
            hidden[c, low + LAT_REACH : high + LAT_REACH, w * CELLS : (w + 1) * CELLS] = erf_gelu(value)

    def second(c, start, pair):
        low, high = max(start, REACH), min(start + block, rows - REACH)
        tall = [hidden[c, start : start + block + REACH, w * CELLS : w * CELLS + WINDOW] for w in pair]
        values = product(toeplitz, low, high, tall, [two[c]] * len(pair))
        at = slice(low - REACH, high - REACH)
        for w, value in zip(pair, values):
            if w in (0, windows - 2):
                ends[c, at, (w > 0) * CELLS : (w > 0) * CELLS + CELLS] = value
        if len(pair) == 2 and pair[0] > 0:
            span = slice((pair[0] - 1) * CELLS, (pair[0] + 1) * CELLS)
            middle[at, span, lanes_of(c)] = jnp.concatenate(values, 1).astype(BF16)

    def export(c):
        for i, row in enumerate((REACH, rows - REACH)):
            part = jnp.concatenate([hidden[c, row : row + REACH], jnp.zeros((REACH, cells - span, LANES), F32)], 1)
            edge_rows[i * REACH : (i + 1) * REACH, :, lanes_of(c)] = part.astype(BF16)
        part = hidden[c, 2 * REACH : rows - REACH]
        edge_cells[:, :, lanes_of(c)] = jnp.concatenate([part[:, :CELLS], part[:, span - CELLS :]], 1).astype(BF16)
        sides[:, :, lanes_of(c)] = ends[c].astype(BF16)

    part = functools.partial
    steps = [([part(load, c)], []) for c in range(chunks)]
    for items in pairs_of([(c, w) for c in range(chunks) for w in range(windows)]):
        steps[items[-1][0]][0].extend(part(first, items, start) for start in starts)
    for c in range(chunks):
        pairs = [[0, windows - 2]] + pairs_of(list(range(1, windows - 2)))
        steps[c][1].extend(part(second, c, start, pair) for start in starts for pair in pairs)
        steps[c][1].append(part(export, c))
    for c in range(chunks - 1, 0, -1):
        if c * windows % 2:
            straddle = steps[c][0][1 : 1 + len(starts)]
            steps[c][0][1 : 1 + len(starts)] = []
            steps[c - 1][0].extend([steps[c][0].pop(0)] + straddle)
    run_mixed(steps)


def ordered(odd, a, b):
    a, b = a.astype(F32), b.astype(F32)
    return jnp.where(odd, a, b), jnp.where(odd, b, a)


def parities():
    return lax.axis_index("lat") % 2 == 1, lax.axis_index("lon") % 2 == 1


def rim_kernel(
    block, x_ref, lat_a, lat_b, lon_b, lon_a, rows_in, cells_in, sides_in, toeplitz, lines_ref, one_ref, two_ref,
    rim_toeplitz, wide_toeplitz, rim_out, side_out, ends, field, hidden,
):
    rows, cells, channels = x_ref.shape
    bases = one_ref.shape[0]
    chunks = channels // LANES
    edge = REACH * cells
    columns = cells // CELLS + 1
    lat_odd, lon_odd = parities()
    one, two = lane_weights(one_ref, 0.5), lane_weights(two_ref)
    kept = list(range(REACH)) + list(range(rows - REACH, rows))

    def place_of(r):
        return r if r < REACH else REACH + r

    tags = ordered(lat_odd, lat_a[edge:, :LANES], lat_b[edge:, :LANES])

    def rim_line(r, k):
        if r < LAT_REACH:
            return tags[0][k * LAT_REACH + r : k * LAT_REACH + r + 1, :]
        if r >= 2 * REACH - LAT_REACH:
            at = k * LAT_REACH + r - (2 * REACH - LAT_REACH)
            return tags[1][at : at + 1, :]
        at = r - LAT_REACH if r < REACH else rows - LAT_REACH + r - REACH
        return lines_ref[k, at : at + 1, :]

    fill_toeplitz(rim_toeplitz, rim_line, 2 * REACH, bases, place_of)
    fill_toeplitz(wide_toeplitz, lambda r, k: lines_ref[k, kept[r] : kept[r] + 1, :], 2 * REACH, bases, place_of)

    def load(c):
        lanes = lanes_of(c)
        lat = ordered(lat_odd, lat_a[:edge, lanes], lat_b[:edge, lanes])
        lon = ordered(lon_odd, lon_a[:, lanes], lon_b[:, lanes])
        inner = slice(REACH, rows - REACH)
        blank = jnp.zeros((REACH, CELLS, LANES), F32)
        for side in range(2):
            at = slice(side * (rows + REACH), side * (rows + REACH) + REACH)
            field[c, at, CELLS : CELLS + cells] = lat[side].reshape(REACH, cells, LANES)
            own = slice(side * (rows - REACH), side * (rows - REACH) + REACH)
            at = slice(own.start + REACH, own.stop + REACH)
            field[c, at, CELLS : CELLS + cells] = x_ref[own, :, lanes].astype(F32)
            own = slice(side * (cells - TILE), side * (cells - TILE) + TILE)
            at = slice(own.start + CELLS, own.stop + CELLS)
            field[c, 2 * REACH : rows, at] = x_ref[inner, own, lanes].astype(F32)
            span = slice(side * (CELLS + cells), side * (CELLS + cells) + CELLS)
            field[c, REACH : REACH + rows, span] = lon[side].reshape(rows, CELLS, LANES)
            for end in range(2):
                at = slice(end * (rows + REACH), end * (rows + REACH) + REACH)
                field[c, at, span] = blank
                hidden[c, end * rows : end * rows + REACH, side * cells : side * cells + CELLS] = blank
        span = cells - CELLS
        for i, at in enumerate((REACH, rows - REACH)):
            part = rows_in[i * REACH : (i + 1) * REACH, :, lanes].astype(F32)
            hidden[c, at : at + REACH, CELLS : CELLS + span] = part[:, :span]
        part = cells_in[:, :, lanes].astype(F32)
        at = slice(2 * REACH, rows - REACH)
        hidden[c, at, CELLS : 2 * CELLS] = part[:, :CELLS]
        hidden[c, at, cells - CELLS : cells] = part[:, CELLS:]

    def rims(ref, c, span):
        last = ref.shape[1] - 2 * REACH
        return jnp.concatenate([ref[c, : 2 * REACH, span], ref[c, last:, span]], 0)

    def first_rows(items):
        tall = [rims(field, c, slice(w * CELLS, w * CELLS + WINDOW)) for c, w in items]
        values = product(rim_toeplitz, 0, 2 * REACH, tall, [one[c] for c, w in items])
        for (c, w), value in zip(items, values):
            value = erf_gelu(value)
            hidden[c, :REACH, w * CELLS : (w + 1) * CELLS] = value[:REACH]
            hidden[c, rows:, w * CELLS : (w + 1) * CELLS] = value[REACH:]

    def first_sides(c, start):
        low, high = max(start, LAT_REACH), min(start + block, rows - LAT_REACH)
        at = slice(start + LAT_REACH, start + LAT_REACH + block + REACH)
        tall = [field[c, at, s : s + WINDOW] for s in (0, cells)]
        values = product(toeplitz, low, high, tall, [one[c]] * 2)
        for s, value in zip((0, cells), values):
            hidden[c, low + LAT_REACH : high + LAT_REACH, s : s + CELLS] = erf_gelu(value)

    def second_rows(c, pair):
        tall = [rims(hidden, c, slice(w * CELLS, w * CELLS + WINDOW)) for w in pair]
        values = product(wide_toeplitz, 0, 2 * REACH, tall, [two[c]] * 2)
        blank = jnp.zeros((2 * REACH, CELLS, LANES), F32)
        if pair == [1, columns - 3]:
            rim_out[:, :TILE, lanes_of(c)] = jnp.concatenate([blank, values[0]], 1).astype(BF16)
            rim_out[:, cells - TILE :, lanes_of(c)] = jnp.concatenate([values[1], blank], 1).astype(BF16)
        else:
            rim_out[:, pair[0] * CELLS : (pair[0] + 2) * CELLS, lanes_of(c)] = jnp.concatenate(values, 1).astype(BF16)

    def second_sides(c, start):
        low, high = max(start, REACH), min(start + block, rows - REACH)
        tall = [hidden[c, start : start + block + REACH, s : s + WINDOW] for s in (0, cells - CELLS)]
        values = product(toeplitz, low, high, tall, [two[c]] * 2)
        at = slice(low - REACH, high - REACH)
        inner = sides_in[at, :, lanes_of(c)].astype(F32)
        side_out[0, at, :, lanes_of(c)] = jnp.concatenate([values[0], inner[:, :CELLS]], 1).astype(BF16)
        side_out[1, at, :, lanes_of(c)] = jnp.concatenate([inner[:, CELLS:], values[1]], 1).astype(BF16)

    def export(c):
        for side in range(2):
            span = slice(side * (cells - CELLS), side * (cells - CELLS) + WINDOW)
            ends[side, :, :, lanes_of(c)] = rims(hidden, c, span).astype(BF16)

    part = functools.partial
    steps = [([part(load, c)], []) for c in range(chunks)]
    items = [(c, w) for c in range(chunks) for w in range(1, columns - 1)]
    for pair in pairs_of(items):
        steps[pair[-1][0]][0].append(part(first_rows, pair))
    for c in range(chunks - 1, 0, -1):
        if c * (columns - 2) % 2:
            steps[c - 1][0].extend([steps[c][0].pop(0), steps[c][0].pop(0)])
    starts = range(0, rows, block)
    for c, (first, second) in enumerate(steps):
        first.extend(part(first_sides, c, start) for start in starts)
        second.extend(
            part(second_rows, c, pair) for pair in [[1, columns - 3]] + pairs_of(list(range(2, columns - 3)))
        )
        second.extend(part(second_sides, c, start) for start in starts)
        second.append(part(export, c))
    run_mixed(steps)


def corner_kernel(
    x_ref, lat_a, lat_b, lon_b, lon_a, corner_b, corner_a, ends, rim_toeplitz, wide_toeplitz, one_ref, two_ref,
    middle, side_out, rim_out, out_ref, corner_out, sems,
):
    rows, cells, channels = x_ref.shape
    chunks = channels // LANES
    edge = REACH * cells
    inner = pl.ds(REACH, rows - 2 * REACH)
    ends_at = (pl.ds(0, REACH), pl.ds(rows - REACH, REACH))
    sides_at = (pl.ds(0, TILE), pl.ds(cells - TILE, TILE))
    span = pl.ds(TILE, cells - 2 * TILE)
    moves = [(middle, out_ref.at[inner, span])]
    for i in range(2):
        moves.append((side_out.at[i], out_ref.at[inner, sides_at[i]]))
        moves.append((rim_out.at[pl.ds(i * REACH, REACH), span], out_ref.at[ends_at[i], span]))
    copies = [pltpu.make_async_copy(source, target, sems.at[i]) for i, (source, target) in enumerate(moves)]
    for copy in copies:
        copy.start()
    lat_odd, lon_odd = parities()
    one, two = lane_weights(one_ref, 0.5), lane_weights(two_ref)

    def first(c):
        lanes = lanes_of(c)
        lat = ordered(lat_odd, lat_a[:edge, lanes], lat_b[:edge, lanes])
        lon = ordered(lon_odd, lon_a[:, lanes], lon_b[:, lanes])
        corner = ordered(lon_odd, corner_a[:, lanes], corner_b[:, lanes])
        tall = []
        for side in range(2):
            own = slice(side * (cells - CELLS), side * (cells - CELLS) + CELLS)
            above = [v.reshape(REACH, cells, LANES)[:, own] for v in lat]
            tiles = slice(side * (cells - TILE), side * (cells - TILE) + TILE)
            half = slice(side * (TILE - CELLS), side * (TILE - CELLS) + CELLS)
            mine = [x_ref[r : r + REACH, tiles, lanes].astype(F32)[:, half] for r in (0, rows - REACH)]
            near = lon[side].reshape(rows, CELLS, LANES)
            far = ordered(lat_odd, corner[side][: REACH * CELLS], corner[side][REACH * CELLS :])
            far = [v.reshape(REACH, CELLS, LANES) for v in far]
            own = jnp.concatenate([above[0], mine[0], mine[1], above[1]], 0)
            other = jnp.concatenate([far[0], near[:REACH], near[rows - REACH :], far[1]], 0)
            tall.append(jnp.concatenate([own, other] if side else [other, own], 1))
        return [erf_gelu(v) for v in product(rim_toeplitz, 0, 2 * REACH, tall, [one[c]] * 2)]

    def second(c, blocks):
        lanes = lanes_of(c)
        tall = []
        for side in range(2):
            near = ends[side, :, :, lanes].astype(F32)
            own = near[:, side * CELLS : side * CELLS + CELLS]
            own = jnp.concatenate([blocks[side][:REACH], own[REACH : 3 * REACH], blocks[side][REACH:]], 0)
            tall.append(jnp.concatenate([near[:, :CELLS], own] if side else [own, near[:, CELLS:]], 1))
        values = product(wide_toeplitz, 0, 2 * REACH, tall, [two[c]] * 2)
        for side in range(2):
            tiles = slice(side * (cells - TILE), side * (cells - TILE) + TILE)
            near = rim_out[:, tiles, lanes].astype(F32)
            near = near[:, : TILE - CELLS] if side else near[:, CELLS:]
            whole = [near, values[side]] if side else [values[side], near]
            corner_out[side, :, :, lanes] = jnp.concatenate(whole, 1).astype(BF16)

    hidden = [first(c) for c in range(chunks)]
    for c in range(chunks):
        second(c, hidden[c])
    last = []
    for side in range(2):
        for end in range(2):
            source = corner_out.at[side, pl.ds(end * REACH, REACH)]
            target = out_ref.at[ends_at[end], sides_at[side]]
            last.append(pltpu.make_async_copy(source, target, sems.at[len(copies) + len(last)]))
            last[-1].start()
    for copy in copies + last:
        copy.wait()


def per_device(state_field, filters, band_edges, basis_mask, weights_one, weights_two):
    rows, cells, channels = state_field.shape
    bases = filters.shape[1]
    group = bases * CELLS
    chunks = channels // LANES
    tiles = cells // TILE
    edge = REACH * cells
    block = max(b for b in range(2, rows + 1, 2) if rows % b == 0 and (b + REACH) * WINDOW <= DEPTH)
    lat_peers, lon_peers = lax.axis_size("lat"), lax.axis_size("lon")
    lon = lax.axis_index("lon")

    anywhere = pl.BlockSpec(memory_space=pl.ANY)
    vmem = pl.BlockSpec(memory_space=pltpu.VMEM)
    params = pltpu.CompilerParams(vmem_limit_bytes=VMEM_BYTES)
    dma = pltpu.SemaphoreType.DMA

    def array(*shape, dtype=BF16):
        return jax.ShapeDtypeStruct(shape, dtype)

    def scratch(*shape, dtype=BF16):
        return pltpu.VMEM(shape, dtype)

    groups = REACH * tiles
    filter_args = (filters.transpose(1, 3, 2, 0), band_edges.T, basis_mask.T)
    lat_a, lat_b, lon_a, lon_b = pl.pallas_call(
        prep_kernel,
        out_shape=(
            array(groups + 1, TILE, channels), array(groups + 1, TILE, channels),
            array(rows * CELLS, channels), array(rows * CELLS, channels),
        ),
        in_specs=[anywhere] * 5,
        out_specs=(vmem,) * 4,
        scratch_shapes=[
            scratch(bases, filters.shape[3], BANDS, rows, dtype=F32),
            scratch(2, rows, dtype=jnp.int32), scratch(bases, rows, dtype=jnp.int32),
            scratch(2, rows, TILE, channels), scratch(bases, LANES, LANES, dtype=F32),
            scratch(2, TILE, LANES, dtype=F32), dma((7,)),
        ],
        compiler_params=pltpu.CompilerParams(vmem_limit_bytes=60 * 1024 * 1024),
        cost_estimate=pl.CostEstimate(flops=0, bytes_accessed=4 * edge * channels, transcendentals=0),
        name="prep",
    )(
        state_field.reshape(rows * tiles, TILE, channels), state_field.reshape(rows, tiles, TILE, channels),
        *filter_args,
    )
    both = ("lat", "lon")
    lat_a = lax.ppermute(lat_a, both, lat_swaps(lat_peers, lon_peers, False)).reshape(edge + TILE, channels)
    lat_b = lax.ppermute(lat_b, both, lat_swaps(lat_peers, lon_peers, True)).reshape(edge + TILE, channels)
    lon_b = lax.ppermute(lon_b, "lon", swaps(lon_peers, True))
    lon_a = lax.ppermute(lon_a, "lon", swaps(lon_peers, False))

    middle = rows - 2 * REACH
    flops = 2 * (2 * rows - 3 * REACH) * (cells - 2 * CELLS) * bases * DEPTH * channels
    cost = pl.CostEstimate(flops=flops, bytes_accessed=4 * state_field.size, transcendentals=0)
    toeplitz, lines, edge_rows, edge_cells, sides, inner = pl.pallas_call(
        functools.partial(inner_kernel, block),
        out_shape=(
            array(rows * group, DEPTH), array(bases, rows, LANES, dtype=F32),
            array(2 * REACH, cells, channels), array(middle - REACH, TILE, channels),
            array(middle, TILE, channels), array(middle, cells - 2 * TILE, channels),
        ),
        in_specs=[vmem] * 6,
        out_specs=(vmem,) * 6,
        scratch_shapes=[
            scratch(bases, LANES, LANES, dtype=F32),
            scratch(chunks, rows + REACH, cells, LANES, dtype=F32),
            scratch(chunks, rows + REACH, cells - CELLS, LANES, dtype=F32),
            scratch(chunks, middle, TILE, LANES, dtype=F32),
        ],
        compiler_params=params,
        cost_estimate=cost,
        name="inner",
    )(state_field, *filter_args, weights_one, weights_two)

    def corner_send(leading, second):
        start = jnp.where(leading, 0, cells - CELLS)
        joined = [v[:edge].reshape(REACH, cells, channels) for v in (lat_a, lat_b)]
        parts = [lax.dynamic_slice_in_dim(v, start, CELLS, 1) for v in joined]
        sent = jnp.concatenate(parts, 0).reshape(2 * REACH * CELLS, channels)
        return lax.ppermute(sent, "lon", swaps(lon_peers, second))

    lat_a, lat_b, inner = lax.optimization_barrier((lat_a, lat_b, inner))
    corner_b = corner_send(lon % 2 == 0, True)
    corner_a = corner_send(lon % 2 == 1, False)
    rim_toeplitz, wide_toeplitz, rim_out, side_out, ends = pl.pallas_call(
        functools.partial(rim_kernel, block),
        out_shape=(
            array(2 * REACH * group, DEPTH), array(2 * REACH * group, DEPTH), array(2 * REACH, cells, channels),
            array(2, middle, TILE, channels), array(2, 4 * REACH, WINDOW, channels),
        ),
        in_specs=[vmem] * 12,
        out_specs=(vmem,) * 5,
        scratch_shapes=[
            scratch(chunks, rows + 2 * REACH, cells + 2 * CELLS, LANES, dtype=F32),
            scratch(chunks, rows + REACH, cells + CELLS, LANES, dtype=F32),
        ],
        compiler_params=params,
        cost_estimate=cost,
        name="rim",
    )(
        state_field, lat_a, lat_b, lon_b, lon_a, edge_rows, edge_cells, sides, toeplitz, lines,
        weights_one, weights_two,
    )
    return pl.pallas_call(
        corner_kernel,
        out_shape=array(rows, cells, channels),
        in_specs=[vmem] * 15,
        out_specs=anywhere,
        scratch_shapes=[scratch(2, 2 * REACH, TILE, channels), dma((9,))],
        compiler_params=params,
        cost_estimate=cost,
        name="corner",
    )(
        state_field, lat_a, lat_b, lon_b, lon_a, corner_b, corner_a, ends, rim_toeplitz, wide_toeplitz,
        weights_one, weights_two, inner, side_out, rim_out,
    )


def solution(mesh):
    placed = (
        P("lat", "lon", None),
        P("lat", None, None, None),
        P("lat", None),
        P("lat", None),
        P(),
        P(),
    )
    return jax.shard_map(
        per_device, mesh=mesh, in_specs=placed, out_specs=P("lat", "lon", None), check_vma=False
    )
```

```python
import functools

import jax
import jax.numpy as jnp
from jax import lax
from jax.experimental import pallas as pl
from jax.experimental.pallas import tpu as pltpu
from jax.sharding import PartitionSpec as P

LAT_REACH = 2
LON_REACH = 4
REACH = 2 * LAT_REACH
BANDS = 2 * LAT_REACH + 1
CELLS = 8
WINDOW = CELLS + 2 * LON_REACH
LANES = 128
DEPTH = 2 * LANES
TILE = 16
VMEM_BYTES = 20 * 1024 * 1024
PIECE = 4
F32, BF16 = jnp.float32, jnp.bfloat16

ERF_SERIES = (
    1.5956562720156744,
    0.2917503271976864,
    -0.003995570947534282,
    -0.003914369984884403,
    0.0005729703632347449,
)


def erf_gelu(half):
    square = half * half
    series = ERF_SERIES[-1] * square + ERF_SERIES[-2]
    for term in ERF_SERIES[-3::-1]:
        series = series * square + term
    return half + half * jnp.tanh(half * series)


def swaps(peers, second):
    pairs = [(i, i + 1) for i in range(1 if second else 0, peers - 1, 2)]
    if second:
        pairs.append((peers - 1, 0))
    return pairs + [(j, i) for i, j in pairs]


def lat_swaps(peers, width, second):
    pairs = [(i, i + 1) for i in range(1 if second else 0, peers - 1, 2)]
    pairs += [(j, i) for i, j in pairs]
    alone = set(range(peers)) - {i for i, _ in pairs}
    result = [(i * width + k, j * width + k) for i, j in pairs for k in range(width)]
    return result + [(i * width + k, i * width + (k ^ 1)) for i in sorted(alone) for k in range(width)]


def pairs_of(items):
    return [items[i : i + 2] for i in range(0, len(items), 2)]


def lanes_of(chunk):
    return slice(chunk * LANES, (chunk + 1) * LANES)


def fill_toeplitz(toeplitz, line_of, rows, bases, place_of, pairs=None):
    group = bases * CELLS
    blank = jnp.zeros((CELLS, DEPTH - LANES), F32)
    for row in pairs or range(0, rows, 2):
        parts = []
        for r in (row, row + 1):
            for basis in range(bases):
                line = jnp.broadcast_to(line_of(r, basis), (CELLS, LANES))
                line = jnp.concatenate([line, blank], 1)
                parts.append(pltpu.roll(line, place_of(r) * WINDOW, 1, stride=1, stride_axis=0))
        toeplitz[row * group : (row + 2) * group, :] = jnp.concatenate(parts, 0).astype(BF16)


def lane_weights(ref, scale=1.0):
    bases, channels = ref.shape
    return [[ref[k : k + 1, lanes_of(c)] * scale for k in range(bases)] for c in range(channels // LANES)]


def product(matrix, low, high, windows, weights):
    wide = [w.astype(BF16).reshape(DEPTH, LANES) for w in windows]
    wide = jnp.concatenate(wide, 1)
    bases = len(weights[0])
    group = bases * CELLS
    scales = [jnp.concatenate([w[k] for w in weights], 1) for k in range(bases)]
    pieces = []
    for at in range(low, high, PIECE):
        to = min(at + PIECE, high)
        result = jnp.dot(matrix[at * group : to * group, :], wide, preferred_element_type=F32)
        result = result.reshape(to - at, bases, CELLS, len(windows) * LANES)
        total = result[:, 0] * scales[0]
        for k in range(1, bases):
            total = total + result[:, k] * scales[k]
        pieces.append(total)
    total = jnp.concatenate(pieces, 0) if len(pieces) > 1 else pieces[0]
    return [total[:, :, i * LANES : (i + 1) * LANES] for i in range(len(windows))]


def run_mixed(steps):
    waiting = []
    for first, second in steps:
        share = -(-len(waiting) // max(len(first), 1))
        for unit in first:
            unit()
            for _ in range(min(share, len(waiting))):
                waiting.pop(0)()
        for unit in waiting:
            unit()
        waiting = list(second)
    for unit in waiting:
        unit()


def line_choice(lags):
    at = lax.broadcasted_iota(jnp.int32, (LANES, LANES), 0)
    lane = lax.broadcasted_iota(jnp.int32, (LANES, LANES), 1)
    chosen = (at // 8 == lane % WINDOW) & (at % 8 == lane // WINDOW) & (at % 8 < BANDS) & (at // 8 < lags)
    return jnp.where(chosen, 1.0, 0.0).astype(BF16)


def filter_lines(filter_ref, edge_ref, mask_ref, padded, chosen):
    bases, lags, bands, rows = filter_ref.shape
    source = lax.axis_index("lat") * rows + lax.broadcasted_iota(jnp.int32, (bands, rows), 1) - LAT_REACH
    source = source + lax.broadcasted_iota(jnp.int32, (bands, rows), 0)
    inside = (source >= edge_ref[0:1, :]) & (source < edge_ref[1:2, :])
    for k in range(bases):
        keep = inside & (mask_ref[k : k + 1, :] != 0)
        for m in range(lags):
            padded[k, m * 8 : m * 8 + bands, :rows] = jnp.where(keep, filter_ref[k, m], 0.0)
    return [jnp.dot(padded[k].T.astype(BF16), chosen, preferred_element_type=F32) for k in range(bases)]


def prep_kernel(
    flat_ref, groups_ref, filter_in, edge_in, mask_in, lat_a, lat_b, lon_a, lon_b,
    filter_ref, edge_ref, mask_ref, ends, sides, padded, tags, packed, sems, out_sems,
):
    bases, lags, bands, rows = filter_in.shape
    across = groups_ref.shape[1]
    edge = REACH * across
    lat_odd, lon_odd = lax.axis_index("lat") % 2, lax.axis_index("lon") % 2
    firsts = (1 - lat_odd, lat_odd)
    small = [
        pltpu.make_async_copy(filter_in, filter_ref, sems.at[0]),
        pltpu.make_async_copy(edge_in, edge_ref, sems.at[1]),
        pltpu.make_async_copy(mask_in, mask_ref, sems.at[2]),
    ]
    rows_in, cells_in = [], []
    for i in range(2):
        place = pl.ds(firsts[i] * (rows - REACH) * across, edge)
        rows_in.append(pltpu.make_async_copy(flat_ref.at[place], ends.at[i], sems.at[3 + i]))
        place = (1 - lon_odd if i == 0 else lon_odd) * (across - 1)
        cells_in.append(pltpu.make_async_copy(groups_ref.at[:, place], sides.at[i], sems.at[5 + i]))
    for copy in rows_in + small + cells_in:
        copy.start()
    padded[...] = jnp.zeros_like(padded)
    tags[...] = jnp.zeros_like(tags)
    chosen = line_choice(lags)
    pending = []

    def send(source, target):
        pending.append(pltpu.make_async_copy(source, target, out_sems.at[len(pending)]))
        pending[-1].start()

    for i, out in enumerate((lat_a, lat_b)):
        rows_in[i].wait()
        send(ends.at[i], out.at[pl.ds(0, edge)])
    for copy in small:
        copy.wait()
    for k, line in enumerate(filter_lines(filter_ref, edge_ref, mask_ref, padded, chosen)):
        tags[0, :LAT_REACH, lanes_of(k)] = line[:LAT_REACH]
        tags[1, :LAT_REACH, lanes_of(k)] = line[rows - LAT_REACH : rows]
    odd = lat_odd == 1
    packed[0] = jnp.where(odd, tags[0], tags[1]).astype(BF16)
    packed[1] = jnp.where(odd, tags[1], tags[0]).astype(BF16)
    for i, out in enumerate((lat_a, lat_b)):
        send(packed.at[i], out.at[edge])
    for i, out in enumerate((lon_a, lon_b)):
        cells_in[i].wait()
        send(sides.at[i], out)
    for copy in pending:
        copy.wait()


def place_of(r):
    return r if r < REACH else REACH + r


def inner_kernel(
    block, x_ref, filter_ref, edge_ref, mask_ref, one_ref, two_ref,
    toeplitz, rim_toeplitz, wide_toeplitz, edge_rows, edge_cells, sides, out_ref,
    middle, padded, field, hidden, ends, sems,
):
    rows, cells, channels = x_ref.shape
    bases = one_ref.shape[0]
    chunks = channels // LANES
    padded[...] = jnp.zeros_like(padded)
    chosen = line_choice(filter_ref.shape[1])
    lines = filter_lines(filter_ref, edge_ref, mask_ref, padded, chosen)
    fill_toeplitz(toeplitz, lambda r, k: lines[k][r : r + 1, :], rows, bases, lambda r: r % block)
    kept = list(range(REACH)) + list(range(rows - REACH, rows))
    fill_toeplitz(wide_toeplitz, lambda r, k: lines[k][kept[r] : kept[r] + 1, :], 2 * REACH, bases, place_of)
    shifted = [r - LAT_REACH for r in range(REACH)] + [rows - LAT_REACH + r for r in range(REACH)]
    own = range(LAT_REACH, 2 * REACH - LAT_REACH, 2)
    rim_toeplitz[...] = jnp.zeros_like(rim_toeplitz)
    fill_toeplitz(
        rim_toeplitz, lambda r, k: lines[k][shifted[r] : shifted[r] + 1, :], 2 * REACH, bases, place_of, own
    )
    one, two = lane_weights(one_ref, 0.5), lane_weights(two_ref)
    starts = range(0, rows, block)
    windows = (cells - WINDOW) // CELLS + 1
    span = windows * CELLS

    def load(c):
        blank = jnp.zeros((LAT_REACH, cells, LANES), F32)
        field[c, :LAT_REACH] = blank
        field[c, LAT_REACH : LAT_REACH + rows] = x_ref[:, :, lanes_of(c)].astype(F32)
        field[c, LAT_REACH + rows :] = blank
        blank = jnp.zeros((REACH, span, LANES), F32)
        hidden[c, :REACH] = blank
        hidden[c, rows:] = blank

    def first(items, start):
        low, high = max(start, LAT_REACH), min(start + block, rows - LAT_REACH)
        tall = [field[c, start : start + block + REACH, w * CELLS : w * CELLS + WINDOW] for c, w in items]
        values = product(toeplitz, low, high, tall, [one[c] for c, w in items])
        for (c, w), value in zip(items, values):
            hidden[c, low + LAT_REACH : high + LAT_REACH, w * CELLS : (w + 1) * CELLS] = erf_gelu(value)

    def second(c, start, pair):
        low, high = max(start, REACH), min(start + block, rows - REACH)
        tall = [hidden[c, start : start + block + REACH, w * CELLS : w * CELLS + WINDOW] for w in pair]
        values = product(toeplitz, low, high, tall, [two[c]] * len(pair))
        at = slice(low - REACH, high - REACH)
        for w, value in zip(pair, values):
            if w in (0, windows - 2):
                ends[c, at, (w > 0) * CELLS : (w > 0) * CELLS + CELLS] = value
        if len(pair) == 2 and pair[0] > 0:
            span = slice((pair[0] - 1) * CELLS, (pair[0] + 1) * CELLS)
            middle[at, span, lanes_of(c)] = jnp.concatenate(values, 1).astype(BF16)

    def export(c):
        for i, row in enumerate((REACH, rows - REACH)):
            part = jnp.concatenate([hidden[c, row : row + REACH], jnp.zeros((REACH, cells - span, LANES), F32)], 1)
            edge_rows[i * REACH : (i + 1) * REACH, :, lanes_of(c)] = part.astype(BF16)
        part = hidden[c, 2 * REACH : rows - REACH]
        edge_cells[:, :, lanes_of(c)] = jnp.concatenate([part[:, :CELLS], part[:, span - CELLS :]], 1).astype(BF16)
        sides[:, :, lanes_of(c)] = ends[c].astype(BF16)

    part = functools.partial
    steps = [([part(load, c)], []) for c in range(chunks)]
    for items in pairs_of([(c, w) for c in range(chunks) for w in range(windows)]):
        steps[items[-1][0]][0].extend(part(first, items, start) for start in starts)
    for c in range(chunks):
        pairs = [[0, windows - 2]] + pairs_of(list(range(1, windows - 2)))
        steps[c][1].extend(part(second, c, start, pair) for start in starts for pair in pairs)
        steps[c][1].append(part(export, c))
    for c in range(chunks - 1, 0, -1):
        if c * windows % 2:
            straddle = steps[c][0][1 : 1 + len(starts)]
            steps[c][0][1 : 1 + len(starts)] = []
            steps[c - 1][0].extend([steps[c][0].pop(0)] + straddle)
    run_mixed(steps)
    target = out_ref.at[pl.ds(REACH, rows - 2 * REACH), pl.ds(TILE, cells - 2 * TILE)]
    copy = pltpu.make_async_copy(middle, target, sems.at[0])
    copy.start()
    copy.wait()


def ordered(odd, a, b):
    a, b = a.astype(F32), b.astype(F32)
    return jnp.where(odd, a, b), jnp.where(odd, b, a)


def parities():
    return lax.axis_index("lat") % 2 == 1, lax.axis_index("lon") % 2 == 1


def rim_kernel(
    block, x_ref, lat_a, lat_b, lon_b, lon_a, rows_in, cells_in, sides_in,
    toeplitz, known_toeplitz, wide_toeplitz, one_ref, two_ref,
    rim_toeplitz, rim_out, side_out, ends, field, hidden,
):
    rows, cells, channels = x_ref.shape
    bases = one_ref.shape[0]
    chunks = channels // LANES
    group = bases * CELLS
    edge = REACH * (cells // CELLS)
    columns = cells // CELLS + 1
    lat_odd, lon_odd = parities()
    one, two = lane_weights(one_ref, 0.5), lane_weights(two_ref)
    tags = ordered(lat_odd, lat_a[edge], lat_b[edge])

    def tag_line(r, k):
        at = r % LAT_REACH
        return tags[0 if r < REACH else 1][at : at + 1, lanes_of(k)]

    own = slice(LAT_REACH * group, (2 * REACH - LAT_REACH) * group)
    rim_toeplitz[own, :] = known_toeplitz[own, :]
    fill_toeplitz(rim_toeplitz, tag_line, 2 * REACH, bases, place_of, (0, 2 * REACH - LAT_REACH))

    def load(c):
        lanes = lanes_of(c)
        lat = ordered(lat_odd, lat_a[:edge, :, lanes], lat_b[:edge, :, lanes])
        lon = ordered(lon_odd, lon_a[:, :, lanes], lon_b[:, :, lanes])
        inner = slice(REACH, rows - REACH)
        blank = jnp.zeros((REACH, CELLS, LANES), F32)
        for side in range(2):
            at = slice(side * (rows + REACH), side * (rows + REACH) + REACH)
            field[c, at, CELLS : CELLS + cells] = lat[side].reshape(REACH, cells, LANES)
            own = slice(side * (rows - REACH), side * (rows - REACH) + REACH)
            at = slice(own.start + REACH, own.stop + REACH)
            field[c, at, CELLS : CELLS + cells] = x_ref[own, :, lanes].astype(F32)
            own = slice(side * (cells - TILE), side * (cells - TILE) + TILE)
            at = slice(own.start + CELLS, own.stop + CELLS)
            field[c, 2 * REACH : rows, at] = x_ref[inner, own, lanes].astype(F32)
            span = slice(side * (CELLS + cells), side * (CELLS + cells) + CELLS)
            field[c, REACH : REACH + rows, span] = lon[side]
            for end in range(2):
                at = slice(end * (rows + REACH), end * (rows + REACH) + REACH)
                field[c, at, span] = blank
                hidden[c, end * rows : end * rows + REACH, side * cells : side * cells + CELLS] = blank
        span = cells - CELLS
        for i, at in enumerate((REACH, rows - REACH)):
            part = rows_in[i * REACH : (i + 1) * REACH, :, lanes].astype(F32)
            hidden[c, at : at + REACH, CELLS : CELLS + span] = part[:, :span]
        part = cells_in[:, :, lanes].astype(F32)
        at = slice(2 * REACH, rows - REACH)
        hidden[c, at, CELLS : 2 * CELLS] = part[:, :CELLS]
        hidden[c, at, cells - CELLS : cells] = part[:, CELLS:]

    def rims(ref, c, span):
        last = ref.shape[1] - 2 * REACH
        return jnp.concatenate([ref[c, : 2 * REACH, span], ref[c, last:, span]], 0)

    def first_rows(items):
        tall = [rims(field, c, slice(w * CELLS, w * CELLS + WINDOW)) for c, w in items]
        values = product(rim_toeplitz, 0, 2 * REACH, tall, [one[c] for c, w in items])
        for (c, w), value in zip(items, values):
            value = erf_gelu(value)
            hidden[c, :REACH, w * CELLS : (w + 1) * CELLS] = value[:REACH]
            hidden[c, rows:, w * CELLS : (w + 1) * CELLS] = value[REACH:]

    def first_sides(c, start):
        low, high = max(start, LAT_REACH), min(start + block, rows - LAT_REACH)
        at = slice(start + LAT_REACH, start + LAT_REACH + block + REACH)
        tall = [field[c, at, s : s + WINDOW] for s in (0, cells)]
        values = product(toeplitz, low, high, tall, [one[c]] * 2)
        for s, value in zip((0, cells), values):
            hidden[c, low + LAT_REACH : high + LAT_REACH, s : s + CELLS] = erf_gelu(value)

    def second_rows(c, pair):
        tall = [rims(hidden, c, slice(w * CELLS, w * CELLS + WINDOW)) for w in pair]
        values = product(wide_toeplitz, 0, 2 * REACH, tall, [two[c]] * 2)
        blank = jnp.zeros((2 * REACH, CELLS, LANES), F32)
        if pair == [1, columns - 3]:
            rim_out[:, :TILE, lanes_of(c)] = jnp.concatenate([blank, values[0]], 1).astype(BF16)
            rim_out[:, cells - TILE :, lanes_of(c)] = jnp.concatenate([values[1], blank], 1).astype(BF16)
        else:
            rim_out[:, pair[0] * CELLS : (pair[0] + 2) * CELLS, lanes_of(c)] = jnp.concatenate(values, 1).astype(BF16)

    def second_sides(c, start):
        low, high = max(start, REACH), min(start + block, rows - REACH)
        tall = [hidden[c, start : start + block + REACH, s : s + WINDOW] for s in (0, cells - CELLS)]
        values = product(toeplitz, low, high, tall, [two[c]] * 2)
        at = slice(low - REACH, high - REACH)
        inner = sides_in[at, :, lanes_of(c)].astype(F32)
        side_out[0, at, :, lanes_of(c)] = jnp.concatenate([values[0], inner[:, :CELLS]], 1).astype(BF16)
        side_out[1, at, :, lanes_of(c)] = jnp.concatenate([inner[:, CELLS:], values[1]], 1).astype(BF16)

    def export(c):
        for side in range(2):
            span = slice(side * (cells - CELLS), side * (cells - CELLS) + WINDOW)
            ends[side, :, :, lanes_of(c)] = rims(hidden, c, span).astype(BF16)

    part = functools.partial
    steps = [([part(load, c)], []) for c in range(chunks)]
    items = [(c, w) for c in range(chunks) for w in range(1, columns - 1)]
    for pair in pairs_of(items):
        steps[pair[-1][0]][0].append(part(first_rows, pair))
    for c in range(chunks - 1, 0, -1):
        if c * (columns - 2) % 2:
            steps[c - 1][0].extend([steps[c][0].pop(0), steps[c][0].pop(0)])
    starts = range(0, rows, block)
    for c, (first, second) in enumerate(steps):
        first.extend(part(first_sides, c, start) for start in starts)
        second.extend(
            part(second_rows, c, pair) for pair in [[1, columns - 3]] + pairs_of(list(range(2, columns - 3)))
        )
        second.extend(part(second_sides, c, start) for start in starts)
        second.append(part(export, c))
    run_mixed(steps)


def corner_kernel(
    x_ref, lat_a, lat_b, lon_b, lon_a, corner_b, corner_a, ends, rim_toeplitz, wide_toeplitz, one_ref, two_ref,
    side_out, rim_out, begun_ref, out_ref, corner_out, sems,
):
    del begun_ref
    rows, cells, channels = x_ref.shape
    chunks = channels // LANES
    edge = REACH * (cells // CELLS)
    inner = pl.ds(REACH, rows - 2 * REACH)
    ends_at = (pl.ds(0, REACH), pl.ds(rows - REACH, REACH))
    sides_at = (pl.ds(0, TILE), pl.ds(cells - TILE, TILE))
    span = pl.ds(TILE, cells - 2 * TILE)
    moves = []
    for i in range(2):
        moves.append((side_out.at[i], out_ref.at[inner, sides_at[i]]))
        moves.append((rim_out.at[pl.ds(i * REACH, REACH), span], out_ref.at[ends_at[i], span]))
    copies = [pltpu.make_async_copy(source, target, sems.at[i]) for i, (source, target) in enumerate(moves)]
    for copy in copies:
        copy.start()
    lat_odd, lon_odd = parities()
    one, two = lane_weights(one_ref, 0.5), lane_weights(two_ref)

    def first(c):
        lanes = lanes_of(c)
        lat = ordered(lat_odd, lat_a[:edge, :, lanes], lat_b[:edge, :, lanes])
        lon = ordered(lon_odd, lon_a[:, :, lanes], lon_b[:, :, lanes])
        corner = ordered(lon_odd, corner_a[:, lanes], corner_b[:, lanes])
        tall = []
        for side in range(2):
            own = slice(side * (cells - CELLS), side * (cells - CELLS) + CELLS)
            above = [v.reshape(REACH, cells, LANES)[:, own] for v in lat]
            tiles = slice(side * (cells - TILE), side * (cells - TILE) + TILE)
            half = slice(side * (TILE - CELLS), side * (TILE - CELLS) + CELLS)
            mine = [x_ref[r : r + REACH, tiles, lanes].astype(F32)[:, half] for r in (0, rows - REACH)]
            near = lon[side]
            far = ordered(lat_odd, corner[side][: REACH * CELLS], corner[side][REACH * CELLS :])
            far = [v.reshape(REACH, CELLS, LANES) for v in far]
            own = jnp.concatenate([above[0], mine[0], mine[1], above[1]], 0)
            other = jnp.concatenate([far[0], near[:REACH], near[rows - REACH :], far[1]], 0)
            tall.append(jnp.concatenate([own, other] if side else [other, own], 1))
        return [erf_gelu(v) for v in product(rim_toeplitz, 0, 2 * REACH, tall, [one[c]] * 2)]

    def second(c, blocks):
        lanes = lanes_of(c)
        tall = []
        for side in range(2):
            near = ends[side, :, :, lanes].astype(F32)
            own = near[:, side * CELLS : side * CELLS + CELLS]
            own = jnp.concatenate([blocks[side][:REACH], own[REACH : 3 * REACH], blocks[side][REACH:]], 0)
            tall.append(jnp.concatenate([near[:, :CELLS], own] if side else [own, near[:, CELLS:]], 1))
        values = product(wide_toeplitz, 0, 2 * REACH, tall, [two[c]] * 2)
        for side in range(2):
            tiles = slice(side * (cells - TILE), side * (cells - TILE) + TILE)
            near = rim_out[:, tiles, lanes].astype(F32)
            near = near[:, : TILE - CELLS] if side else near[:, CELLS:]
            whole = [near, values[side]] if side else [values[side], near]
            corner_out[side, :, :, lanes] = jnp.concatenate(whole, 1).astype(BF16)

    hidden = [first(c) for c in range(chunks)]
    for c in range(chunks):
        second(c, hidden[c])
    last = []
    for side in range(2):
        for end in range(2):
            source = corner_out.at[side, pl.ds(end * REACH, REACH)]
            target = out_ref.at[ends_at[end], sides_at[side]]
            last.append(pltpu.make_async_copy(source, target, sems.at[len(copies) + len(last)]))
            last[-1].start()
    for copy in copies + last:
        copy.wait()


def per_device(state_field, filters, band_edges, basis_mask, weights_one, weights_two):
    rows, cells, channels = state_field.shape
    bases = filters.shape[1]
    group = bases * CELLS
    chunks = channels // LANES
    block = max(b for b in range(2, rows + 1, 2) if rows % b == 0 and (b + REACH) * WINDOW <= DEPTH)
    lat_peers, lon_peers = lax.axis_size("lat"), lax.axis_size("lon")
    lon = lax.axis_index("lon")

    anywhere = pl.BlockSpec(memory_space=pl.ANY)
    vmem = pl.BlockSpec(memory_space=pltpu.VMEM)
    params = pltpu.CompilerParams(vmem_limit_bytes=VMEM_BYTES)
    dma = pltpu.SemaphoreType.DMA

    def array(*shape, dtype=BF16):
        return jax.ShapeDtypeStruct(shape, dtype)

    def scratch(*shape, dtype=BF16):
        return pltpu.VMEM(shape, dtype)

    across = cells // CELLS
    edge = REACH * across
    filter_args = (filters.transpose(1, 3, 2, 0), band_edges.T, basis_mask.T)
    lat_a, lat_b, lon_a, lon_b = pl.pallas_call(
        prep_kernel,
        out_shape=(array(edge + 1, CELLS, channels),) * 2 + (array(rows, CELLS, channels),) * 2,
        in_specs=[anywhere] * 5,
        out_specs=(anywhere,) * 4,
        scratch_shapes=[
            scratch(bases, filters.shape[3], BANDS, rows, dtype=F32),
            scratch(2, rows, dtype=jnp.int32), scratch(bases, rows, dtype=jnp.int32),
            scratch(2, edge, CELLS, channels), scratch(2, rows, CELLS, channels),
            scratch(bases, LANES, LANES, dtype=F32), scratch(2, CELLS, channels, dtype=F32),
            scratch(2, CELLS, channels), dma((7,)), dma((6,)),
        ],
        compiler_params=pltpu.CompilerParams(vmem_limit_bytes=60 * 1024 * 1024),
        cost_estimate=pl.CostEstimate(flops=0, bytes_accessed=8 * REACH * cells * channels, transcendentals=0),
        name="prep",
    )(
        state_field.reshape(rows * across, CELLS, channels), state_field.reshape(rows, across, CELLS, channels),
        *filter_args,
    )
    both = ("lat", "lon")
    lat_a = lax.ppermute(lat_a, both, lat_swaps(lat_peers, lon_peers, False))
    lat_b = lax.ppermute(lat_b, both, lat_swaps(lat_peers, lon_peers, True))
    lon_b = lax.ppermute(lon_b, "lon", swaps(lon_peers, True))
    lon_a = lax.ppermute(lon_a, "lon", swaps(lon_peers, False))

    middle = rows - 2 * REACH
    flops = 2 * (2 * rows - 3 * REACH) * (cells - 2 * CELLS) * bases * DEPTH * channels
    cost = pl.CostEstimate(flops=flops, bytes_accessed=4 * state_field.size, transcendentals=0)
    toeplitz, known, wide, edge_rows, edge_cells, sides, begun = pl.pallas_call(
        functools.partial(inner_kernel, block),
        out_shape=(
            array(rows * group, DEPTH), array(2 * REACH * group, DEPTH), array(2 * REACH * group, DEPTH),
            array(2 * REACH, cells, channels), array(middle - REACH, TILE, channels),
            array(middle, TILE, channels), array(rows, cells, channels),
        ),
        in_specs=[vmem] * 6,
        out_specs=(vmem,) * 6 + (anywhere,),
        scratch_shapes=[
            scratch(middle, cells - 2 * TILE, channels), scratch(bases, LANES, LANES, dtype=F32),
            scratch(chunks, rows + REACH, cells, LANES, dtype=F32),
            scratch(chunks, rows + REACH, cells - CELLS, LANES, dtype=F32),
            scratch(chunks, middle, TILE, LANES, dtype=F32), dma((1,)),
        ],
        compiler_params=params,
        cost_estimate=cost,
        name="inner",
    )(state_field, *filter_args, weights_one, weights_two)

    def corner_send(leading, second):
        start = jnp.where(leading, 0, cells - CELLS)
        joined = [v[:edge].reshape(REACH, cells, channels) for v in (lat_a, lat_b)]
        parts = [lax.dynamic_slice_in_dim(v, start, CELLS, 1) for v in joined]
        sent = jnp.concatenate(parts, 0).reshape(2 * REACH * CELLS, channels)
        return lax.ppermute(sent, "lon", swaps(lon_peers, second))

    lat_a, lat_b, sides = lax.optimization_barrier((lat_a, lat_b, sides))
    corner_b = corner_send(lon % 2 == 0, True)
    corner_a = corner_send(lon % 2 == 1, False)
    rim_toeplitz, rim_out, side_out, ends = pl.pallas_call(
        functools.partial(rim_kernel, block),
        out_shape=(
            array(2 * REACH * group, DEPTH), array(2 * REACH, cells, channels), array(2, middle, TILE, channels),
            array(2, 4 * REACH, WINDOW, channels),
        ),
        in_specs=[vmem] * 13,
        out_specs=(vmem,) * 4,
        scratch_shapes=[
            scratch(chunks, rows + 2 * REACH, cells + 2 * CELLS, LANES, dtype=F32),
            scratch(chunks, rows + REACH, cells + CELLS, LANES, dtype=F32),
        ],
        compiler_params=params,
        cost_estimate=cost,
        name="rim",
    )(
        state_field, lat_a, lat_b, lon_b, lon_a, edge_rows, edge_cells, sides,
        toeplitz, known, wide, weights_one, weights_two,
    )
    return pl.pallas_call(
        corner_kernel,
        out_shape=array(rows, cells, channels),
        in_specs=[vmem] * 14 + [anywhere],
        out_specs=anywhere,
        input_output_aliases={14: 0},
        scratch_shapes=[scratch(2, 2 * REACH, TILE, channels), dma((8,))],
        compiler_params=params,
        cost_estimate=cost,
        name="corner",
    )(
        state_field, lat_a, lat_b, lon_b, lon_a, corner_b, corner_a, ends, rim_toeplitz, wide,
        weights_one, weights_two, side_out, rim_out, begun,
    )


def solution(mesh):
    placed = (
        P("lat", "lon", None),
        P("lat", None, None, None),
        P("lat", None),
        P("lat", None),
        P(),
        P(),
    )
    return jax.shard_map(
        per_device, mesh=mesh, in_specs=placed, out_specs=P("lat", "lon", None), check_vma=False
    )
```

```python
import functools

import jax
import jax.numpy as jnp
from jax import lax
from jax.experimental import pallas as pl
from jax.experimental.pallas import tpu as pltpu
from jax.sharding import PartitionSpec as P

LAT_REACH = 2
LON_REACH = 4
REACH = 2 * LAT_REACH
BANDS = 2 * LAT_REACH + 1
CELLS = 8
WINDOW = CELLS + 2 * LON_REACH
LANES = 128
DEPTH = 2 * LANES
TILE = 16
VMEM_BYTES = 20 * 1024 * 1024
TURNS = 3
PIECE = 4
F32, BF16 = jnp.float32, jnp.bfloat16

ERF_SERIES = (
    1.5956562720156744,
    0.2917503271976864,
    -0.003995570947534282,
    -0.003914369984884403,
    0.0005729703632347449,
)


def erf_gelu(half):
    square = half * half
    series = ERF_SERIES[-1] * square + ERF_SERIES[-2]
    for term in ERF_SERIES[-3::-1]:
        series = series * square + term
    return half + half * jnp.tanh(half * series)


def swaps(peers, second):
    pairs = [(i, i + 1) for i in range(1 if second else 0, peers - 1, 2)]
    if second:
        pairs.append((peers - 1, 0))
    return pairs + [(j, i) for i, j in pairs]


def turn_swaps(peers, width, turn):
    pairs = [(i, i + 1) for i in range(peers - 1) if i % TURNS == turn]
    pairs += [(j, i) for i, j in pairs]
    alone = set(range(peers)) - {i for i, _ in pairs}
    result = [(i * width + k, j * width + k) for i, j in pairs for k in range(width)]
    return result + [(i * width + k, i * width + (k ^ 1)) for i in sorted(alone) for k in range(width)]


def pairs_of(items):
    return [items[i : i + 2] for i in range(0, len(items), 2)]


def lanes_of(chunk):
    return slice(chunk * LANES, (chunk + 1) * LANES)


def fill_toeplitz(toeplitz, line_of, rows, bases, place_of, pairs=None):
    group = bases * CELLS
    blank = jnp.zeros((CELLS, DEPTH - LANES), F32)
    for row in pairs or range(0, rows, 2):
        parts = []
        for r in (row, row + 1):
            for basis in range(bases):
                line = jnp.broadcast_to(line_of(r, basis), (CELLS, LANES))
                line = jnp.concatenate([line, blank], 1)
                parts.append(pltpu.roll(line, place_of(r) * WINDOW, 1, stride=1, stride_axis=0))
        toeplitz[row * group : (row + 2) * group, :] = jnp.concatenate(parts, 0).astype(BF16)


def lane_weights(ref, scale=1.0):
    bases, channels = ref.shape
    return [[ref[k : k + 1, lanes_of(c)] * scale for k in range(bases)] for c in range(channels // LANES)]


def product(matrix, low, high, windows, weights):
    wide = [w.astype(BF16).reshape(DEPTH, LANES) for w in windows]
    wide = jnp.concatenate(wide, 1)
    bases = len(weights[0])
    group = bases * CELLS
    scales = [jnp.concatenate([w[k] for w in weights], 1) for k in range(bases)]
    pieces = []
    for at in range(low, high, PIECE):
        to = min(at + PIECE, high)
        result = jnp.dot(matrix[at * group : to * group, :], wide, preferred_element_type=F32)
        result = result.reshape(to - at, bases, CELLS, len(windows) * LANES)
        total = result[:, 0] * scales[0]
        for k in range(1, bases):
            total = total + result[:, k] * scales[k]
        pieces.append(total)
    total = jnp.concatenate(pieces, 0) if len(pieces) > 1 else pieces[0]
    return [total[:, :, i * LANES : (i + 1) * LANES] for i in range(len(windows))]


def run_mixed(steps):
    waiting = []
    for first, second in steps:
        share = -(-len(waiting) // max(len(first), 1))
        for unit in first:
            unit()
            for _ in range(min(share, len(waiting))):
                waiting.pop(0)()
        for unit in waiting:
            unit()
        waiting = list(second)
    for unit in waiting:
        unit()


def line_choice(lags):
    at = lax.broadcasted_iota(jnp.int32, (LANES, LANES), 0)
    lane = lax.broadcasted_iota(jnp.int32, (LANES, LANES), 1)
    chosen = (at // 8 == lane % WINDOW) & (at % 8 == lane // WINDOW) & (at % 8 < BANDS) & (at // 8 < lags)
    return jnp.where(chosen, 1.0, 0.0).astype(BF16)


def filter_lines(filter_ref, edge_ref, mask_ref, padded, chosen):
    bases, lags, bands, rows = filter_ref.shape
    source = lax.axis_index("lat") * rows + lax.broadcasted_iota(jnp.int32, (bands, rows), 1) - LAT_REACH
    source = source + lax.broadcasted_iota(jnp.int32, (bands, rows), 0)
    inside = (source >= edge_ref[0:1, :]) & (source < edge_ref[1:2, :])
    for k in range(bases):
        keep = inside & (mask_ref[k : k + 1, :] != 0)
        for m in range(lags):
            padded[k, m * 8 : m * 8 + bands, :rows] = jnp.where(keep, filter_ref[k, m], 0.0)
    return [jnp.dot(padded[k].T.astype(BF16), chosen, preferred_element_type=F32) for k in range(bases)]


def prep_kernel(
    flat_ref, groups_ref, filter_in, edge_in, mask_in, turn_0, turn_1, turn_2, lon_b,
    filter_ref, edge_ref, mask_ref, payloads, far, padded, tags, sems, out_sems,
):
    bases, lags, bands, rows = filter_in.shape
    across = groups_ref.shape[1]
    edge = REACH * across
    turn, lon_odd = lax.axis_index("lat") % TURNS, lax.axis_index("lon") % 2
    small = [
        pltpu.make_async_copy(filter_in, filter_ref, sems.at[0]),
        pltpu.make_async_copy(edge_in, edge_ref, sems.at[1]),
        pltpu.make_async_copy(mask_in, mask_ref, sems.at[2]),
    ]
    last, first = pl.ds((rows - REACH) * across, edge), pl.ds(0, edge)
    near_at, far_at = (1 - lon_odd) * (across - 1), lon_odd * (across - 1)
    copies = [
        pltpu.make_async_copy(flat_ref.at[last], payloads.at[0, pl.ds(0, edge)], sems.at[3]),
        pltpu.make_async_copy(flat_ref.at[first], payloads.at[1, pl.ds(0, edge)], sems.at[4]),
        pltpu.make_async_copy(groups_ref.at[:, near_at], payloads.at[2, pl.ds(0, rows)], sems.at[5]),
        pltpu.make_async_copy(groups_ref.at[:, far_at], far, sems.at[6]),
    ]
    for copy in copies[:2] + small + copies[2:]:
        copy.start()
    padded[...] = jnp.zeros_like(padded)
    tags[...] = jnp.zeros_like(tags)
    payloads[2, rows:] = jnp.zeros((edge + 1 - rows,) + payloads.shape[2:], BF16)
    chosen = line_choice(lags)
    pending = []

    def send(source, target):
        pending.append(pltpu.make_async_copy(source, target, out_sems.at[len(pending)]))
        pending[-1].start()

    outs = [(out, (turn + TURNS - j) % TURNS) for j, out in enumerate((turn_0, turn_1, turn_2))]
    for copy in copies[:3]:
        copy.wait()
    for out, role in outs:
        send(payloads.at[role, pl.ds(0, edge)], out.at[pl.ds(0, edge)])
    copies[3].wait()
    send(far, lon_b)
    for copy in small:
        copy.wait()
    for k, line in enumerate(filter_lines(filter_ref, edge_ref, mask_ref, padded, chosen)):
        tags[0, :LAT_REACH, lanes_of(k)] = line[rows - LAT_REACH : rows]
        tags[1, :LAT_REACH, lanes_of(k)] = line[:LAT_REACH]
    payloads[0, edge] = tags[0].astype(BF16)
    payloads[1, edge] = tags[1].astype(BF16)
    for out, role in outs:
        send(payloads.at[role, edge], out.at[edge])
    for copy in pending:
        copy.wait()


def place_of(r):
    return r if r < REACH else REACH + r


def inner_kernel(
    block, x_ref, filter_ref, edge_ref, mask_ref, one_ref, two_ref,
    toeplitz, rim_toeplitz, wide_toeplitz, edge_rows, edge_cells, sides, out_ref,
    middle, padded, field, hidden, ends, sems,
):
    rows, cells, channels = x_ref.shape
    bases = one_ref.shape[0]
    chunks = channels // LANES
    padded[...] = jnp.zeros_like(padded)
    chosen = line_choice(filter_ref.shape[1])
    lines = filter_lines(filter_ref, edge_ref, mask_ref, padded, chosen)
    fill_toeplitz(toeplitz, lambda r, k: lines[k][r : r + 1, :], rows, bases, lambda r: r % block)
    kept = list(range(REACH)) + list(range(rows - REACH, rows))
    fill_toeplitz(wide_toeplitz, lambda r, k: lines[k][kept[r] : kept[r] + 1, :], 2 * REACH, bases, place_of)
    shifted = [r - LAT_REACH for r in range(REACH)] + [rows - LAT_REACH + r for r in range(REACH)]
    own = range(LAT_REACH, 2 * REACH - LAT_REACH, 2)
    rim_toeplitz[...] = jnp.zeros_like(rim_toeplitz)
    fill_toeplitz(
        rim_toeplitz, lambda r, k: lines[k][shifted[r] : shifted[r] + 1, :], 2 * REACH, bases, place_of, own
    )
    one, two = lane_weights(one_ref, 0.5), lane_weights(two_ref)
    starts = range(0, rows, block)
    windows = (cells - WINDOW) // CELLS + 1
    span = windows * CELLS

    def load(c):
        blank = jnp.zeros((LAT_REACH, cells, LANES), F32)
        field[c, :LAT_REACH] = blank
        field[c, LAT_REACH : LAT_REACH + rows] = x_ref[:, :, lanes_of(c)].astype(F32)
        field[c, LAT_REACH + rows :] = blank
        blank = jnp.zeros((REACH, span, LANES), F32)
        hidden[c, :REACH] = blank
        hidden[c, rows:] = blank

    def first(items, start):
        low, high = max(start, LAT_REACH), min(start + block, rows - LAT_REACH)
        tall = [field[c, start : start + block + REACH, w * CELLS : w * CELLS + WINDOW] for c, w in items]
        values = product(toeplitz, low, high, tall, [one[c] for c, w in items])
        for (c, w), value in zip(items, values):
            hidden[c, low + LAT_REACH : high + LAT_REACH, w * CELLS : (w + 1) * CELLS] = erf_gelu(value)

    def second(c, start, pair):
        low, high = max(start, REACH), min(start + block, rows - REACH)
        tall = [hidden[c, start : start + block + REACH, w * CELLS : w * CELLS + WINDOW] for w in pair]
        values = product(toeplitz, low, high, tall, [two[c]] * len(pair))
        at = slice(low - REACH, high - REACH)
        for w, value in zip(pair, values):
            if w in (0, windows - 2):
                ends[c, at, (w > 0) * CELLS : (w > 0) * CELLS + CELLS] = value
        if len(pair) == 2 and pair[0] > 0:
            span = slice((pair[0] - 1) * CELLS, (pair[0] + 1) * CELLS)
            middle[at, span, lanes_of(c)] = jnp.concatenate(values, 1).astype(BF16)

    def export(c):
        for i, row in enumerate((REACH, rows - REACH)):
            part = jnp.concatenate([hidden[c, row : row + REACH], jnp.zeros((REACH, cells - span, LANES), F32)], 1)
            edge_rows[i * REACH : (i + 1) * REACH, :, lanes_of(c)] = part.astype(BF16)
        part = hidden[c, 2 * REACH : rows - REACH]
        edge_cells[:, :, lanes_of(c)] = jnp.concatenate([part[:, :CELLS], part[:, span - CELLS :]], 1).astype(BF16)
        sides[:, :, lanes_of(c)] = ends[c].astype(BF16)

    part = functools.partial
    steps = [([part(load, c)], []) for c in range(chunks)]
    for items in pairs_of([(c, w) for c in range(chunks) for w in range(windows)]):
        steps[items[-1][0]][0].extend(part(first, items, start) for start in starts)
    for c in range(chunks):
        pairs = [[0, windows - 2]] + pairs_of(list(range(1, windows - 2)))
        steps[c][1].extend(part(second, c, start, pair) for start in starts for pair in pairs)
        steps[c][1].append(part(export, c))
    for c in range(chunks - 1, 0, -1):
        if c * windows % 2:
            straddle = steps[c][0][1 : 1 + len(starts)]
            steps[c][0][1 : 1 + len(starts)] = []
            steps[c - 1][0].extend([steps[c][0].pop(0)] + straddle)
    run_mixed(steps)
    target = out_ref.at[pl.ds(REACH, rows - 2 * REACH), pl.ds(TILE, cells - 2 * TILE)]
    copy = pltpu.make_async_copy(middle, target, sems.at[0])
    copy.start()
    copy.wait()


def ordered(odd, a, b):
    a, b = a.astype(F32), b.astype(F32)
    return jnp.where(odd, a, b), jnp.where(odd, b, a)


def pick(received, turn):
    value = received[-1].astype(F32)
    for j in range(TURNS - 1):
        value = jnp.where(turn == j, received[j].astype(F32), value)
    return value


def below_and_above(received):
    turn = lax.axis_index("lat") % TURNS
    return pick(received, (turn + TURNS - 1) % TURNS), pick(received, turn)


def in_chip(received):
    return pick(received, (lax.axis_index("lat") + 1) % TURNS)


def rim_kernel(
    block, x_ref, turn_0, turn_1, turn_2, lon_b, rows_in, cells_in, sides_in,
    toeplitz, known_toeplitz, wide_toeplitz, one_ref, two_ref,
    rim_toeplitz, rim_out, side_out, ends, field, hidden,
):
    rows, cells, channels = x_ref.shape
    bases = one_ref.shape[0]
    chunks = channels // LANES
    group = bases * CELLS
    edge = REACH * (cells // CELLS)
    columns = cells // CELLS + 1
    turns, lon_odd = (turn_0, turn_1, turn_2), lax.axis_index("lon") % 2 == 1
    one, two = lane_weights(one_ref, 0.5), lane_weights(two_ref)
    tags = below_and_above([v[edge] for v in turns])

    def tag_line(r, k):
        at = r % LAT_REACH
        return tags[0 if r < REACH else 1][at : at + 1, lanes_of(k)]

    own = slice(LAT_REACH * group, (2 * REACH - LAT_REACH) * group)
    rim_toeplitz[own, :] = known_toeplitz[own, :]
    fill_toeplitz(rim_toeplitz, tag_line, 2 * REACH, bases, place_of, (0, 2 * REACH - LAT_REACH))

    def load(c):
        lanes = lanes_of(c)
        lat = below_and_above([v[:edge, :, lanes] for v in turns])
        lon = ordered(lon_odd, in_chip([v[:rows, :, lanes] for v in turns]), lon_b[:, :, lanes])
        inner = slice(REACH, rows - REACH)
        blank = jnp.zeros((REACH, CELLS, LANES), F32)
        for side in range(2):
            at = slice(side * (rows + REACH), side * (rows + REACH) + REACH)
            field[c, at, CELLS : CELLS + cells] = lat[side].reshape(REACH, cells, LANES)
            own = slice(side * (rows - REACH), side * (rows - REACH) + REACH)
            at = slice(own.start + REACH, own.stop + REACH)
            field[c, at, CELLS : CELLS + cells] = x_ref[own, :, lanes].astype(F32)
            own = slice(side * (cells - TILE), side * (cells - TILE) + TILE)
            at = slice(own.start + CELLS, own.stop + CELLS)
            field[c, 2 * REACH : rows, at] = x_ref[inner, own, lanes].astype(F32)
            span = slice(side * (CELLS + cells), side * (CELLS + cells) + CELLS)
            field[c, REACH : REACH + rows, span] = lon[side]
            for end in range(2):
                at = slice(end * (rows + REACH), end * (rows + REACH) + REACH)
                field[c, at, span] = blank
                hidden[c, end * rows : end * rows + REACH, side * cells : side * cells + CELLS] = blank
        span = cells - CELLS
        for i, at in enumerate((REACH, rows - REACH)):
            part = rows_in[i * REACH : (i + 1) * REACH, :, lanes].astype(F32)
            hidden[c, at : at + REACH, CELLS : CELLS + span] = part[:, :span]
        part = cells_in[:, :, lanes].astype(F32)
        at = slice(2 * REACH, rows - REACH)
        hidden[c, at, CELLS : 2 * CELLS] = part[:, :CELLS]
        hidden[c, at, cells - CELLS : cells] = part[:, CELLS:]

    def rims(ref, c, span):
        last = ref.shape[1] - 2 * REACH
        return jnp.concatenate([ref[c, : 2 * REACH, span], ref[c, last:, span]], 0)

    def first_rows(items):
        tall = [rims(field, c, slice(w * CELLS, w * CELLS + WINDOW)) for c, w in items]
        values = product(rim_toeplitz, 0, 2 * REACH, tall, [one[c] for c, w in items])
        for (c, w), value in zip(items, values):
            value = erf_gelu(value)
            hidden[c, :REACH, w * CELLS : (w + 1) * CELLS] = value[:REACH]
            hidden[c, rows:, w * CELLS : (w + 1) * CELLS] = value[REACH:]

    def first_sides(c, start):
        low, high = max(start, LAT_REACH), min(start + block, rows - LAT_REACH)
        at = slice(start + LAT_REACH, start + LAT_REACH + block + REACH)
        tall = [field[c, at, s : s + WINDOW] for s in (0, cells)]
        values = product(toeplitz, low, high, tall, [one[c]] * 2)
        for s, value in zip((0, cells), values):
            hidden[c, low + LAT_REACH : high + LAT_REACH, s : s + CELLS] = erf_gelu(value)

    def second_rows(c, pair):
        tall = [rims(hidden, c, slice(w * CELLS, w * CELLS + WINDOW)) for w in pair]
        values = product(wide_toeplitz, 0, 2 * REACH, tall, [two[c]] * 2)
        blank = jnp.zeros((2 * REACH, CELLS, LANES), F32)
        if pair == [1, columns - 3]:
            rim_out[:, :TILE, lanes_of(c)] = jnp.concatenate([blank, values[0]], 1).astype(BF16)
            rim_out[:, cells - TILE :, lanes_of(c)] = jnp.concatenate([values[1], blank], 1).astype(BF16)
        else:
            rim_out[:, pair[0] * CELLS : (pair[0] + 2) * CELLS, lanes_of(c)] = jnp.concatenate(values, 1).astype(BF16)

    def second_sides(c, start):
        low, high = max(start, REACH), min(start + block, rows - REACH)
        tall = [hidden[c, start : start + block + REACH, s : s + WINDOW] for s in (0, cells - CELLS)]
        values = product(toeplitz, low, high, tall, [two[c]] * 2)
        at = slice(low - REACH, high - REACH)
        inner = sides_in[at, :, lanes_of(c)].astype(F32)
        side_out[0, at, :, lanes_of(c)] = jnp.concatenate([values[0], inner[:, :CELLS]], 1).astype(BF16)
        side_out[1, at, :, lanes_of(c)] = jnp.concatenate([inner[:, CELLS:], values[1]], 1).astype(BF16)

    def export(c):
        for side in range(2):
            span = slice(side * (cells - CELLS), side * (cells - CELLS) + WINDOW)
            ends[side, :, :, lanes_of(c)] = rims(hidden, c, span).astype(BF16)

    part = functools.partial
    steps = [([part(load, c)], []) for c in range(chunks)]
    items = [(c, w) for c in range(chunks) for w in range(1, columns - 1)]
    for pair in pairs_of(items):
        steps[pair[-1][0]][0].append(part(first_rows, pair))
    for c in range(chunks - 1, 0, -1):
        if c * (columns - 2) % 2:
            steps[c - 1][0].extend([steps[c][0].pop(0), steps[c][0].pop(0)])
    starts = range(0, rows, block)
    for c, (first, second) in enumerate(steps):
        first.extend(part(first_sides, c, start) for start in starts)
        second.extend(
            part(second_rows, c, pair) for pair in [[1, columns - 3]] + pairs_of(list(range(2, columns - 3)))
        )
        second.extend(part(second_sides, c, start) for start in starts)
        second.append(part(export, c))
    run_mixed(steps)


def corner_kernel(
    x_ref, turn_0, turn_1, turn_2, lon_b, corner_b, corner_a, ends, rim_toeplitz, wide_toeplitz, one_ref, two_ref,
    side_out, rim_out, begun_ref, out_ref, corner_out, sems,
):
    del begun_ref
    rows, cells, channels = x_ref.shape
    chunks = channels // LANES
    edge = REACH * (cells // CELLS)
    inner = pl.ds(REACH, rows - 2 * REACH)
    ends_at = (pl.ds(0, REACH), pl.ds(rows - REACH, REACH))
    sides_at = (pl.ds(0, TILE), pl.ds(cells - TILE, TILE))
    span = pl.ds(TILE, cells - 2 * TILE)
    moves = []
    for i in range(2):
        moves.append((side_out.at[i], out_ref.at[inner, sides_at[i]]))
        moves.append((rim_out.at[pl.ds(i * REACH, REACH), span], out_ref.at[ends_at[i], span]))
    copies = [pltpu.make_async_copy(source, target, sems.at[i]) for i, (source, target) in enumerate(moves)]
    for copy in copies:
        copy.start()
    turns, lon_odd = (turn_0, turn_1, turn_2), lax.axis_index("lon") % 2 == 1
    one, two = lane_weights(one_ref, 0.5), lane_weights(two_ref)

    def first(c):
        lanes = lanes_of(c)
        lat = below_and_above([v[:edge, :, lanes] for v in turns])
        lon = ordered(lon_odd, in_chip([v[:rows, :, lanes] for v in turns]), lon_b[:, :, lanes])
        corner = ordered(lon_odd, corner_a[:, lanes], corner_b[:, lanes])
        tall = []
        for side in range(2):
            own = slice(side * (cells - CELLS), side * (cells - CELLS) + CELLS)
            above = [v.reshape(REACH, cells, LANES)[:, own] for v in lat]
            tiles = slice(side * (cells - TILE), side * (cells - TILE) + TILE)
            half = slice(side * (TILE - CELLS), side * (TILE - CELLS) + CELLS)
            mine = [x_ref[r : r + REACH, tiles, lanes].astype(F32)[:, half] for r in (0, rows - REACH)]
            near = lon[side]
            far = corner[side].reshape(2, REACH, CELLS, LANES)
            own = jnp.concatenate([above[0], mine[0], mine[1], above[1]], 0)
            other = jnp.concatenate([far[0], near[:REACH], near[rows - REACH :], far[1]], 0)
            tall.append(jnp.concatenate([own, other] if side else [other, own], 1))
        return [erf_gelu(v) for v in product(rim_toeplitz, 0, 2 * REACH, tall, [one[c]] * 2)]

    def second(c, blocks):
        lanes = lanes_of(c)
        tall = []
        for side in range(2):
            near = ends[side, :, :, lanes].astype(F32)
            own = near[:, side * CELLS : side * CELLS + CELLS]
            own = jnp.concatenate([blocks[side][:REACH], own[REACH : 3 * REACH], blocks[side][REACH:]], 0)
            tall.append(jnp.concatenate([near[:, :CELLS], own] if side else [own, near[:, CELLS:]], 1))
        values = product(wide_toeplitz, 0, 2 * REACH, tall, [two[c]] * 2)
        for side in range(2):
            tiles = slice(side * (cells - TILE), side * (cells - TILE) + TILE)
            near = rim_out[:, tiles, lanes].astype(F32)
            near = near[:, : TILE - CELLS] if side else near[:, CELLS:]
            whole = [near, values[side]] if side else [values[side], near]
            corner_out[side, :, :, lanes] = jnp.concatenate(whole, 1).astype(BF16)

    hidden = [first(c) for c in range(chunks)]
    for c in range(chunks):
        second(c, hidden[c])
    last = []
    for side in range(2):
        for end in range(2):
            source = corner_out.at[side, pl.ds(end * REACH, REACH)]
            target = out_ref.at[ends_at[end], sides_at[side]]
            last.append(pltpu.make_async_copy(source, target, sems.at[len(copies) + len(last)]))
            last[-1].start()
    for copy in copies + last:
        copy.wait()


def per_device(state_field, filters, band_edges, basis_mask, weights_one, weights_two):
    rows, cells, channels = state_field.shape
    bases = filters.shape[1]
    group = bases * CELLS
    chunks = channels // LANES
    block = max(b for b in range(2, rows + 1, 2) if rows % b == 0 and (b + REACH) * WINDOW <= DEPTH)
    lat_peers, lon_peers = lax.axis_size("lat"), lax.axis_size("lon")
    turn, lon = lax.axis_index("lat") % TURNS, lax.axis_index("lon")

    anywhere = pl.BlockSpec(memory_space=pl.ANY)
    vmem = pl.BlockSpec(memory_space=pltpu.VMEM)
    params = pltpu.CompilerParams(vmem_limit_bytes=VMEM_BYTES)
    dma = pltpu.SemaphoreType.DMA

    def array(*shape, dtype=BF16):
        return jax.ShapeDtypeStruct(shape, dtype)

    def scratch(*shape, dtype=BF16):
        return pltpu.VMEM(shape, dtype)

    across = cells // CELLS
    edge = REACH * across
    filter_args = (filters.transpose(1, 3, 2, 0), band_edges.T, basis_mask.T)
    *turns, lon_b = pl.pallas_call(
        prep_kernel,
        out_shape=(array(edge + 1, CELLS, channels),) * TURNS + (array(rows, CELLS, channels),),
        in_specs=[anywhere] * 5,
        out_specs=(anywhere,) * (TURNS + 1),
        scratch_shapes=[
            scratch(bases, filters.shape[3], BANDS, rows, dtype=F32),
            scratch(2, rows, dtype=jnp.int32), scratch(bases, rows, dtype=jnp.int32),
            scratch(TURNS, edge + 1, CELLS, channels), scratch(rows, CELLS, channels),
            scratch(bases, LANES, LANES, dtype=F32), scratch(2, CELLS, channels, dtype=F32),
            dma((7,)), dma((2 * TURNS + 1,)),
        ],
        compiler_params=pltpu.CompilerParams(vmem_limit_bytes=60 * 1024 * 1024),
        cost_estimate=pl.CostEstimate(flops=0, bytes_accessed=8 * REACH * cells * channels, transcendentals=0),
        name="prep",
    )(
        state_field.reshape(rows * across, CELLS, channels), state_field.reshape(rows, across, CELLS, channels),
        *filter_args,
    )
    both = ("lat", "lon")
    turns = [lax.ppermute(v, both, turn_swaps(lat_peers, lon_peers, j)) for j, v in enumerate(turns)]
    lon_b = lax.ppermute(lon_b, "lon", swaps(lon_peers, True))

    middle = rows - 2 * REACH
    flops = 2 * (2 * rows - 3 * REACH) * (cells - 2 * CELLS) * bases * DEPTH * channels
    cost = pl.CostEstimate(flops=flops, bytes_accessed=4 * state_field.size, transcendentals=0)
    toeplitz, known, wide, edge_rows, edge_cells, sides, begun = pl.pallas_call(
        functools.partial(inner_kernel, block),
        out_shape=(
            array(rows * group, DEPTH), array(2 * REACH * group, DEPTH), array(2 * REACH * group, DEPTH),
            array(2 * REACH, cells, channels), array(middle - REACH, TILE, channels),
            array(middle, TILE, channels), array(rows, cells, channels),
        ),
        in_specs=[vmem] * 6,
        out_specs=(vmem,) * 6 + (anywhere,),
        scratch_shapes=[
            scratch(middle, cells - 2 * TILE, channels), scratch(bases, LANES, LANES, dtype=F32),
            scratch(chunks, rows + REACH, cells, LANES, dtype=F32),
            scratch(chunks, rows + REACH, cells - CELLS, LANES, dtype=F32),
            scratch(chunks, middle, TILE, LANES, dtype=F32), dma((1,)),
        ],
        compiler_params=params,
        cost_estimate=cost,
        name="inner",
    )(state_field, *filter_args, weights_one, weights_two)

    *turns, sides = lax.optimization_barrier((*turns, sides))

    def corner_send(leading, second):
        start = jnp.where(leading, 0, cells - CELLS)
        parts = [v[:edge].reshape(REACH, cells, channels) for v in turns]
        parts = [lax.dynamic_slice_in_dim(v, start, CELLS, 1) for v in parts]
        below = jnp.where(turn == 1, parts[0], jnp.where(turn == 2, parts[1], parts[2]))
        above = jnp.where(turn == 0, parts[0], jnp.where(turn == 1, parts[1], parts[2]))
        sent = jnp.concatenate([below, above], 0).reshape(2 * REACH * CELLS, channels)
        return lax.ppermute(sent, "lon", swaps(lon_peers, second))

    corner_b = corner_send(lon % 2 == 0, True)
    corner_a = corner_send(lon % 2 == 1, False)
    rim_toeplitz, rim_out, side_out, ends = pl.pallas_call(
        functools.partial(rim_kernel, block),
        out_shape=(
            array(2 * REACH * group, DEPTH), array(2 * REACH, cells, channels), array(2, middle, TILE, channels),
            array(2, 4 * REACH, WINDOW, channels),
        ),
        in_specs=[vmem] * 13,
        out_specs=(vmem,) * 4,
        scratch_shapes=[
            scratch(chunks, rows + 2 * REACH, cells + 2 * CELLS, LANES, dtype=F32),
            scratch(chunks, rows + REACH, cells + CELLS, LANES, dtype=F32),
        ],
        compiler_params=params,
        cost_estimate=cost,
        name="rim",
    )(
        state_field, *turns, lon_b, edge_rows, edge_cells, sides,
        toeplitz, known, wide, weights_one, weights_two,
    )
    return pl.pallas_call(
        corner_kernel,
        out_shape=array(rows, cells, channels),
        in_specs=[vmem] * 14 + [anywhere],
        out_specs=anywhere,
        input_output_aliases={14: 0},
        scratch_shapes=[scratch(2, 2 * REACH, TILE, channels), dma((8,))],
        compiler_params=params,
        cost_estimate=cost,
        name="corner",
    )(
        state_field, *turns, lon_b, corner_b, corner_a, ends, rim_toeplitz, wide,
        weights_one, weights_two, side_out, rim_out, begun,
    )


def solution(mesh):
    placed = (
        P("lat", "lon", None),
        P("lat", None, None, None),
        P("lat", None),
        P("lat", None),
        P(),
        P(),
    )
    return jax.shard_map(
        per_device, mesh=mesh, in_specs=placed, out_specs=P("lat", "lon", None), check_vma=False
    )
```

```python
import functools

import jax
import jax.numpy as jnp
from jax import lax
from jax.experimental import pallas as pl
from jax.experimental.pallas import tpu as pltpu
from jax.sharding import PartitionSpec as P

LAT_REACH = 2
LON_REACH = 4
REACH = 2 * LAT_REACH
BANDS = 2 * LAT_REACH + 1
CELLS = 8
WINDOW = CELLS + 2 * LON_REACH
LANES = 128
DEPTH = 2 * LANES
TILE = 16
VMEM_BYTES = 20 * 1024 * 1024
TURNS = 3
PIECE = 4
F32, BF16 = jnp.float32, jnp.bfloat16

ERF_SERIES = (
    1.5956562720156744,
    0.2917503271976864,
    -0.003995570947534282,
    -0.003914369984884403,
    0.0005729703632347449,
)


def erf_gelu(half):
    square = half * half
    series = ERF_SERIES[-1] * square + ERF_SERIES[-2]
    for term in ERF_SERIES[-3::-1]:
        series = series * square + term
    return half + half * jnp.tanh(half * series)


def swaps(peers, second):
    pairs = [(i, i + 1) for i in range(1 if second else 0, peers - 1, 2)]
    if second:
        pairs.append((peers - 1, 0))
    return pairs + [(j, i) for i, j in pairs]


def turn_swaps(peers, width, turn):
    pairs = [(i, i + 1) for i in range(peers - 1) if i % TURNS == turn]
    pairs += [(j, i) for i, j in pairs]
    alone = set(range(peers)) - {i for i, _ in pairs}
    result = [(i * width + k, j * width + k) for i, j in pairs for k in range(width)]
    return result + [(i * width + k, i * width + (k ^ 1)) for i in sorted(alone) for k in range(width)]


def pairs_of(items):
    return [items[i : i + 2] for i in range(0, len(items), 2)]


def lanes_of(chunk):
    return slice(chunk * LANES, (chunk + 1) * LANES)


def fill_toeplitz(toeplitz, line_of, rows, bases, place_of, pairs=None):
    group = bases * CELLS
    blank = jnp.zeros((CELLS, DEPTH - LANES), F32)
    for row in pairs or range(0, rows, 2):
        parts = []
        for r in (row, row + 1):
            for basis in range(bases):
                line = jnp.broadcast_to(line_of(r, basis), (CELLS, LANES))
                line = jnp.concatenate([line, blank], 1)
                parts.append(pltpu.roll(line, place_of(r) * WINDOW, 1, stride=1, stride_axis=0))
        toeplitz[row * group : (row + 2) * group, :] = jnp.concatenate(parts, 0).astype(BF16)


def lane_weights(ref, scale=1.0):
    bases, channels = ref.shape
    return [[ref[k : k + 1, lanes_of(c)] * scale for k in range(bases)] for c in range(channels // LANES)]


def product(matrix, low, high, windows, weights):
    wide = [w.astype(BF16).reshape(DEPTH, LANES) for w in windows]
    wide = jnp.concatenate(wide, 1)
    bases = len(weights[0])
    group = bases * CELLS
    scales = [jnp.concatenate([w[k] for w in weights], 1) for k in range(bases)]
    pieces = []
    for at in range(low, high, PIECE):
        to = min(at + PIECE, high)
        result = jnp.dot(matrix[at * group : to * group, :], wide, preferred_element_type=F32)
        result = result.reshape(to - at, bases, CELLS, len(windows) * LANES)
        total = result[:, 0] * scales[0]
        for k in range(1, bases):
            total = total + result[:, k] * scales[k]
        pieces.append(total)
    total = jnp.concatenate(pieces, 0) if len(pieces) > 1 else pieces[0]
    return [total[:, :, i * LANES : (i + 1) * LANES] for i in range(len(windows))]


def run_mixed(steps):
    waiting = []
    for first, second in steps:
        total, done = len(waiting), 0
        for i, unit in enumerate(first):
            unit()
            while done * len(first) < total * (i + 1):
                waiting.pop(0)()
                done += 1
        for unit in waiting:
            unit()
        waiting = list(second)
    for unit in waiting:
        unit()


def line_choice(lags):
    at = lax.broadcasted_iota(jnp.int32, (LANES, LANES), 0)
    lane = lax.broadcasted_iota(jnp.int32, (LANES, LANES), 1)
    chosen = (at // 8 == lane % WINDOW) & (at % 8 == lane // WINDOW) & (at % 8 < BANDS) & (at // 8 < lags)
    return jnp.where(chosen, 1.0, 0.0).astype(BF16)


def filter_lines(filter_ref, edge_ref, mask_ref, padded, chosen):
    bases, lags, bands, rows = filter_ref.shape
    source = lax.axis_index("lat") * rows + lax.broadcasted_iota(jnp.int32, (bands, rows), 1) - LAT_REACH
    source = source + lax.broadcasted_iota(jnp.int32, (bands, rows), 0)
    inside = (source >= edge_ref[0:1, :]) & (source < edge_ref[1:2, :])
    for k in range(bases):
        keep = inside & (mask_ref[k : k + 1, :] != 0)
        for m in range(lags):
            padded[k, m * 8 : m * 8 + bands, :rows] = jnp.where(keep, filter_ref[k, m], 0.0)
    return [jnp.dot(padded[k].T.astype(BF16), chosen, preferred_element_type=F32) for k in range(bases)]


def prep_kernel(
    flat_ref, groups_ref, filter_in, edge_in, mask_in, turn_0, turn_1, turn_2, lon_b,
    filter_ref, edge_ref, mask_ref, payloads, far, padded, tags, sems, out_sems,
):
    bases, lags, bands, rows = filter_in.shape
    across = groups_ref.shape[1]
    edge = REACH * across
    turn, lon_odd = lax.axis_index("lat") % TURNS, lax.axis_index("lon") % 2
    small = [
        pltpu.make_async_copy(filter_in, filter_ref, sems.at[0]),
        pltpu.make_async_copy(edge_in, edge_ref, sems.at[1]),
        pltpu.make_async_copy(mask_in, mask_ref, sems.at[2]),
    ]
    last, first = pl.ds((rows - REACH) * across, edge), pl.ds(0, edge)
    near_at, far_at = (1 - lon_odd) * (across - 1), lon_odd * (across - 1)
    copies = [
        pltpu.make_async_copy(flat_ref.at[last], payloads.at[0, pl.ds(0, edge)], sems.at[3]),
        pltpu.make_async_copy(flat_ref.at[first], payloads.at[1, pl.ds(0, edge)], sems.at[4]),
        pltpu.make_async_copy(groups_ref.at[:, near_at], payloads.at[2, pl.ds(0, rows)], sems.at[5]),
        pltpu.make_async_copy(groups_ref.at[:, far_at], far, sems.at[6]),
    ]
    for copy in copies[:2] + small + copies[2:]:
        copy.start()
    padded[...] = jnp.zeros_like(padded)
    tags[...] = jnp.zeros_like(tags)
    payloads[2, rows:] = jnp.zeros((edge + 1 - rows,) + payloads.shape[2:], BF16)
    chosen = line_choice(lags)
    pending = []

    def send(source, target):
        pending.append(pltpu.make_async_copy(source, target, out_sems.at[len(pending)]))
        pending[-1].start()

    outs = [(out, (turn + TURNS - j) % TURNS) for j, out in enumerate((turn_0, turn_1, turn_2))]
    for copy in copies[:3]:
        copy.wait()
    for out, role in outs:
        send(payloads.at[role, pl.ds(0, edge)], out.at[pl.ds(0, edge)])
    copies[3].wait()
    send(far, lon_b)
    for copy in small:
        copy.wait()
    for k, line in enumerate(filter_lines(filter_ref, edge_ref, mask_ref, padded, chosen)):
        tags[0, :LAT_REACH, lanes_of(k)] = line[rows - LAT_REACH : rows]
        tags[1, :LAT_REACH, lanes_of(k)] = line[:LAT_REACH]
    payloads[0, edge] = tags[0].astype(BF16)
    payloads[1, edge] = tags[1].astype(BF16)
    for out, role in outs:
        send(payloads.at[role, edge], out.at[edge])
    for copy in pending:
        copy.wait()


def place_of(r):
    return r if r < REACH else REACH + r


def inner_kernel(
    block, x_ref, filter_ref, edge_ref, mask_ref, one_ref, two_ref,
    toeplitz, rim_toeplitz, wide_toeplitz, edge_rows, edge_cells, sides, out_ref,
    middle, padded, field, hidden, ends, sems,
):
    rows, cells, channels = x_ref.shape
    bases = one_ref.shape[0]
    chunks = channels // LANES
    padded[...] = jnp.zeros_like(padded)
    chosen = line_choice(filter_ref.shape[1])
    lines = filter_lines(filter_ref, edge_ref, mask_ref, padded, chosen)
    fill_toeplitz(toeplitz, lambda r, k: lines[k][r : r + 1, :], rows, bases, lambda r: r % block)
    kept = list(range(REACH)) + list(range(rows - REACH, rows))
    fill_toeplitz(wide_toeplitz, lambda r, k: lines[k][kept[r] : kept[r] + 1, :], 2 * REACH, bases, place_of)
    shifted = [r - LAT_REACH for r in range(REACH)] + [rows - LAT_REACH + r for r in range(REACH)]
    own = range(LAT_REACH, 2 * REACH - LAT_REACH, 2)
    rim_toeplitz[...] = jnp.zeros_like(rim_toeplitz)
    fill_toeplitz(
        rim_toeplitz, lambda r, k: lines[k][shifted[r] : shifted[r] + 1, :], 2 * REACH, bases, place_of, own
    )
    one, two = lane_weights(one_ref, 0.5), lane_weights(two_ref)
    starts = range(0, rows, block)
    windows = (cells - WINDOW) // CELLS + 1
    span = windows * CELLS

    def load(c):
        blank = jnp.zeros((LAT_REACH, cells, LANES), F32)
        field[c, :LAT_REACH] = blank
        field[c, LAT_REACH : LAT_REACH + rows] = x_ref[:, :, lanes_of(c)].astype(F32)
        field[c, LAT_REACH + rows :] = blank
        blank = jnp.zeros((REACH, span, LANES), F32)
        hidden[c, :REACH] = blank
        hidden[c, rows:] = blank

    def first(items, start):
        low, high = max(start, LAT_REACH), min(start + block, rows - LAT_REACH)
        tall = [field[c, start : start + block + REACH, w * CELLS : w * CELLS + WINDOW] for c, w in items]
        values = product(toeplitz, low, high, tall, [one[c] for c, w in items])
        for (c, w), value in zip(items, values):
            hidden[c, low + LAT_REACH : high + LAT_REACH, w * CELLS : (w + 1) * CELLS] = erf_gelu(value)

    def second(c, start, pair):
        low, high = max(start, REACH), min(start + block, rows - REACH)
        tall = [hidden[c, start : start + block + REACH, w * CELLS : w * CELLS + WINDOW] for w in pair]
        values = product(toeplitz, low, high, tall, [two[c]] * len(pair))
        at = slice(low - REACH, high - REACH)
        for w, value in zip(pair, values):
            if w in (0, windows - 2):
                ends[c, at, (w > 0) * CELLS : (w > 0) * CELLS + CELLS] = value
        if len(pair) == 2 and pair[0] > 0:
            span = slice((pair[0] - 1) * CELLS, (pair[0] + 1) * CELLS)
            middle[at, span, lanes_of(c)] = jnp.concatenate(values, 1).astype(BF16)

    def export(c):
        for i, row in enumerate((REACH, rows - REACH)):
            part = jnp.concatenate([hidden[c, row : row + REACH], jnp.zeros((REACH, cells - span, LANES), F32)], 1)
            edge_rows[i * REACH : (i + 1) * REACH, :, lanes_of(c)] = part.astype(BF16)
        part = hidden[c, 2 * REACH : rows - REACH]
        edge_cells[:, :, lanes_of(c)] = jnp.concatenate([part[:, :CELLS], part[:, span - CELLS :]], 1).astype(BF16)
        sides[:, :, lanes_of(c)] = ends[c].astype(BF16)

    part = functools.partial
    steps = [([part(load, c)], []) for c in range(chunks)]
    for items in pairs_of([(c, w) for c in range(chunks) for w in range(windows)]):
        steps[items[-1][0]][0].extend(part(first, items, start) for start in starts)
    for c in range(chunks):
        pairs = [[0, windows - 2]] + pairs_of(list(range(1, windows - 2)))
        steps[c][1].extend(part(second, c, start, pair) for start in starts for pair in pairs)
        steps[c][1].append(part(export, c))
    for c in range(chunks - 1, 0, -1):
        if c * windows % 2:
            straddle = steps[c][0][1 : 1 + len(starts)]
            steps[c][0][1 : 1 + len(starts)] = []
            steps[c - 1][0].extend([steps[c][0].pop(0)] + straddle)
    run_mixed(steps)
    target = out_ref.at[pl.ds(REACH, rows - 2 * REACH), pl.ds(TILE, cells - 2 * TILE)]
    copy = pltpu.make_async_copy(middle, target, sems.at[0])
    copy.start()
    copy.wait()


def ordered(odd, a, b):
    return jnp.where(odd, a, b).astype(F32), jnp.where(odd, b, a).astype(F32)


def pick(received, turn):
    value = received[-1]
    for j in range(TURNS - 1):
        value = jnp.where(turn == j, received[j], value)
    return value


def below_and_above(received):
    turn = lax.axis_index("lat") % TURNS
    return pick(received, (turn + TURNS - 1) % TURNS).astype(F32), pick(received, turn).astype(F32)


def in_chip(received):
    return pick(received, (lax.axis_index("lat") + 1) % TURNS)


def rim_kernel(
    block, x_ref, turn_0, turn_1, turn_2, lon_b, rows_in, cells_in, sides_in,
    toeplitz, known_toeplitz, wide_toeplitz, one_ref, two_ref,
    rim_toeplitz, rim_out, side_out, ends, field, hidden,
):
    rows, cells, channels = x_ref.shape
    bases = one_ref.shape[0]
    chunks = channels // LANES
    group = bases * CELLS
    edge = REACH * (cells // CELLS)
    columns = cells // CELLS + 1
    turns, lon_odd = (turn_0, turn_1, turn_2), lax.axis_index("lon") % 2 == 1
    one, two = lane_weights(one_ref, 0.5), lane_weights(two_ref)
    tags = below_and_above([v[edge] for v in turns])

    def tag_line(r, k):
        at = r % LAT_REACH
        return tags[0 if r < REACH else 1][at : at + 1, lanes_of(k)]

    own = slice(LAT_REACH * group, (2 * REACH - LAT_REACH) * group)
    rim_toeplitz[own, :] = known_toeplitz[own, :]
    fill_toeplitz(rim_toeplitz, tag_line, 2 * REACH, bases, place_of, (0, 2 * REACH - LAT_REACH))

    def load(c):
        lanes = lanes_of(c)
        lat = below_and_above([v[:edge, :, lanes] for v in turns])
        lon = ordered(lon_odd, in_chip([v[:rows, :, lanes] for v in turns]), lon_b[:, :, lanes])
        inner = slice(REACH, rows - REACH)
        blank = jnp.zeros((REACH, CELLS, LANES), F32)
        for side in range(2):
            at = slice(side * (rows + REACH), side * (rows + REACH) + REACH)
            field[c, at, CELLS : CELLS + cells] = lat[side].reshape(REACH, cells, LANES)
            own = slice(side * (rows - REACH), side * (rows - REACH) + REACH)
            at = slice(own.start + REACH, own.stop + REACH)
            field[c, at, CELLS : CELLS + cells] = x_ref[own, :, lanes].astype(F32)
            own = slice(side * (cells - TILE), side * (cells - TILE) + TILE)
            at = slice(own.start + CELLS, own.stop + CELLS)
            field[c, 2 * REACH : rows, at] = x_ref[inner, own, lanes].astype(F32)
            span = slice(side * (CELLS + cells), side * (CELLS + cells) + CELLS)
            field[c, REACH : REACH + rows, span] = lon[side]
            for end in range(2):
                at = slice(end * (rows + REACH), end * (rows + REACH) + REACH)
                field[c, at, span] = blank
                hidden[c, end * rows : end * rows + REACH, side * cells : side * cells + CELLS] = blank
        span = cells - CELLS
        for i, at in enumerate((REACH, rows - REACH)):
            part = rows_in[i * REACH : (i + 1) * REACH, :, lanes].astype(F32)
            hidden[c, at : at + REACH, CELLS : CELLS + span] = part[:, :span]
        part = cells_in[:, :, lanes].astype(F32)
        at = slice(2 * REACH, rows - REACH)
        hidden[c, at, CELLS : 2 * CELLS] = part[:, :CELLS]
        hidden[c, at, cells - CELLS : cells] = part[:, CELLS:]

    def rims(ref, c, span):
        last = ref.shape[1] - 2 * REACH
        return jnp.concatenate([ref[c, : 2 * REACH, span], ref[c, last:, span]], 0)

    def first_rows(items):
        tall = [rims(field, c, slice(w * CELLS, w * CELLS + WINDOW)) for c, w in items]
        values = product(rim_toeplitz, 0, 2 * REACH, tall, [one[c] for c, w in items])
        for (c, w), value in zip(items, values):
            value = erf_gelu(value)
            hidden[c, :REACH, w * CELLS : (w + 1) * CELLS] = value[:REACH]
            hidden[c, rows:, w * CELLS : (w + 1) * CELLS] = value[REACH:]

    def first_sides(c, start):
        low, high = max(start, LAT_REACH), min(start + block, rows - LAT_REACH)
        at = slice(start + LAT_REACH, start + LAT_REACH + block + REACH)
        tall = [field[c, at, s : s + WINDOW] for s in (0, cells)]
        values = product(toeplitz, low, high, tall, [one[c]] * 2)
        for s, value in zip((0, cells), values):
            hidden[c, low + LAT_REACH : high + LAT_REACH, s : s + CELLS] = erf_gelu(value)

    def second_rows(c, pair):
        tall = [rims(hidden, c, slice(w * CELLS, w * CELLS + WINDOW)) for w in pair]
        values = product(wide_toeplitz, 0, 2 * REACH, tall, [two[c]] * 2)
        blank = jnp.zeros((2 * REACH, CELLS, LANES), F32)
        if pair == [1, columns - 3]:
            rim_out[:, :TILE, lanes_of(c)] = jnp.concatenate([blank, values[0]], 1).astype(BF16)
            rim_out[:, cells - TILE :, lanes_of(c)] = jnp.concatenate([values[1], blank], 1).astype(BF16)
        else:
            rim_out[:, pair[0] * CELLS : (pair[0] + 2) * CELLS, lanes_of(c)] = jnp.concatenate(values, 1).astype(BF16)

    def second_sides(c, start):
        low, high = max(start, REACH), min(start + block, rows - REACH)
        tall = [hidden[c, start : start + block + REACH, s : s + WINDOW] for s in (0, cells - CELLS)]
        values = product(toeplitz, low, high, tall, [two[c]] * 2)
        at = slice(low - REACH, high - REACH)
        inner = sides_in[at, :, lanes_of(c)].astype(F32)
        side_out[0, at, :, lanes_of(c)] = jnp.concatenate([values[0], inner[:, :CELLS]], 1).astype(BF16)
        side_out[1, at, :, lanes_of(c)] = jnp.concatenate([inner[:, CELLS:], values[1]], 1).astype(BF16)

    def export(c):
        for side in range(2):
            span = slice(side * (cells - CELLS), side * (cells - CELLS) + WINDOW)
            ends[side, :, :, lanes_of(c)] = rims(hidden, c, span).astype(BF16)

    part = functools.partial
    steps = [([part(load, c)], []) for c in range(chunks)]
    items = [(c, w) for c in range(chunks) for w in range(1, columns - 1)]
    for pair in pairs_of(items):
        steps[pair[-1][0]][0].append(part(first_rows, pair))
    for c in range(chunks - 1, 0, -1):
        if c * (columns - 2) % 2:
            steps[c - 1][0].extend([steps[c][0].pop(0), steps[c][0].pop(0)])
    starts = range(0, rows, block)
    for c, (first, second) in enumerate(steps):
        first.extend(part(first_sides, c, start) for start in starts)
        second.extend(
            part(second_rows, c, pair) for pair in [[1, columns - 3]] + pairs_of(list(range(2, columns - 3)))
        )
        second.extend(part(second_sides, c, start) for start in starts)
        second.append(part(export, c))
    run_mixed(steps)


def corner_kernel(
    x_ref, turn_0, turn_1, turn_2, lon_b, corner_b, corner_a, ends, rim_toeplitz, wide_toeplitz, one_ref, two_ref,
    side_out, rim_out, begun_ref, out_ref, corner_out, sems,
):
    del begun_ref
    rows, cells, channels = x_ref.shape
    chunks = channels // LANES
    edge = REACH * (cells // CELLS)
    inner = pl.ds(REACH, rows - 2 * REACH)
    ends_at = (pl.ds(0, REACH), pl.ds(rows - REACH, REACH))
    sides_at = (pl.ds(0, TILE), pl.ds(cells - TILE, TILE))
    span = pl.ds(TILE, cells - 2 * TILE)
    moves = []
    for i in range(2):
        moves.append((side_out.at[i], out_ref.at[inner, sides_at[i]]))
        moves.append((rim_out.at[pl.ds(i * REACH, REACH), span], out_ref.at[ends_at[i], span]))
    copies = [pltpu.make_async_copy(source, target, sems.at[i]) for i, (source, target) in enumerate(moves)]
    for copy in copies:
        copy.start()
    turns, lon_odd = (turn_0, turn_1, turn_2), lax.axis_index("lon") % 2 == 1
    one, two = lane_weights(one_ref, 0.5), lane_weights(two_ref)

    def first(c):
        lanes = lanes_of(c)
        lat = below_and_above([v[:edge, :, lanes] for v in turns])
        lon = ordered(lon_odd, in_chip([v[:rows, :, lanes] for v in turns]), lon_b[:, :, lanes])
        corner = ordered(lon_odd, corner_a[:, lanes], corner_b[:, lanes])
        tall = []
        for side in range(2):
            own = slice(side * (cells - CELLS), side * (cells - CELLS) + CELLS)
            above = [v.reshape(REACH, cells, LANES)[:, own] for v in lat]
            tiles = slice(side * (cells - TILE), side * (cells - TILE) + TILE)
            half = slice(side * (TILE - CELLS), side * (TILE - CELLS) + CELLS)
            mine = [x_ref[r : r + REACH, tiles, lanes].astype(F32)[:, half] for r in (0, rows - REACH)]
            near = lon[side]
            far = corner[side].reshape(2, REACH, CELLS, LANES)
            own = jnp.concatenate([above[0], mine[0], mine[1], above[1]], 0)
            other = jnp.concatenate([far[0], near[:REACH], near[rows - REACH :], far[1]], 0)
            tall.append(jnp.concatenate([own, other] if side else [other, own], 1))
        return [erf_gelu(v) for v in product(rim_toeplitz, 0, 2 * REACH, tall, [one[c]] * 2)]

    def second(c, blocks):
        lanes = lanes_of(c)
        tall = []
        for side in range(2):
            near = ends[side, :, :, lanes].astype(F32)
            own = near[:, side * CELLS : side * CELLS + CELLS]
            own = jnp.concatenate([blocks[side][:REACH], own[REACH : 3 * REACH], blocks[side][REACH:]], 0)
            tall.append(jnp.concatenate([near[:, :CELLS], own] if side else [own, near[:, CELLS:]], 1))
        values = product(wide_toeplitz, 0, 2 * REACH, tall, [two[c]] * 2)
        for side in range(2):
            tiles = slice(side * (cells - TILE), side * (cells - TILE) + TILE)
            near = rim_out[:, tiles, lanes].astype(F32)
            near = near[:, : TILE - CELLS] if side else near[:, CELLS:]
            whole = [near, values[side]] if side else [values[side], near]
            corner_out[side, :, :, lanes] = jnp.concatenate(whole, 1).astype(BF16)

    hidden = [first(c) for c in range(chunks)]
    for c in range(chunks):
        second(c, hidden[c])
    last = []
    for side in range(2):
        for end in range(2):
            source = corner_out.at[side, pl.ds(end * REACH, REACH)]
            target = out_ref.at[ends_at[end], sides_at[side]]
            last.append(pltpu.make_async_copy(source, target, sems.at[len(copies) + len(last)]))
            last[-1].start()
    for copy in copies + last:
        copy.wait()


def per_device(state_field, filters, band_edges, basis_mask, weights_one, weights_two):
    rows, cells, channels = state_field.shape
    bases = filters.shape[1]
    group = bases * CELLS
    chunks = channels // LANES
    block = max(b for b in range(2, rows + 1, 2) if rows % b == 0 and (b + REACH) * WINDOW <= DEPTH)
    lat_peers, lon_peers = lax.axis_size("lat"), lax.axis_size("lon")
    turn, lon = lax.axis_index("lat") % TURNS, lax.axis_index("lon")

    anywhere = pl.BlockSpec(memory_space=pl.ANY)
    vmem = pl.BlockSpec(memory_space=pltpu.VMEM)
    params = pltpu.CompilerParams(vmem_limit_bytes=VMEM_BYTES)
    dma = pltpu.SemaphoreType.DMA

    def array(*shape, dtype=BF16):
        return jax.ShapeDtypeStruct(shape, dtype)

    def scratch(*shape, dtype=BF16):
        return pltpu.VMEM(shape, dtype)

    across = cells // CELLS
    edge = REACH * across
    filter_args = (filters.transpose(1, 3, 2, 0), band_edges.T, basis_mask.T)
    *turns, lon_b = pl.pallas_call(
        prep_kernel,
        out_shape=(array(edge + 1, CELLS, channels),) * TURNS + (array(rows, CELLS, channels),),
        in_specs=[anywhere] * 5,
        out_specs=(anywhere,) * (TURNS + 1),
        scratch_shapes=[
            scratch(bases, filters.shape[3], BANDS, rows, dtype=F32),
            scratch(2, rows, dtype=jnp.int32), scratch(bases, rows, dtype=jnp.int32),
            scratch(TURNS, edge + 1, CELLS, channels), scratch(rows, CELLS, channels),
            scratch(bases, LANES, LANES, dtype=F32), scratch(2, CELLS, channels, dtype=F32),
            dma((7,)), dma((2 * TURNS + 1,)),
        ],
        compiler_params=pltpu.CompilerParams(vmem_limit_bytes=60 * 1024 * 1024),
        cost_estimate=pl.CostEstimate(flops=0, bytes_accessed=8 * REACH * cells * channels, transcendentals=0),
        name="prep",
    )(
        state_field.reshape(rows * across, CELLS, channels), state_field.reshape(rows, across, CELLS, channels),
        *filter_args,
    )
    both = ("lat", "lon")
    turns = [lax.ppermute(v, both, turn_swaps(lat_peers, lon_peers, j)) for j, v in enumerate(turns)]
    lon_b = lax.ppermute(lon_b, "lon", swaps(lon_peers, True))

    middle = rows - 2 * REACH
    flops = 2 * (2 * rows - 3 * REACH) * (cells - 2 * CELLS) * bases * DEPTH * channels
    cost = pl.CostEstimate(flops=flops, bytes_accessed=4 * state_field.size, transcendentals=0)
    toeplitz, known, wide, edge_rows, edge_cells, sides, begun = pl.pallas_call(
        functools.partial(inner_kernel, block),
        out_shape=(
            array(rows * group, DEPTH), array(2 * REACH * group, DEPTH), array(2 * REACH * group, DEPTH),
            array(2 * REACH, cells, channels), array(middle - REACH, TILE, channels),
            array(middle, TILE, channels), array(rows, cells, channels),
        ),
        in_specs=[vmem] * 6,
        out_specs=(vmem,) * 6 + (anywhere,),
        scratch_shapes=[
            scratch(middle, cells - 2 * TILE, channels), scratch(bases, LANES, LANES, dtype=F32),
            scratch(chunks, rows + REACH, cells, LANES, dtype=F32),
            scratch(chunks, rows + REACH, cells - CELLS, LANES, dtype=F32),
            scratch(chunks, middle, TILE, LANES, dtype=F32), dma((1,)),
        ],
        compiler_params=params,
        cost_estimate=cost,
        name="inner",
    )(state_field, *filter_args, weights_one, weights_two)

    *turns, sides = lax.optimization_barrier((*turns, sides))

    def corner_send(leading, second):
        start = jnp.where(leading, 0, cells - CELLS)
        parts = [v[:edge].reshape(REACH, cells, channels) for v in turns]
        parts = [lax.dynamic_slice_in_dim(v, start, CELLS, 1) for v in parts]
        below = jnp.where(turn == 1, parts[0], jnp.where(turn == 2, parts[1], parts[2]))
        above = jnp.where(turn == 0, parts[0], jnp.where(turn == 1, parts[1], parts[2]))
        sent = jnp.concatenate([below, above], 0).reshape(2 * REACH * CELLS, channels)
        return lax.ppermute(sent, "lon", swaps(lon_peers, second))

    corner_b = corner_send(lon % 2 == 0, True)
    corner_a = corner_send(lon % 2 == 1, False)
    rim_toeplitz, rim_out, side_out, ends = pl.pallas_call(
        functools.partial(rim_kernel, block),
        out_shape=(
            array(2 * REACH * group, DEPTH), array(2 * REACH, cells, channels), array(2, middle, TILE, channels),
            array(2, 4 * REACH, WINDOW, channels),
        ),
        in_specs=[vmem] * 13,
        out_specs=(vmem,) * 4,
        scratch_shapes=[
            scratch(chunks, rows + 2 * REACH, cells + 2 * CELLS, LANES, dtype=F32),
            scratch(chunks, rows + REACH, cells + CELLS, LANES, dtype=F32),
        ],
        compiler_params=params,
        cost_estimate=cost,
        name="rim",
    )(
        state_field, *turns, lon_b, edge_rows, edge_cells, sides,
        toeplitz, known, wide, weights_one, weights_two,
    )
    return pl.pallas_call(
        corner_kernel,
        out_shape=array(rows, cells, channels),
        in_specs=[vmem] * 14 + [anywhere],
        out_specs=anywhere,
        input_output_aliases={14: 0},
        scratch_shapes=[scratch(2, 2 * REACH, TILE, channels), dma((8,))],
        compiler_params=params,
        cost_estimate=cost,
        name="corner",
    )(
        state_field, *turns, lon_b, corner_b, corner_a, ends, rim_toeplitz, wide,
        weights_one, weights_two, side_out, rim_out, begun,
    )


def solution(mesh):
    placed = (
        P("lat", "lon", None),
        P("lat", None, None, None),
        P("lat", None),
        P("lat", None),
        P(),
        P(),
    )
    return jax.shard_map(
        per_device, mesh=mesh, in_specs=placed, out_specs=P("lat", "lon", None), check_vma=False
    )
```

```python
import functools

import jax
import jax.numpy as jnp
from jax import lax
from jax.experimental import pallas as pl
from jax.experimental.pallas import tpu as pltpu
from jax.sharding import PartitionSpec as P

LAT_REACH = 2
LON_REACH = 4
REACH = 2 * LAT_REACH
BANDS = 2 * LAT_REACH + 1
CELLS = 8
WINDOW = CELLS + 2 * LON_REACH
LANES = 128
DEPTH = 2 * LANES
TILE = 16
VMEM_BYTES = 20 * 1024 * 1024
TURNS = 3
PIECE = 4
F32, BF16 = jnp.float32, jnp.bfloat16

ERF_SERIES = (
    1.5956562720156744,
    0.2917503271976864,
    -0.003995570947534282,
    -0.003914369984884403,
    0.0005729703632347449,
)


def erf_gelu(half):
    square = half * half
    series = ERF_SERIES[-1] * square + ERF_SERIES[-2]
    for term in ERF_SERIES[-3::-1]:
        series = series * square + term
    return half + half * jnp.tanh(half * series)


def swaps(peers, second):
    pairs = [(i, i + 1) for i in range(1 if second else 0, peers - 1, 2)]
    if second:
        pairs.append((peers - 1, 0))
    return pairs + [(j, i) for i, j in pairs]


def turn_swaps(peers, width, turn):
    pairs = [(i, i + 1) for i in range(peers - 1) if i % TURNS == turn]
    pairs += [(j, i) for i, j in pairs]
    alone = set(range(peers)) - {i for i, _ in pairs}
    result = [(i * width + k, j * width + k) for i, j in pairs for k in range(width)]
    return result + [(i * width + k, i * width + (k ^ 1)) for i in sorted(alone) for k in range(width)]


def pairs_of(items):
    return [items[i : i + 2] for i in range(0, len(items), 2)]


def lanes_of(chunk):
    return slice(chunk * LANES, (chunk + 1) * LANES)


def fill_toeplitz(toeplitz, line_of, rows, bases, place_of, pairs=None):
    group = bases * CELLS
    blank = jnp.zeros((CELLS, DEPTH - LANES), F32)
    for row in pairs or range(0, rows, 2):
        parts = []
        for r in (row, row + 1):
            for basis in range(bases):
                line = jnp.broadcast_to(line_of(r, basis), (CELLS, LANES))
                line = jnp.concatenate([line, blank], 1)
                parts.append(pltpu.roll(line, place_of(r) * WINDOW, 1, stride=1, stride_axis=0))
        toeplitz[row * group : (row + 2) * group, :] = jnp.concatenate(parts, 0).astype(BF16)


def lane_weights(ref, scale=1.0):
    bases, channels = ref.shape
    return [[ref[k : k + 1, lanes_of(c)] * scale for k in range(bases)] for c in range(channels // LANES)]


def product(matrix, low, high, windows, weights):
    wide = [w.astype(BF16).reshape(DEPTH, LANES) for w in windows]
    wide = jnp.concatenate(wide, 1)
    bases = len(weights[0])
    group = bases * CELLS
    scales = [jnp.concatenate([w[k] for w in weights], 1) for k in range(bases)]
    pieces = []
    for at in range(low, high, PIECE):
        to = min(at + PIECE, high)
        result = jnp.dot(matrix[at * group : to * group, :], wide, preferred_element_type=F32)
        result = result.reshape(to - at, bases, CELLS, len(windows) * LANES)
        total = result[:, 0] * scales[0]
        for k in range(1, bases):
            total = total + result[:, k] * scales[k]
        pieces.append(total)
    total = jnp.concatenate(pieces, 0) if len(pieces) > 1 else pieces[0]
    return [total[:, :, i * LANES : (i + 1) * LANES] for i in range(len(windows))]


def run_mixed(steps):
    waiting = []
    for first, second in steps:
        total, done = len(waiting), 0
        for i, unit in enumerate(first):
            unit()
            while done * len(first) < total * (i + 1):
                waiting.pop(0)()
                done += 1
        for unit in waiting:
            unit()
        waiting = list(second)
    for unit in waiting:
        unit()


def line_choice(lags):
    at = lax.broadcasted_iota(jnp.int32, (LANES, LANES), 0)
    lane = lax.broadcasted_iota(jnp.int32, (LANES, LANES), 1)
    chosen = (at // 8 == lane % WINDOW) & (at % 8 == lane // WINDOW) & (at % 8 < BANDS) & (at // 8 < lags)
    return jnp.where(chosen, 1.0, 0.0).astype(BF16)


def filter_lines(filter_ref, edge_ref, mask_ref, padded, chosen):
    bases, lags, bands, rows = filter_ref.shape
    source = lax.axis_index("lat") * rows + lax.broadcasted_iota(jnp.int32, (bands, rows), 1) - LAT_REACH
    source = source + lax.broadcasted_iota(jnp.int32, (bands, rows), 0)
    inside = (source >= edge_ref[0:1, :]) & (source < edge_ref[1:2, :])
    for k in range(bases):
        keep = inside & (mask_ref[k : k + 1, :] != 0)
        for m in range(lags):
            padded[k, m * 8 : m * 8 + bands, :rows] = jnp.where(keep, filter_ref[k, m], 0.0)
    return [jnp.dot(padded[k].T.astype(BF16), chosen, preferred_element_type=F32) for k in range(bases)]


def prep_kernel(
    flat_ref, groups_ref, filter_in, edge_in, mask_in, turn_0, turn_1, turn_2, lon_b,
    filter_ref, edge_ref, mask_ref, payloads, far, padded, tags, sems, out_sems,
):
    bases, lags, bands, rows = filter_in.shape
    across = groups_ref.shape[1]
    edge = REACH * across
    turn, lon_odd = lax.axis_index("lat") % TURNS, lax.axis_index("lon") % 2
    small = [
        pltpu.make_async_copy(filter_in, filter_ref, sems.at[0]),
        pltpu.make_async_copy(edge_in, edge_ref, sems.at[1]),
        pltpu.make_async_copy(mask_in, mask_ref, sems.at[2]),
    ]
    last, first = pl.ds((rows - REACH) * across, edge), pl.ds(0, edge)
    near_at, far_at = (1 - lon_odd) * (across - 1), lon_odd * (across - 1)
    copies = [
        pltpu.make_async_copy(flat_ref.at[last], payloads.at[0, pl.ds(0, edge)], sems.at[3]),
        pltpu.make_async_copy(flat_ref.at[first], payloads.at[1, pl.ds(0, edge)], sems.at[4]),
        pltpu.make_async_copy(groups_ref.at[:, near_at], payloads.at[2, pl.ds(0, rows)], sems.at[5]),
        pltpu.make_async_copy(groups_ref.at[:, far_at], far, sems.at[6]),
    ]
    for copy in copies[:2] + small + copies[2:]:
        copy.start()
    padded[...] = jnp.zeros_like(padded)
    tags[...] = jnp.zeros_like(tags)
    payloads[2, rows:] = jnp.zeros((edge + 1 - rows,) + payloads.shape[2:], BF16)
    chosen = line_choice(lags)
    pending = []

    def send(source, target):
        pending.append(pltpu.make_async_copy(source, target, out_sems.at[len(pending)]))
        pending[-1].start()

    outs = [(out, (turn + TURNS - j) % TURNS) for j, out in enumerate((turn_0, turn_1, turn_2))]
    for copy in copies[:3]:
        copy.wait()
    for out, role in outs:
        send(payloads.at[role, pl.ds(0, edge)], out.at[pl.ds(0, edge)])
    copies[3].wait()
    send(far, lon_b)
    for copy in small:
        copy.wait()
    for k, line in enumerate(filter_lines(filter_ref, edge_ref, mask_ref, padded, chosen)):
        tags[0, :LAT_REACH, lanes_of(k)] = line[rows - LAT_REACH : rows]
        tags[1, :LAT_REACH, lanes_of(k)] = line[:LAT_REACH]
    payloads[0, edge] = tags[0].astype(BF16)
    payloads[1, edge] = tags[1].astype(BF16)
    for out, role in outs:
        send(payloads.at[role, edge], out.at[edge])
    for copy in pending:
        copy.wait()


def place_of(r):
    return r if r < REACH else REACH + r


def inner_kernel(
    block, x_ref, filter_ref, edge_ref, mask_ref, one_ref, two_ref,
    toeplitz, rim_toeplitz, wide_toeplitz, edge_rows, edge_cells, sides, out_ref,
    middle, padded, field, hidden, ends, sems,
):
    rows, cells, channels = x_ref.shape
    bases = one_ref.shape[0]
    chunks = channels // LANES
    padded[...] = jnp.zeros_like(padded)
    chosen = line_choice(filter_ref.shape[1])
    lines = filter_lines(filter_ref, edge_ref, mask_ref, padded, chosen)
    fill_toeplitz(toeplitz, lambda r, k: lines[k][r : r + 1, :], rows, bases, lambda r: r % block)
    kept = list(range(REACH)) + list(range(rows - REACH, rows))
    fill_toeplitz(wide_toeplitz, lambda r, k: lines[k][kept[r] : kept[r] + 1, :], 2 * REACH, bases, place_of)
    shifted = [r - LAT_REACH for r in range(REACH)] + [rows - LAT_REACH + r for r in range(REACH)]
    own = range(LAT_REACH, 2 * REACH - LAT_REACH, 2)
    rim_toeplitz[...] = jnp.zeros_like(rim_toeplitz)
    fill_toeplitz(
        rim_toeplitz, lambda r, k: lines[k][shifted[r] : shifted[r] + 1, :], 2 * REACH, bases, place_of, own
    )
    one, two = lane_weights(one_ref, 0.5), lane_weights(two_ref)
    starts = range(0, rows, block)
    windows = (cells - WINDOW) // CELLS + 1
    span = windows * CELLS

    def load(c):
        blank = jnp.zeros((LAT_REACH, cells, LANES), F32)
        field[c, :LAT_REACH] = blank
        field[c, LAT_REACH : LAT_REACH + rows] = x_ref[:, :, lanes_of(c)].astype(F32)
        field[c, LAT_REACH + rows :] = blank
        blank = jnp.zeros((REACH, span, LANES), F32)
        hidden[c, :REACH] = blank
        hidden[c, rows:] = blank

    def first(items, start):
        low, high = max(start, LAT_REACH), min(start + block, rows - LAT_REACH)
        tall = [field[c, start : start + block + REACH, w * CELLS : w * CELLS + WINDOW] for c, w in items]
        values = product(toeplitz, low, high, tall, [one[c] for c, w in items])
        for (c, w), value in zip(items, values):
            hidden[c, low + LAT_REACH : high + LAT_REACH, w * CELLS : (w + 1) * CELLS] = erf_gelu(value)

    def second(c, start, pair):
        low, high = max(start, REACH), min(start + block, rows - REACH)
        tall = [hidden[c, start : start + block + REACH, w * CELLS : w * CELLS + WINDOW] for w in pair]
        values = product(toeplitz, low, high, tall, [two[c]] * len(pair))
        at = slice(low - REACH, high - REACH)
        for w, value in zip(pair, values):
            if w in (0, windows - 2):
                ends[c, at, (w > 0) * CELLS : (w > 0) * CELLS + CELLS] = value
        if len(pair) == 2 and pair[0] > 0:
            span = slice((pair[0] - 1) * CELLS, (pair[0] + 1) * CELLS)
            middle[at, span, lanes_of(c)] = jnp.concatenate(values, 1).astype(BF16)

    def export(c):
        for i, row in enumerate((REACH, rows - REACH)):
            part = jnp.concatenate([hidden[c, row : row + REACH], jnp.zeros((REACH, cells - span, LANES), F32)], 1)
            edge_rows[i * REACH : (i + 1) * REACH, :, lanes_of(c)] = part.astype(BF16)
        part = hidden[c, 2 * REACH : rows - REACH]
        edge_cells[:, :, lanes_of(c)] = jnp.concatenate([part[:, :CELLS], part[:, span - CELLS :]], 1).astype(BF16)
        sides[:, :, lanes_of(c)] = ends[c].astype(BF16)

    part = functools.partial
    steps = [([part(load, c)], []) for c in range(chunks)]
    for items in pairs_of([(c, w) for c in range(chunks) for w in range(windows)]):
        steps[items[-1][0]][0].extend(part(first, items, start) for start in starts)
    for c in range(chunks):
        pairs = [[0, windows - 2]] + pairs_of(list(range(1, windows - 2)))
        steps[c][1].extend(part(second, c, start, pair) for start in starts for pair in pairs)
        steps[c][1].append(part(export, c))
    for c in range(chunks - 1, 0, -1):
        if c * windows % 2:
            straddle = steps[c][0][1 : 1 + len(starts)]
            steps[c][0][1 : 1 + len(starts)] = []
            steps[c - 1][0].extend([steps[c][0].pop(0)] + straddle)
    run_mixed(steps)
    target = out_ref.at[pl.ds(REACH, rows - 2 * REACH), pl.ds(TILE, cells - 2 * TILE)]
    copy = pltpu.make_async_copy(middle, target, sems.at[0])
    copy.start()
    copy.wait()


def ordered(odd, a, b):
    return jnp.where(odd, a, b).astype(F32), jnp.where(odd, b, a).astype(F32)


def pick(received, turn):
    value = received[-1]
    for j in range(TURNS - 1):
        value = jnp.where(turn == j, received[j], value)
    return value


def below_and_above(received):
    turn = lax.axis_index("lat") % TURNS
    return pick(received, (turn + TURNS - 1) % TURNS).astype(F32), pick(received, turn).astype(F32)


def in_chip(received):
    return pick(received, (lax.axis_index("lat") + 1) % TURNS)


def rim_kernel(
    block, x_ref, turn_0, turn_1, turn_2, lon_b, rows_in, cells_in, sides_in,
    toeplitz, known_toeplitz, wide_toeplitz, one_ref, two_ref,
    rim_toeplitz, rim_out, side_out, ends, field, hidden,
):
    rows, cells, channels = x_ref.shape
    bases = one_ref.shape[0]
    chunks = channels // LANES
    group = bases * CELLS
    edge = REACH * (cells // CELLS)
    columns = cells // CELLS + 1
    turns, lon_odd = (turn_0, turn_1, turn_2), lax.axis_index("lon") % 2 == 1
    one, two = lane_weights(one_ref, 0.5), lane_weights(two_ref)
    tags = below_and_above([v[edge] for v in turns])

    def tag_line(r, k):
        at = r % LAT_REACH
        return tags[0 if r < REACH else 1][at : at + 1, lanes_of(k)]

    own = slice(LAT_REACH * group, (2 * REACH - LAT_REACH) * group)
    rim_toeplitz[own, :] = known_toeplitz[own, :]
    fill_toeplitz(rim_toeplitz, tag_line, 2 * REACH, bases, place_of, (0, 2 * REACH - LAT_REACH))

    def load(c):
        lanes = lanes_of(c)
        lat = below_and_above([v[:edge, :, lanes] for v in turns])
        lon = ordered(lon_odd, in_chip([v[:rows, :, lanes] for v in turns]), lon_b[:, :, lanes])
        inner = slice(REACH, rows - REACH)
        blank = jnp.zeros((REACH, CELLS, LANES), F32)
        for side in range(2):
            at = slice(side * (rows + REACH), side * (rows + REACH) + REACH)
            field[c, at, CELLS : CELLS + cells] = lat[side].reshape(REACH, cells, LANES)
            own = slice(side * (rows - REACH), side * (rows - REACH) + REACH)
            at = slice(own.start + REACH, own.stop + REACH)
            field[c, at, CELLS : CELLS + cells] = x_ref[own, :, lanes].astype(F32)
            own = slice(side * (cells - TILE), side * (cells - TILE) + TILE)
            at = slice(own.start + CELLS, own.stop + CELLS)
            field[c, 2 * REACH : rows, at] = x_ref[inner, own, lanes].astype(F32)
            span = slice(side * (CELLS + cells), side * (CELLS + cells) + CELLS)
            field[c, REACH : REACH + rows, span] = lon[side]
            for end in range(2):
                at = slice(end * (rows + REACH), end * (rows + REACH) + REACH)
                field[c, at, span] = blank
                hidden[c, end * rows : end * rows + REACH, side * cells : side * cells + CELLS] = blank
        span = cells - CELLS
        for i, at in enumerate((REACH, rows - REACH)):
            part = rows_in[i * REACH : (i + 1) * REACH, :, lanes].astype(F32)
            hidden[c, at : at + REACH, CELLS : CELLS + span] = part[:, :span]
        part = cells_in[:, :, lanes].astype(F32)
        at = slice(2 * REACH, rows - REACH)
        hidden[c, at, CELLS : 2 * CELLS] = part[:, :CELLS]
        hidden[c, at, cells - CELLS : cells] = part[:, CELLS:]

    def rims(ref, c, span):
        last = ref.shape[1] - 2 * REACH
        return jnp.concatenate([ref[c, : 2 * REACH, span], ref[c, last:, span]], 0)

    def first_rows(items):
        tall = [rims(field, c, slice(w * CELLS, w * CELLS + WINDOW)) for c, w in items]
        values = product(rim_toeplitz, 0, 2 * REACH, tall, [one[c] for c, w in items])
        for (c, w), value in zip(items, values):
            value = erf_gelu(value)
            hidden[c, :REACH, w * CELLS : (w + 1) * CELLS] = value[:REACH]
            hidden[c, rows:, w * CELLS : (w + 1) * CELLS] = value[REACH:]

    def first_sides(c, start):
        low, high = max(start, LAT_REACH), min(start + block, rows - LAT_REACH)
        at = slice(start + LAT_REACH, start + LAT_REACH + block + REACH)
        tall = [field[c, at, s : s + WINDOW] for s in (0, cells)]
        values = product(toeplitz, low, high, tall, [one[c]] * 2)
        for s, value in zip((0, cells), values):
            hidden[c, low + LAT_REACH : high + LAT_REACH, s : s + CELLS] = erf_gelu(value)

    def second_rows(c, pair):
        tall = [rims(hidden, c, slice(w * CELLS, w * CELLS + WINDOW)) for w in pair]
        values = product(wide_toeplitz, 0, 2 * REACH, tall, [two[c]] * 2)
        blank = jnp.zeros((2 * REACH, CELLS, LANES), F32)
        if pair == [1, columns - 3]:
            rim_out[:, :TILE, lanes_of(c)] = jnp.concatenate([blank, values[0]], 1).astype(BF16)
            rim_out[:, cells - TILE :, lanes_of(c)] = jnp.concatenate([values[1], blank], 1).astype(BF16)
        else:
            rim_out[:, pair[0] * CELLS : (pair[0] + 2) * CELLS, lanes_of(c)] = jnp.concatenate(values, 1).astype(BF16)

    def second_sides(c, start):
        low, high = max(start, REACH), min(start + block, rows - REACH)
        tall = [hidden[c, start : start + block + REACH, s : s + WINDOW] for s in (0, cells - CELLS)]
        values = product(toeplitz, low, high, tall, [two[c]] * 2)
        at = slice(low - REACH, high - REACH)
        inner = sides_in[at, :, lanes_of(c)].astype(F32)
        side_out[0, at, :, lanes_of(c)] = jnp.concatenate([values[0], inner[:, :CELLS]], 1).astype(BF16)
        side_out[1, at, :, lanes_of(c)] = jnp.concatenate([inner[:, CELLS:], values[1]], 1).astype(BF16)

    def export(c):
        for side in range(2):
            span = slice(side * (cells - CELLS), side * (cells - CELLS) + WINDOW)
            ends[side, :, :, lanes_of(c)] = rims(hidden, c, span).astype(BF16)

    part = functools.partial
    steps = [([part(load, c)], []) for c in range(chunks)]
    items = [(c, w) for c in range(chunks) for w in range(1, columns - 1)]
    for pair in pairs_of(items):
        steps[pair[-1][0]][0].append(part(first_rows, pair))
    for c in range(chunks - 1, 0, -1):
        if c * (columns - 2) % 2:
            steps[c - 1][0].extend([steps[c][0].pop(0), steps[c][0].pop(0)])
    starts = range(0, rows, block)
    for c, (first, second) in enumerate(steps):
        first.extend(part(first_sides, c, start) for start in starts)
        second.extend(
            part(second_rows, c, pair) for pair in [[1, columns - 3]] + pairs_of(list(range(2, columns - 3)))
        )
        second.extend(part(second_sides, c, start) for start in starts)
        second.append(part(export, c))
    run_mixed(steps)


def corner_kernel(
    x_ref, turn_0, turn_1, turn_2, lon_b, corner_b, corner_a, ends, rim_toeplitz, wide_toeplitz, one_ref, two_ref,
    side_out, rim_out, begun_ref, out_ref, corner_out, sems,
):
    del begun_ref
    rows, cells, channels = x_ref.shape
    chunks = channels // LANES
    edge = REACH * (cells // CELLS)
    inner = pl.ds(REACH, rows - 2 * REACH)
    ends_at = (pl.ds(0, REACH), pl.ds(rows - REACH, REACH))
    sides_at = (pl.ds(0, TILE), pl.ds(cells - TILE, TILE))
    span = pl.ds(TILE, cells - 2 * TILE)
    moves = []
    for i in range(2):
        moves.append((side_out.at[i], out_ref.at[inner, sides_at[i]]))
        moves.append((rim_out.at[pl.ds(i * REACH, REACH), span], out_ref.at[ends_at[i], span]))
    copies = [pltpu.make_async_copy(source, target, sems.at[i]) for i, (source, target) in enumerate(moves)]
    for copy in copies:
        copy.start()
    turns, lon_odd = (turn_0, turn_1, turn_2), lax.axis_index("lon") % 2 == 1
    one, two = lane_weights(one_ref, 0.5), lane_weights(two_ref)

    def first(c):
        lanes = lanes_of(c)
        lat = below_and_above([v[:edge, :, lanes] for v in turns])
        lon = ordered(lon_odd, in_chip([v[:rows, :, lanes] for v in turns]), lon_b[:, :, lanes])
        corner = ordered(lon_odd, corner_a[:, lanes], corner_b[:, lanes])
        tall = []
        for side in range(2):
            own = slice(side * (cells - CELLS), side * (cells - CELLS) + CELLS)
            above = [v.reshape(REACH, cells, LANES)[:, own] for v in lat]
            tiles = slice(side * (cells - TILE), side * (cells - TILE) + TILE)
            half = slice(side * (TILE - CELLS), side * (TILE - CELLS) + CELLS)
            mine = [x_ref[r : r + REACH, tiles, lanes].astype(F32)[:, half] for r in (0, rows - REACH)]
            near = lon[side]
            far = corner[side].reshape(2, REACH, CELLS, LANES)
            own = jnp.concatenate([above[0], mine[0], mine[1], above[1]], 0)
            other = jnp.concatenate([far[0], near[:REACH], near[rows - REACH :], far[1]], 0)
            tall.append(jnp.concatenate([own, other] if side else [other, own], 1))
        return [erf_gelu(v) for v in product(rim_toeplitz, 0, 2 * REACH, tall, [one[c]] * 2)]

    def second(c, blocks):
        lanes = lanes_of(c)
        tall = []
        for side in range(2):
            near = ends[side, :, :, lanes].astype(F32)
            own = near[:, side * CELLS : side * CELLS + CELLS]
            own = jnp.concatenate([blocks[side][:REACH], own[REACH : 3 * REACH], blocks[side][REACH:]], 0)
            tall.append(jnp.concatenate([near[:, :CELLS], own] if side else [own, near[:, CELLS:]], 1))
        values = product(wide_toeplitz, 0, 2 * REACH, tall, [two[c]] * 2)
        for side in range(2):
            tiles = slice(side * (cells - TILE), side * (cells - TILE) + TILE)
            near = rim_out[:, tiles, lanes].astype(F32)
            near = near[:, : TILE - CELLS] if side else near[:, CELLS:]
            whole = [near, values[side]] if side else [values[side], near]
            corner_out[side, :, :, lanes] = jnp.concatenate(whole, 1).astype(BF16)

    hidden = [first(c) for c in range(chunks)]
    for c in range(chunks):
        second(c, hidden[c])
    last = []
    for side in range(2):
        for end in range(2):
            source = corner_out.at[side, pl.ds(end * REACH, REACH)]
            target = out_ref.at[ends_at[end], sides_at[side]]
            last.append(pltpu.make_async_copy(source, target, sems.at[len(copies) + len(last)]))
            last[-1].start()
    for copy in copies + last:
        copy.wait()


def per_device(state_field, filters, band_edges, basis_mask, weights_one, weights_two):
    rows, cells, channels = state_field.shape
    bases = filters.shape[1]
    group = bases * CELLS
    chunks = channels // LANES
    block = max(b for b in range(2, rows + 1, 2) if rows % b == 0 and (b + REACH) * WINDOW <= DEPTH)
    lat_peers, lon_peers = lax.axis_size("lat"), lax.axis_size("lon")
    turn, lon = lax.axis_index("lat") % TURNS, lax.axis_index("lon")

    anywhere = pl.BlockSpec(memory_space=pl.ANY)
    vmem = pl.BlockSpec(memory_space=pltpu.VMEM)
    params = pltpu.CompilerParams(vmem_limit_bytes=VMEM_BYTES)
    dma = pltpu.SemaphoreType.DMA

    def array(*shape, dtype=BF16):
        return jax.ShapeDtypeStruct(shape, dtype)

    def scratch(*shape, dtype=BF16):
        return pltpu.VMEM(shape, dtype)

    across = cells // CELLS
    edge = REACH * across
    filter_args = (filters.transpose(1, 3, 2, 0), band_edges.T, basis_mask.T)
    *turns, lon_b = pl.pallas_call(
        prep_kernel,
        out_shape=(array(edge + 1, CELLS, channels),) * TURNS + (array(rows, CELLS, channels),),
        in_specs=[anywhere] * 5,
        out_specs=(anywhere,) * (TURNS + 1),
        scratch_shapes=[
            scratch(bases, filters.shape[3], BANDS, rows, dtype=F32),
            scratch(2, rows, dtype=jnp.int32), scratch(bases, rows, dtype=jnp.int32),
            scratch(TURNS, edge + 1, CELLS, channels), scratch(rows, CELLS, channels),
            scratch(bases, LANES, LANES, dtype=F32), scratch(2, CELLS, channels, dtype=F32),
            dma((7,)), dma((2 * TURNS + 1,)),
        ],
        compiler_params=pltpu.CompilerParams(vmem_limit_bytes=60 * 1024 * 1024),
        cost_estimate=pl.CostEstimate(flops=0, bytes_accessed=8 * REACH * cells * channels, transcendentals=0),
        name="prep",
    )(
        state_field.reshape(rows * across, CELLS, channels), state_field.reshape(rows, across, CELLS, channels),
        *filter_args,
    )
    both = ("lat", "lon")
    turns = [lax.ppermute(v, both, turn_swaps(lat_peers, lon_peers, j)) for j, v in enumerate(turns)]
    lon_b = lax.ppermute(lon_b, "lon", swaps(lon_peers, True))

    middle = rows - 2 * REACH
    flops = 2 * (2 * rows - 3 * REACH) * (cells - 2 * CELLS) * bases * DEPTH * channels
    cost = pl.CostEstimate(flops=flops, bytes_accessed=4 * state_field.size, transcendentals=0)
    toeplitz, known, wide, edge_rows, edge_cells, sides, begun = pl.pallas_call(
        functools.partial(inner_kernel, block),
        out_shape=(
            array(rows * group, DEPTH), array(2 * REACH * group, DEPTH), array(2 * REACH * group, DEPTH),
            array(2 * REACH, cells, channels), array(middle - REACH, TILE, channels),
            array(middle, TILE, channels), array(rows, cells, channels),
        ),
        in_specs=[vmem] * 6,
        out_specs=(vmem,) * 6 + (anywhere,),
        scratch_shapes=[
            scratch(middle, cells - 2 * TILE, channels), scratch(bases, LANES, LANES, dtype=F32),
            scratch(chunks, rows + REACH, cells, LANES, dtype=F32),
            scratch(chunks, rows + REACH, cells - CELLS, LANES, dtype=F32),
            scratch(chunks, middle, TILE, LANES, dtype=F32), dma((1,)),
        ],
        compiler_params=params,
        cost_estimate=cost,
        name="inner",
    )(state_field, *filter_args, weights_one, weights_two)

    *turns, sides = lax.optimization_barrier((*turns, sides))

    def corner_send(leading, second):
        parts = [jnp.where(leading, v[:edge:across], v[across - 1 : edge : across]) for v in turns]
        below = jnp.where(turn == 1, parts[0], jnp.where(turn == 2, parts[1], parts[2]))
        above = jnp.where(turn == 0, parts[0], jnp.where(turn == 1, parts[1], parts[2]))
        sent = jnp.concatenate([below, above], 0).reshape(2 * REACH * CELLS, channels)
        return lax.ppermute(sent, "lon", swaps(lon_peers, second))

    corner_b = corner_send(lon % 2 == 0, True)
    corner_a = corner_send(lon % 2 == 1, False)
    rim_toeplitz, rim_out, side_out, ends = pl.pallas_call(
        functools.partial(rim_kernel, block),
        out_shape=(
            array(2 * REACH * group, DEPTH), array(2 * REACH, cells, channels), array(2, middle, TILE, channels),
            array(2, 4 * REACH, WINDOW, channels),
        ),
        in_specs=[vmem] * 13,
        out_specs=(vmem,) * 4,
        scratch_shapes=[
            scratch(chunks, rows + 2 * REACH, cells + 2 * CELLS, LANES, dtype=F32),
            scratch(chunks, rows + REACH, cells + CELLS, LANES, dtype=F32),
        ],
        compiler_params=params,
        cost_estimate=cost,
        name="rim",
    )(
        state_field, *turns, lon_b, edge_rows, edge_cells, sides,
        toeplitz, known, wide, weights_one, weights_two,
    )
    return pl.pallas_call(
        corner_kernel,
        out_shape=array(rows, cells, channels),
        in_specs=[vmem] * 14 + [anywhere],
        out_specs=anywhere,
        input_output_aliases={14: 0},
        scratch_shapes=[scratch(2, 2 * REACH, TILE, channels), dma((8,))],
        compiler_params=params,
        cost_estimate=cost,
        name="corner",
    )(
        state_field, *turns, lon_b, corner_b, corner_a, ends, rim_toeplitz, wide,
        weights_one, weights_two, side_out, rim_out, begun,
    )


def solution(mesh):
    placed = (
        P("lat", "lon", None),
        P("lat", None, None, None),
        P("lat", None),
        P("lat", None),
        P(),
        P(),
    )
    return jax.shard_map(
        per_device, mesh=mesh, in_specs=placed, out_specs=P("lat", "lon", None), check_vma=False
    )
```

```python
import functools

import jax
import jax.numpy as jnp
from jax import lax
from jax.experimental import pallas as pl
from jax.experimental.pallas import tpu as pltpu
from jax.sharding import PartitionSpec as P

LAT_REACH = 2
LON_REACH = 4
REACH = 2 * LAT_REACH
BANDS = 2 * LAT_REACH + 1
CELLS = 8
WINDOW = CELLS + 2 * LON_REACH
LANES = 128
DEPTH = 2 * LANES
TILE = 16
VMEM_BYTES = 20 * 1024 * 1024
TURNS = 3
PIECE = 4
F32, BF16 = jnp.float32, jnp.bfloat16

ERF_SERIES = (
    1.5956562720156744,
    0.2917503271976864,
    -0.003995570947534282,
    -0.003914369984884403,
    0.0005729703632347449,
)


def erf_gelu(half):
    square = half * half
    series = ERF_SERIES[-1] * square + ERF_SERIES[-2]
    for term in ERF_SERIES[-3::-1]:
        series = series * square + term
    return half + half * jnp.tanh(half * series)


def swaps(peers, second):
    pairs = [(i, i + 1) for i in range(1 if second else 0, peers - 1, 2)]
    if second:
        pairs.append((peers - 1, 0))
    return pairs + [(j, i) for i, j in pairs]


def turn_swaps(peers, width, turn):
    pairs = [(i, i + 1) for i in range(peers - 1) if i % TURNS == turn]
    pairs += [(j, i) for i, j in pairs]
    alone = set(range(peers)) - {i for i, _ in pairs}
    result = [(i * width + k, j * width + k) for i, j in pairs for k in range(width)]
    return result + [(i * width + k, i * width + (k ^ 1)) for i in sorted(alone) for k in range(width)]


def pairs_of(items):
    return [items[i : i + 2] for i in range(0, len(items), 2)]


def lanes_of(chunk):
    return slice(chunk * LANES, (chunk + 1) * LANES)


def fill_toeplitz(toeplitz, line_of, rows, bases, place_of, pairs=None):
    group = bases * CELLS
    blank = jnp.zeros((CELLS, DEPTH - LANES), F32)
    for row in pairs or range(0, rows, 2):
        parts = []
        for r in (row, row + 1):
            for basis in range(bases):
                line = jnp.broadcast_to(line_of(r, basis), (CELLS, LANES))
                line = jnp.concatenate([line, blank], 1)
                parts.append(pltpu.roll(line, place_of(r) * WINDOW, 1, stride=1, stride_axis=0))
        toeplitz[row * group : (row + 2) * group, :] = jnp.concatenate(parts, 0).astype(BF16)


def lane_weights(ref, scale=1.0):
    bases, channels = ref.shape
    return [[ref[k : k + 1, lanes_of(c)] * scale for k in range(bases)] for c in range(channels // LANES)]


def product(matrix, low, high, windows, weights):
    wide = [w.astype(BF16).reshape(DEPTH, LANES) for w in windows]
    wide = jnp.concatenate(wide, 1)
    bases = len(weights[0])
    group = bases * CELLS
    scales = [jnp.concatenate([w[k] for w in weights], 1) for k in range(bases)]
    pieces = []
    for at in range(low, high, PIECE):
        to = min(at + PIECE, high)
        result = jnp.dot(matrix[at * group : to * group, :], wide, preferred_element_type=F32)
        result = result.reshape(to - at, bases, CELLS, len(windows) * LANES)
        total = result[:, 0] * scales[0]
        for k in range(1, bases):
            total = total + result[:, k] * scales[k]
        pieces.append(total)
    total = jnp.concatenate(pieces, 0) if len(pieces) > 1 else pieces[0]
    return [total[:, :, i * LANES : (i + 1) * LANES] for i in range(len(windows))]


def run_mixed(steps):
    waiting = []
    for first, second in steps:
        total, done = len(waiting), 0
        for i, unit in enumerate(first):
            unit()
            while done * len(first) < total * (i + 1):
                waiting.pop(0)()
                done += 1
        for unit in waiting:
            unit()
        waiting = list(second)
    for unit in waiting:
        unit()


def line_choice(lags):
    at = lax.broadcasted_iota(jnp.int32, (LANES, LANES), 0)
    lane = lax.broadcasted_iota(jnp.int32, (LANES, LANES), 1)
    chosen = (at // 8 == lane % WINDOW) & (at % 8 == lane // WINDOW) & (at % 8 < BANDS) & (at // 8 < lags)
    return jnp.where(chosen, 1.0, 0.0).astype(BF16)


def filter_lines(filter_ref, edge_ref, mask_ref, padded, chosen):
    bases, lags, bands, rows = filter_ref.shape
    source = lax.axis_index("lat") * rows + lax.broadcasted_iota(jnp.int32, (bands, rows), 1) - LAT_REACH
    source = source + lax.broadcasted_iota(jnp.int32, (bands, rows), 0)
    inside = (source >= edge_ref[0:1, :]) & (source < edge_ref[1:2, :])
    for k in range(bases):
        keep = inside & (mask_ref[k : k + 1, :] != 0)
        for m in range(lags):
            padded[k, m * 8 : m * 8 + bands, :rows] = jnp.where(keep, filter_ref[k, m], 0.0)
    return [jnp.dot(padded[k].T.astype(BF16), chosen, preferred_element_type=F32) for k in range(bases)]


def prep_kernel(
    flat_ref, groups_ref, filter_in, edge_in, mask_in, turn_0, turn_1, turn_2, lon_b, lines_ref,
    filter_ref, edge_ref, mask_ref, payloads, far, padded, tags, sems, out_sems,
):
    bases, lags, bands, rows = filter_in.shape
    across = groups_ref.shape[1]
    edge = REACH * across
    turn, lon_odd = lax.axis_index("lat") % TURNS, lax.axis_index("lon") % 2
    small = [
        pltpu.make_async_copy(filter_in, filter_ref, sems.at[0]),
        pltpu.make_async_copy(edge_in, edge_ref, sems.at[1]),
        pltpu.make_async_copy(mask_in, mask_ref, sems.at[2]),
    ]
    last, first = pl.ds((rows - REACH) * across, edge), pl.ds(0, edge)
    near_at, far_at = (1 - lon_odd) * (across - 1), lon_odd * (across - 1)
    copies = [
        pltpu.make_async_copy(flat_ref.at[last], payloads.at[0, pl.ds(0, edge)], sems.at[3]),
        pltpu.make_async_copy(flat_ref.at[first], payloads.at[1, pl.ds(0, edge)], sems.at[4]),
        pltpu.make_async_copy(groups_ref.at[:, near_at], payloads.at[2, pl.ds(0, rows)], sems.at[5]),
        pltpu.make_async_copy(groups_ref.at[:, far_at], far, sems.at[6]),
    ]
    for copy in copies[:2] + small + copies[2:]:
        copy.start()
    padded[...] = jnp.zeros_like(padded)
    tags[...] = jnp.zeros_like(tags)
    payloads[2, rows:] = jnp.zeros((edge + 1 - rows,) + payloads.shape[2:], BF16)
    chosen = line_choice(lags)
    pending = []

    def send(source, target):
        pending.append(pltpu.make_async_copy(source, target, out_sems.at[len(pending)]))
        pending[-1].start()

    outs = [(out, (turn + TURNS - j) % TURNS) for j, out in enumerate((turn_0, turn_1, turn_2))]
    for copy in copies[:3]:
        copy.wait()
    for out, role in outs:
        send(payloads.at[role, pl.ds(0, edge)], out.at[pl.ds(0, edge)])
    copies[3].wait()
    send(far, lon_b)
    for copy in small:
        copy.wait()
    for k, line in enumerate(filter_lines(filter_ref, edge_ref, mask_ref, padded, chosen)):
        lines_ref[k] = line[:rows]
        tags[0, :LAT_REACH, lanes_of(k)] = line[rows - LAT_REACH : rows]
        tags[1, :LAT_REACH, lanes_of(k)] = line[:LAT_REACH]
    payloads[0, edge] = tags[0].astype(BF16)
    payloads[1, edge] = tags[1].astype(BF16)
    for out, role in outs:
        send(payloads.at[role, edge], out.at[edge])
    for copy in pending:
        copy.wait()


def place_of(r):
    return r if r < REACH else REACH + r


def inner_kernel(
    block, x_ref, lines_ref, one_ref, two_ref,
    toeplitz, rim_toeplitz, wide_toeplitz, edge_rows, edge_cells, sides, out_ref,
    middle, field, hidden, ends, sems,
):
    rows, cells, channels = x_ref.shape
    bases = one_ref.shape[0]
    chunks = channels // LANES
    lines = [lines_ref[k] for k in range(bases)]
    fill_toeplitz(toeplitz, lambda r, k: lines[k][r : r + 1, :], rows, bases, lambda r: r % block)
    kept = list(range(REACH)) + list(range(rows - REACH, rows))
    fill_toeplitz(wide_toeplitz, lambda r, k: lines[k][kept[r] : kept[r] + 1, :], 2 * REACH, bases, place_of)
    shifted = [r - LAT_REACH for r in range(REACH)] + [rows - LAT_REACH + r for r in range(REACH)]
    own = range(LAT_REACH, 2 * REACH - LAT_REACH, 2)
    rim_toeplitz[...] = jnp.zeros_like(rim_toeplitz)
    fill_toeplitz(
        rim_toeplitz, lambda r, k: lines[k][shifted[r] : shifted[r] + 1, :], 2 * REACH, bases, place_of, own
    )
    one, two = lane_weights(one_ref, 0.5), lane_weights(two_ref)
    starts = range(0, rows, block)
    windows = (cells - WINDOW) // CELLS + 1
    span = windows * CELLS

    def load(c):
        blank = jnp.zeros((LAT_REACH, cells, LANES), F32)
        field[c, :LAT_REACH] = blank
        field[c, LAT_REACH : LAT_REACH + rows] = x_ref[:, :, lanes_of(c)].astype(F32)
        field[c, LAT_REACH + rows :] = blank
        blank = jnp.zeros((REACH, span, LANES), F32)
        hidden[c, :REACH] = blank
        hidden[c, rows:] = blank

    def first(items, start):
        low, high = max(start, LAT_REACH), min(start + block, rows - LAT_REACH)
        tall = [field[c, start : start + block + REACH, w * CELLS : w * CELLS + WINDOW] for c, w in items]
        values = product(toeplitz, low, high, tall, [one[c] for c, w in items])
        for (c, w), value in zip(items, values):
            hidden[c, low + LAT_REACH : high + LAT_REACH, w * CELLS : (w + 1) * CELLS] = erf_gelu(value)

    def second(c, start, pair):
        low, high = max(start, REACH), min(start + block, rows - REACH)
        tall = [hidden[c, start : start + block + REACH, w * CELLS : w * CELLS + WINDOW] for w in pair]
        values = product(toeplitz, low, high, tall, [two[c]] * len(pair))
        at = slice(low - REACH, high - REACH)
        for w, value in zip(pair, values):
            if w in (0, windows - 2):
                ends[c, at, (w > 0) * CELLS : (w > 0) * CELLS + CELLS] = value
        if len(pair) == 2 and pair[0] > 0:
            span = slice((pair[0] - 1) * CELLS, (pair[0] + 1) * CELLS)
            middle[at, span, lanes_of(c)] = jnp.concatenate(values, 1).astype(BF16)

    def export(c):
        for i, row in enumerate((REACH, rows - REACH)):
            part = jnp.concatenate([hidden[c, row : row + REACH], jnp.zeros((REACH, cells - span, LANES), F32)], 1)
            edge_rows[i * REACH : (i + 1) * REACH, :, lanes_of(c)] = part.astype(BF16)
        part = hidden[c, 2 * REACH : rows - REACH]
        edge_cells[:, :, lanes_of(c)] = jnp.concatenate([part[:, :CELLS], part[:, span - CELLS :]], 1).astype(BF16)
        sides[:, :, lanes_of(c)] = ends[c].astype(BF16)

    part = functools.partial
    steps = [([part(load, c)], []) for c in range(chunks)]
    for items in pairs_of([(c, w) for c in range(chunks) for w in range(windows)]):
        steps[items[-1][0]][0].extend(part(first, items, start) for start in starts)
    for c in range(chunks):
        pairs = [[0, windows - 2]] + pairs_of(list(range(1, windows - 2)))
        steps[c][1].extend(part(second, c, start, pair) for start in starts for pair in pairs)
        steps[c][1].append(part(export, c))
    for c in range(chunks - 1, 0, -1):
        if c * windows % 2:
            straddle = steps[c][0][1 : 1 + len(starts)]
            steps[c][0][1 : 1 + len(starts)] = []
            steps[c - 1][0].extend([steps[c][0].pop(0)] + straddle)
    run_mixed(steps)
    target = out_ref.at[pl.ds(REACH, rows - 2 * REACH), pl.ds(TILE, cells - 2 * TILE)]
    copy = pltpu.make_async_copy(middle, target, sems.at[0])
    copy.start()
    copy.wait()


def ordered(odd, a, b):
    return jnp.where(odd, a, b).astype(F32), jnp.where(odd, b, a).astype(F32)


def pick(received, turn):
    value = received[-1]
    for j in range(TURNS - 1):
        value = jnp.where(turn == j, received[j], value)
    return value


def below_and_above(received):
    turn = lax.axis_index("lat") % TURNS
    return pick(received, (turn + TURNS - 1) % TURNS).astype(F32), pick(received, turn).astype(F32)


def in_chip(received):
    return pick(received, (lax.axis_index("lat") + 1) % TURNS)


def rim_kernel(
    block, x_ref, turn_0, turn_1, turn_2, lon_b, rows_in, cells_in, sides_in,
    toeplitz, known_toeplitz, wide_toeplitz, one_ref, two_ref,
    rim_toeplitz, rim_out, side_out, ends, field, hidden,
):
    rows, cells, channels = x_ref.shape
    bases = one_ref.shape[0]
    chunks = channels // LANES
    group = bases * CELLS
    edge = REACH * (cells // CELLS)
    columns = cells // CELLS + 1
    turns, lon_odd = (turn_0, turn_1, turn_2), lax.axis_index("lon") % 2 == 1
    one, two = lane_weights(one_ref, 0.5), lane_weights(two_ref)
    tags = below_and_above([v[edge] for v in turns])

    def tag_line(r, k):
        at = r % LAT_REACH
        return tags[0 if r < REACH else 1][at : at + 1, lanes_of(k)]

    own = slice(LAT_REACH * group, (2 * REACH - LAT_REACH) * group)
    rim_toeplitz[own, :] = known_toeplitz[own, :]
    fill_toeplitz(rim_toeplitz, tag_line, 2 * REACH, bases, place_of, (0, 2 * REACH - LAT_REACH))

    def load(c):
        lanes = lanes_of(c)
        lat = below_and_above([v[:edge, :, lanes] for v in turns])
        lon = ordered(lon_odd, in_chip([v[:rows, :, lanes] for v in turns]), lon_b[:, :, lanes])
        inner = slice(REACH, rows - REACH)
        blank = jnp.zeros((REACH, CELLS, LANES), F32)
        for side in range(2):
            at = slice(side * (rows + REACH), side * (rows + REACH) + REACH)
            field[c, at, CELLS : CELLS + cells] = lat[side].reshape(REACH, cells, LANES)
            own = slice(side * (rows - REACH), side * (rows - REACH) + REACH)
            at = slice(own.start + REACH, own.stop + REACH)
            field[c, at, CELLS : CELLS + cells] = x_ref[own, :, lanes].astype(F32)
            own = slice(side * (cells - TILE), side * (cells - TILE) + TILE)
            at = slice(own.start + CELLS, own.stop + CELLS)
            field[c, 2 * REACH : rows, at] = x_ref[inner, own, lanes].astype(F32)
            span = slice(side * (CELLS + cells), side * (CELLS + cells) + CELLS)
            field[c, REACH : REACH + rows, span] = lon[side]
            for end in range(2):
                at = slice(end * (rows + REACH), end * (rows + REACH) + REACH)
                field[c, at, span] = blank
                hidden[c, end * rows : end * rows + REACH, side * cells : side * cells + CELLS] = blank
        span = cells - CELLS
        for i, at in enumerate((REACH, rows - REACH)):
            part = rows_in[i * REACH : (i + 1) * REACH, :, lanes].astype(F32)
            hidden[c, at : at + REACH, CELLS : CELLS + span] = part[:, :span]
        part = cells_in[:, :, lanes].astype(F32)
        at = slice(2 * REACH, rows - REACH)
        hidden[c, at, CELLS : 2 * CELLS] = part[:, :CELLS]
        hidden[c, at, cells - CELLS : cells] = part[:, CELLS:]

    def rims(ref, c, span):
        last = ref.shape[1] - 2 * REACH
        return jnp.concatenate([ref[c, : 2 * REACH, span], ref[c, last:, span]], 0)

    def first_rows(items):
        tall = [rims(field, c, slice(w * CELLS, w * CELLS + WINDOW)) for c, w in items]
        values = product(rim_toeplitz, 0, 2 * REACH, tall, [one[c] for c, w in items])
        for (c, w), value in zip(items, values):
            value = erf_gelu(value)
            hidden[c, :REACH, w * CELLS : (w + 1) * CELLS] = value[:REACH]
            hidden[c, rows:, w * CELLS : (w + 1) * CELLS] = value[REACH:]

    def first_sides(c, start):
        low, high = max(start, LAT_REACH), min(start + block, rows - LAT_REACH)
        at = slice(start + LAT_REACH, start + LAT_REACH + block + REACH)
        tall = [field[c, at, s : s + WINDOW] for s in (0, cells)]
        values = product(toeplitz, low, high, tall, [one[c]] * 2)
        for s, value in zip((0, cells), values):
            hidden[c, low + LAT_REACH : high + LAT_REACH, s : s + CELLS] = erf_gelu(value)

    def second_rows(c, pair):
        tall = [rims(hidden, c, slice(w * CELLS, w * CELLS + WINDOW)) for w in pair]
        values = product(wide_toeplitz, 0, 2 * REACH, tall, [two[c]] * 2)
        blank = jnp.zeros((2 * REACH, CELLS, LANES), F32)
        if pair == [1, columns - 3]:
            rim_out[:, :TILE, lanes_of(c)] = jnp.concatenate([blank, values[0]], 1).astype(BF16)
            rim_out[:, cells - TILE :, lanes_of(c)] = jnp.concatenate([values[1], blank], 1).astype(BF16)
        else:
            rim_out[:, pair[0] * CELLS : (pair[0] + 2) * CELLS, lanes_of(c)] = jnp.concatenate(values, 1).astype(BF16)

    def second_sides(c, start):
        low, high = max(start, REACH), min(start + block, rows - REACH)
        tall = [hidden[c, start : start + block + REACH, s : s + WINDOW] for s in (0, cells - CELLS)]
        values = product(toeplitz, low, high, tall, [two[c]] * 2)
        at = slice(low - REACH, high - REACH)
        inner = sides_in[at, :, lanes_of(c)].astype(F32)
        side_out[0, at, :, lanes_of(c)] = jnp.concatenate([values[0], inner[:, :CELLS]], 1).astype(BF16)
        side_out[1, at, :, lanes_of(c)] = jnp.concatenate([inner[:, CELLS:], values[1]], 1).astype(BF16)

    def export(c):
        for side in range(2):
            span = slice(side * (cells - CELLS), side * (cells - CELLS) + WINDOW)
            ends[side, :, :, lanes_of(c)] = rims(hidden, c, span).astype(BF16)

    part = functools.partial
    steps = [([part(load, c)], []) for c in range(chunks)]
    items = [(c, w) for c in range(chunks) for w in range(1, columns - 1)]
    for pair in pairs_of(items):
        steps[pair[-1][0]][0].append(part(first_rows, pair))
    for c in range(chunks - 1, 0, -1):
        if c * (columns - 2) % 2:
            steps[c - 1][0].extend([steps[c][0].pop(0), steps[c][0].pop(0)])
    starts = range(0, rows, block)
    for c, (first, second) in enumerate(steps):
        first.extend(part(first_sides, c, start) for start in starts)
        second.extend(
            part(second_rows, c, pair) for pair in [[1, columns - 3]] + pairs_of(list(range(2, columns - 3)))
        )
        second.extend(part(second_sides, c, start) for start in starts)
        second.append(part(export, c))
    run_mixed(steps)


def corner_kernel(
    x_ref, turn_0, turn_1, turn_2, lon_b, corner_b, corner_a, ends, rim_toeplitz, wide_toeplitz, one_ref, two_ref,
    side_out, rim_out, begun_ref, out_ref, corner_out, sems,
):
    del begun_ref
    rows, cells, channels = x_ref.shape
    chunks = channels // LANES
    edge = REACH * (cells // CELLS)
    inner = pl.ds(REACH, rows - 2 * REACH)
    ends_at = (pl.ds(0, REACH), pl.ds(rows - REACH, REACH))
    sides_at = (pl.ds(0, TILE), pl.ds(cells - TILE, TILE))
    span = pl.ds(TILE, cells - 2 * TILE)
    moves = []
    for i in range(2):
        moves.append((side_out.at[i], out_ref.at[inner, sides_at[i]]))
        moves.append((rim_out.at[pl.ds(i * REACH, REACH), span], out_ref.at[ends_at[i], span]))
    copies = [pltpu.make_async_copy(source, target, sems.at[i]) for i, (source, target) in enumerate(moves)]
    for copy in copies:
        copy.start()
    turns, lon_odd = (turn_0, turn_1, turn_2), lax.axis_index("lon") % 2 == 1
    one, two = lane_weights(one_ref, 0.5), lane_weights(two_ref)

    def first(c):
        lanes = lanes_of(c)
        lat = below_and_above([v[:edge, :, lanes] for v in turns])
        lon = ordered(lon_odd, in_chip([v[:rows, :, lanes] for v in turns]), lon_b[:, :, lanes])
        corner = ordered(lon_odd, corner_a[:, lanes], corner_b[:, lanes])
        tall = []
        for side in range(2):
            own = slice(side * (cells - CELLS), side * (cells - CELLS) + CELLS)
            above = [v.reshape(REACH, cells, LANES)[:, own] for v in lat]
            tiles = slice(side * (cells - TILE), side * (cells - TILE) + TILE)
            half = slice(side * (TILE - CELLS), side * (TILE - CELLS) + CELLS)
            mine = [x_ref[r : r + REACH, tiles, lanes].astype(F32)[:, half] for r in (0, rows - REACH)]
            near = lon[side]
            far = corner[side].reshape(2, REACH, CELLS, LANES)
            own = jnp.concatenate([above[0], mine[0], mine[1], above[1]], 0)
            other = jnp.concatenate([far[0], near[:REACH], near[rows - REACH :], far[1]], 0)
            tall.append(jnp.concatenate([own, other] if side else [other, own], 1))
        return [erf_gelu(v) for v in product(rim_toeplitz, 0, 2 * REACH, tall, [one[c]] * 2)]

    def second(c, blocks):
        lanes = lanes_of(c)
        tall = []
        for side in range(2):
            near = ends[side, :, :, lanes].astype(F32)
            own = near[:, side * CELLS : side * CELLS + CELLS]
            own = jnp.concatenate([blocks[side][:REACH], own[REACH : 3 * REACH], blocks[side][REACH:]], 0)
            tall.append(jnp.concatenate([near[:, :CELLS], own] if side else [own, near[:, CELLS:]], 1))
        values = product(wide_toeplitz, 0, 2 * REACH, tall, [two[c]] * 2)
        for side in range(2):
            tiles = slice(side * (cells - TILE), side * (cells - TILE) + TILE)
            near = rim_out[:, tiles, lanes].astype(F32)
            near = near[:, : TILE - CELLS] if side else near[:, CELLS:]
            whole = [near, values[side]] if side else [values[side], near]
            corner_out[side, :, :, lanes] = jnp.concatenate(whole, 1).astype(BF16)

    hidden = [first(c) for c in range(chunks)]
    for c in range(chunks):
        second(c, hidden[c])
    last = []
    for side in range(2):
        for end in range(2):
            source = corner_out.at[side, pl.ds(end * REACH, REACH)]
            target = out_ref.at[ends_at[end], sides_at[side]]
            last.append(pltpu.make_async_copy(source, target, sems.at[len(copies) + len(last)]))
            last[-1].start()
    for copy in copies + last:
        copy.wait()


def per_device(state_field, filters, band_edges, basis_mask, weights_one, weights_two):
    rows, cells, channels = state_field.shape
    bases = filters.shape[1]
    group = bases * CELLS
    chunks = channels // LANES
    block = max(b for b in range(2, rows + 1, 2) if rows % b == 0 and (b + REACH) * WINDOW <= DEPTH)
    lat_peers, lon_peers = lax.axis_size("lat"), lax.axis_size("lon")
    turn, lon = lax.axis_index("lat") % TURNS, lax.axis_index("lon")

    anywhere = pl.BlockSpec(memory_space=pl.ANY)
    vmem = pl.BlockSpec(memory_space=pltpu.VMEM)
    params = pltpu.CompilerParams(vmem_limit_bytes=VMEM_BYTES)
    dma = pltpu.SemaphoreType.DMA

    def array(*shape, dtype=BF16):
        return jax.ShapeDtypeStruct(shape, dtype)

    def scratch(*shape, dtype=BF16):
        return pltpu.VMEM(shape, dtype)

    across = cells // CELLS
    edge = REACH * across
    filter_args = (filters.transpose(1, 3, 2, 0), band_edges.T, basis_mask.T)
    *turns, lon_b, lines = pl.pallas_call(
        prep_kernel,
        out_shape=(array(edge + 1, CELLS, channels),) * TURNS
        + (array(rows, CELLS, channels), scratch(bases, rows, LANES, dtype=F32)),
        in_specs=[anywhere] * 5,
        out_specs=(anywhere,) * (TURNS + 1) + (vmem,),
        scratch_shapes=[
            scratch(bases, filters.shape[3], BANDS, rows, dtype=F32),
            scratch(2, rows, dtype=jnp.int32), scratch(bases, rows, dtype=jnp.int32),
            scratch(TURNS, edge + 1, CELLS, channels), scratch(rows, CELLS, channels),
            scratch(bases, LANES, LANES, dtype=F32), scratch(2, CELLS, channels, dtype=F32),
            dma((7,)), dma((2 * TURNS + 1,)),
        ],
        compiler_params=pltpu.CompilerParams(vmem_limit_bytes=60 * 1024 * 1024),
        cost_estimate=pl.CostEstimate(flops=0, bytes_accessed=8 * REACH * cells * channels, transcendentals=0),
        name="prep",
    )(
        state_field.reshape(rows * across, CELLS, channels), state_field.reshape(rows, across, CELLS, channels),
        *filter_args,
    )
    both = ("lat", "lon")
    turns = [lax.ppermute(v, both, turn_swaps(lat_peers, lon_peers, j)) for j, v in enumerate(turns)]
    lon_b = lax.ppermute(lon_b, "lon", swaps(lon_peers, True))

    middle = rows - 2 * REACH
    flops = 2 * (2 * rows - 3 * REACH) * (cells - 2 * CELLS) * bases * DEPTH * channels
    cost = pl.CostEstimate(flops=flops, bytes_accessed=4 * state_field.size, transcendentals=0)
    toeplitz, known, wide, edge_rows, edge_cells, sides, begun = pl.pallas_call(
        functools.partial(inner_kernel, block),
        out_shape=(
            array(rows * group, DEPTH), array(2 * REACH * group, DEPTH), array(2 * REACH * group, DEPTH),
            array(2 * REACH, cells, channels), array(middle - REACH, TILE, channels),
            array(middle, TILE, channels), array(rows, cells, channels),
        ),
        in_specs=[vmem] * 4,
        out_specs=(vmem,) * 6 + (anywhere,),
        scratch_shapes=[
            scratch(middle, cells - 2 * TILE, channels),
            scratch(chunks, rows + REACH, cells, LANES, dtype=F32),
            scratch(chunks, rows + REACH, cells - CELLS, LANES, dtype=F32),
            scratch(chunks, middle, TILE, LANES, dtype=F32), dma((1,)),
        ],
        compiler_params=params,
        cost_estimate=cost,
        name="inner",
    )(state_field, lines, weights_one, weights_two)

    *turns, sides = lax.optimization_barrier((*turns, sides))

    def corner_send(leading, second):
        parts = [jnp.where(leading, v[:edge:across], v[across - 1 : edge : across]) for v in turns]
        below = jnp.where(turn == 1, parts[0], jnp.where(turn == 2, parts[1], parts[2]))
        above = jnp.where(turn == 0, parts[0], jnp.where(turn == 1, parts[1], parts[2]))
        sent = jnp.concatenate([below, above], 0).reshape(2 * REACH * CELLS, channels)
        return lax.ppermute(sent, "lon", swaps(lon_peers, second))

    corner_b = corner_send(lon % 2 == 0, True)
    corner_a = corner_send(lon % 2 == 1, False)
    rim_toeplitz, rim_out, side_out, ends = pl.pallas_call(
        functools.partial(rim_kernel, block),
        out_shape=(
            array(2 * REACH * group, DEPTH), array(2 * REACH, cells, channels), array(2, middle, TILE, channels),
            array(2, 4 * REACH, WINDOW, channels),
        ),
        in_specs=[vmem] * 13,
        out_specs=(vmem,) * 4,
        scratch_shapes=[
            scratch(chunks, rows + 2 * REACH, cells + 2 * CELLS, LANES, dtype=F32),
            scratch(chunks, rows + REACH, cells + CELLS, LANES, dtype=F32),
        ],
        compiler_params=params,
        cost_estimate=cost,
        name="rim",
    )(
        state_field, *turns, lon_b, edge_rows, edge_cells, sides,
        toeplitz, known, wide, weights_one, weights_two,
    )
    return pl.pallas_call(
        corner_kernel,
        out_shape=array(rows, cells, channels),
        in_specs=[vmem] * 14 + [anywhere],
        out_specs=anywhere,
        input_output_aliases={14: 0},
        scratch_shapes=[scratch(2, 2 * REACH, TILE, channels), dma((8,))],
        compiler_params=params,
        cost_estimate=cost,
        name="corner",
    )(
        state_field, *turns, lon_b, corner_b, corner_a, ends, rim_toeplitz, wide,
        weights_one, weights_two, side_out, rim_out, begun,
    )


def solution(mesh):
    placed = (
        P("lat", "lon", None),
        P("lat", None, None, None),
        P("lat", None),
        P("lat", None),
        P(),
        P(),
    )
    return jax.shard_map(
        per_device, mesh=mesh, in_specs=placed, out_specs=P("lat", "lon", None), check_vma=False
    )
```

```python
import functools

import jax
import jax.numpy as jnp
from jax import lax
from jax.experimental import pallas as pl
from jax.experimental.pallas import tpu as pltpu
from jax.sharding import PartitionSpec as P

LAT_REACH = 2
LON_REACH = 4
REACH = 2 * LAT_REACH
BANDS = 2 * LAT_REACH + 1
CELLS = 8
WINDOW = CELLS + 2 * LON_REACH
LANES = 128
DEPTH = 2 * LANES
TILE = 16
VMEM_BYTES = 20 * 1024 * 1024
TURNS = 3
PIECE = 4
F32, BF16 = jnp.float32, jnp.bfloat16

ERF_SERIES = (
    1.5956562720156744,
    0.2917503271976864,
    -0.003995570947534282,
    -0.003914369984884403,
    0.0005729703632347449,
)


def erf_gelu(half):
    square = half * half
    series = ERF_SERIES[-1] * square + ERF_SERIES[-2]
    for term in ERF_SERIES[-3::-1]:
        series = series * square + term
    return half + half * jnp.tanh(half * series)


def swaps(peers, second):
    pairs = [(i, i + 1) for i in range(1 if second else 0, peers - 1, 2)]
    if second:
        pairs.append((peers - 1, 0))
    return pairs + [(j, i) for i, j in pairs]


def turn_swaps(peers, width, turn):
    pairs = [(i, i + 1) for i in range(peers - 1) if i % TURNS == turn]
    pairs += [(j, i) for i, j in pairs]
    alone = set(range(peers)) - {i for i, _ in pairs}
    result = [(i * width + k, j * width + k) for i, j in pairs for k in range(width)]
    return result + [(i * width + k, i * width + (k ^ 1)) for i in sorted(alone) for k in range(width)]


def pairs_of(items):
    return [items[i : i + 2] for i in range(0, len(items), 2)]


def lanes_of(chunk):
    return slice(chunk * LANES, (chunk + 1) * LANES)


def fill_toeplitz(toeplitz, line_of, rows, bases, place_of, pairs=None):
    group = bases * CELLS
    blank = jnp.zeros((CELLS, DEPTH - LANES), F32)
    for row in pairs or range(0, rows, 2):
        parts = []
        for r in (row, row + 1):
            for basis in range(bases):
                line = jnp.broadcast_to(line_of(r, basis), (CELLS, LANES))
                line = jnp.concatenate([line, blank], 1)
                parts.append(pltpu.roll(line, place_of(r) * WINDOW, 1, stride=1, stride_axis=0))
        toeplitz[row * group : (row + 2) * group, :] = jnp.concatenate(parts, 0).astype(BF16)


def lane_weights(ref, scale=1.0):
    bases, channels = ref.shape
    return [[ref[k : k + 1, lanes_of(c)] * scale for k in range(bases)] for c in range(channels // LANES)]


def product(matrix, low, high, windows, weights):
    wide = [w.astype(BF16).reshape(DEPTH, LANES) for w in windows]
    wide = jnp.concatenate(wide, 1)
    bases = len(weights[0])
    group = bases * CELLS
    scales = [jnp.concatenate([w[k] for w in weights], 1) for k in range(bases)]
    pieces = []
    for at in range(low, high, PIECE):
        to = min(at + PIECE, high)
        result = jnp.dot(matrix[at * group : to * group, :], wide, preferred_element_type=F32)
        result = result.reshape(to - at, bases, CELLS, len(windows) * LANES)
        total = result[:, 0] * scales[0]
        for k in range(1, bases):
            total = total + result[:, k] * scales[k]
        pieces.append(total)
    total = jnp.concatenate(pieces, 0) if len(pieces) > 1 else pieces[0]
    return [total[:, :, i * LANES : (i + 1) * LANES] for i in range(len(windows))]


def run_mixed(steps):
    waiting = []
    for first, second in steps:
        total, done = len(waiting), 0
        for i, unit in enumerate(first):
            unit()
            while done * len(first) < total * (i + 1):
                waiting.pop(0)()
                done += 1
        for unit in waiting:
            unit()
        waiting = list(second)
    for unit in waiting:
        unit()


def line_choice(lags):
    at = lax.broadcasted_iota(jnp.int32, (LANES, LANES), 0)
    lane = lax.broadcasted_iota(jnp.int32, (LANES, LANES), 1)
    chosen = (at // 8 == lane % WINDOW) & (at % 8 == lane // WINDOW) & (at % 8 < BANDS) & (at // 8 < lags)
    return jnp.where(chosen, 1.0, 0.0).astype(BF16)


def filter_lines(filter_ref, edge_ref, mask_ref, padded, chosen):
    bases, lags, bands, rows = filter_ref.shape
    source = lax.axis_index("lat") * rows + lax.broadcasted_iota(jnp.int32, (bands, rows), 1) - LAT_REACH
    source = source + lax.broadcasted_iota(jnp.int32, (bands, rows), 0)
    inside = (source >= edge_ref[0:1, :]) & (source < edge_ref[1:2, :])
    for k in range(bases):
        keep = inside & (mask_ref[k : k + 1, :] != 0)
        for m in range(lags):
            padded[k, m * 8 : m * 8 + bands, :rows] = jnp.where(keep, filter_ref[k, m], 0.0)
    return [jnp.dot(padded[k].T.astype(BF16), chosen, preferred_element_type=F32) for k in range(bases)]


def prep_kernel(
    flat_ref, groups_ref, filter_in, edge_in, mask_in, turn_0, turn_1, turn_2, lon_b, lines_ref,
    filter_ref, edge_ref, mask_ref, payloads, far, padded, tags, sems, out_sems,
):
    bases, lags, bands, rows = filter_in.shape
    across = groups_ref.shape[1]
    edge = REACH * across
    turn, lon_odd = lax.axis_index("lat") % TURNS, lax.axis_index("lon") % 2
    small = [
        pltpu.make_async_copy(filter_in, filter_ref, sems.at[0]),
        pltpu.make_async_copy(edge_in, edge_ref, sems.at[1]),
        pltpu.make_async_copy(mask_in, mask_ref, sems.at[2]),
    ]
    last, first = pl.ds((rows - REACH) * across, edge), pl.ds(0, edge)
    near_at, far_at = (1 - lon_odd) * (across - 1), lon_odd * (across - 1)
    copies = [
        pltpu.make_async_copy(flat_ref.at[last], payloads.at[0, pl.ds(0, edge)], sems.at[3]),
        pltpu.make_async_copy(flat_ref.at[first], payloads.at[1, pl.ds(0, edge)], sems.at[4]),
        pltpu.make_async_copy(groups_ref.at[:, near_at], payloads.at[2, pl.ds(0, rows)], sems.at[5]),
        pltpu.make_async_copy(groups_ref.at[:, far_at], far, sems.at[6]),
    ]
    for copy in copies[:2] + small + copies[2:]:
        copy.start()
    padded[...] = jnp.zeros_like(padded)
    tags[...] = jnp.zeros_like(tags)
    payloads[2, rows:] = jnp.zeros((edge + 1 - rows,) + payloads.shape[2:], BF16)
    chosen = line_choice(lags)
    pending = []

    def send(source, target):
        pending.append(pltpu.make_async_copy(source, target, out_sems.at[len(pending)]))
        pending[-1].start()

    outs = [(out, (turn + TURNS - j) % TURNS) for j, out in enumerate((turn_0, turn_1, turn_2))]
    for copy in copies[:3]:
        copy.wait()
    for out, role in outs:
        send(payloads.at[role, pl.ds(0, edge)], out.at[pl.ds(0, edge)])
    copies[3].wait()
    send(far, lon_b)
    for copy in small:
        copy.wait()
    for k, line in enumerate(filter_lines(filter_ref, edge_ref, mask_ref, padded, chosen)):
        lines_ref[k] = line[:rows]
        tags[0, :LAT_REACH, lanes_of(k)] = line[rows - LAT_REACH : rows]
        tags[1, :LAT_REACH, lanes_of(k)] = line[:LAT_REACH]
    payloads[0, edge] = tags[0].astype(BF16)
    payloads[1, edge] = tags[1].astype(BF16)
    for out, role in outs:
        send(payloads.at[role, edge], out.at[edge])
    for copy in pending:
        copy.wait()


def place_of(r):
    return r if r < REACH else REACH + r


def inner_kernel(
    block, x_ref, lines_ref, one_ref, two_ref,
    toeplitz, rim_toeplitz, wide_toeplitz, edge_rows, edge_cells, sides, out_ref,
    middle, field, hidden, ends, sems,
):
    rows, cells, channels = x_ref.shape
    bases = one_ref.shape[0]
    chunks = channels // LANES
    lines = [lines_ref[k] for k in range(bases)]
    fill_toeplitz(toeplitz, lambda r, k: lines[k][r : r + 1, :], rows, bases, lambda r: r % block)
    kept = list(range(REACH)) + list(range(rows - REACH, rows))
    fill_toeplitz(wide_toeplitz, lambda r, k: lines[k][kept[r] : kept[r] + 1, :], 2 * REACH, bases, place_of)
    shifted = [r - LAT_REACH for r in range(REACH)] + [rows - LAT_REACH + r for r in range(REACH)]
    own = range(LAT_REACH, 2 * REACH - LAT_REACH, 2)
    rim_toeplitz[...] = jnp.zeros_like(rim_toeplitz)
    fill_toeplitz(
        rim_toeplitz, lambda r, k: lines[k][shifted[r] : shifted[r] + 1, :], 2 * REACH, bases, place_of, own
    )
    one, two = lane_weights(one_ref, 0.5), lane_weights(two_ref)
    starts = range(0, rows, block)
    windows = (cells - WINDOW) // CELLS + 1
    span = windows * CELLS

    def load(c):
        blank = jnp.zeros((LAT_REACH, cells, LANES), F32)
        field[c, :LAT_REACH] = blank
        field[c, LAT_REACH : LAT_REACH + rows] = x_ref[:, :, lanes_of(c)].astype(F32)
        field[c, LAT_REACH + rows :] = blank
        blank = jnp.zeros((REACH, span, LANES), F32)
        hidden[c, :REACH] = blank
        hidden[c, rows:] = blank

    def first(items, start):
        low, high = max(start, LAT_REACH), min(start + block, rows - LAT_REACH)
        tall = [field[c, start : start + block + REACH, w * CELLS : w * CELLS + WINDOW] for c, w in items]
        values = product(toeplitz, low, high, tall, [one[c] for c, w in items])
        for (c, w), value in zip(items, values):
            hidden[c, low + LAT_REACH : high + LAT_REACH, w * CELLS : (w + 1) * CELLS] = erf_gelu(value)

    def second(c, start, pair):
        low, high = max(start, REACH), min(start + block, rows - REACH)
        tall = [hidden[c, start : start + block + REACH, w * CELLS : w * CELLS + WINDOW] for w in pair]
        values = product(toeplitz, low, high, tall, [two[c]] * len(pair))
        at = slice(low - REACH, high - REACH)
        for w, value in zip(pair, values):
            if w in (0, windows - 2):
                ends[c, at, (w > 0) * CELLS : (w > 0) * CELLS + CELLS] = value
        if len(pair) == 2 and pair[0] > 0:
            span = slice((pair[0] - 1) * CELLS, (pair[0] + 1) * CELLS)
            middle[at, span, lanes_of(c)] = jnp.concatenate(values, 1).astype(BF16)

    def export(c):
        for i, row in enumerate((REACH, rows - REACH)):
            part = jnp.concatenate([hidden[c, row : row + REACH], jnp.zeros((REACH, cells - span, LANES), F32)], 1)
            edge_rows[i * REACH : (i + 1) * REACH, :, lanes_of(c)] = part.astype(BF16)
        part = hidden[c, 2 * REACH : rows - REACH]
        edge_cells[:, :, lanes_of(c)] = jnp.concatenate([part[:, :CELLS], part[:, span - CELLS :]], 1).astype(BF16)
        sides[:, :, lanes_of(c)] = ends[c].astype(BF16)

    part = functools.partial
    steps = [([part(load, c)], []) for c in range(chunks)]
    for items in pairs_of([(c, w) for c in range(chunks) for w in range(windows)]):
        steps[items[-1][0]][0].extend(part(first, items, start) for start in starts)
    for c in range(chunks):
        pairs = [[0, windows - 2]] + pairs_of(list(range(1, windows - 2)))
        steps[c][1].extend(part(second, c, start, pair) for start in starts for pair in pairs)
        steps[c][1].append(part(export, c))
    for c in range(chunks - 1, 0, -1):
        if c * windows % 2:
            straddle = steps[c][0][1 : 1 + len(starts)]
            steps[c][0][1 : 1 + len(starts)] = []
            steps[c - 1][0].extend([steps[c][0].pop(0)] + straddle)
    run_mixed(steps)
    target = out_ref.at[pl.ds(REACH, rows - 2 * REACH), pl.ds(TILE, cells - 2 * TILE)]
    copy = pltpu.make_async_copy(middle, target, sems.at[0])
    copy.start()
    copy.wait()


def ordered(odd, a, b):
    return jnp.where(odd, a, b).astype(F32), jnp.where(odd, b, a).astype(F32)


def pick(received, turn):
    value = received[-1]
    for j in range(TURNS - 1):
        value = jnp.where(turn == j, received[j], value)
    return value


def below_and_above(received):
    turn = lax.axis_index("lat") % TURNS
    return pick(received, (turn + TURNS - 1) % TURNS).astype(F32), pick(received, turn).astype(F32)


def in_chip(received):
    return pick(received, (lax.axis_index("lat") + 1) % TURNS)


def rim_kernel(
    block, x_ref, turn_0, turn_1, turn_2, lon_b, rows_in, cells_in, sides_in,
    toeplitz, known_toeplitz, wide_toeplitz, one_ref, two_ref,
    rim_toeplitz, rim_out, side_out, ends, field, hidden,
):
    rows, cells, channels = x_ref.shape
    bases = one_ref.shape[0]
    chunks = channels // LANES
    group = bases * CELLS
    edge = REACH * (cells // CELLS)
    columns = cells // CELLS + 1
    turns, lon_odd = (turn_0, turn_1, turn_2), lax.axis_index("lon") % 2 == 1
    one, two = lane_weights(one_ref, 0.5), lane_weights(two_ref)
    tags = below_and_above([v[edge] for v in turns])

    def tag_line(r, k):
        at = r % LAT_REACH
        return tags[0 if r < REACH else 1][at : at + 1, lanes_of(k)]

    own = slice(LAT_REACH * group, (2 * REACH - LAT_REACH) * group)
    rim_toeplitz[own, :] = known_toeplitz[own, :]
    fill_toeplitz(rim_toeplitz, tag_line, 2 * REACH, bases, place_of, (0, 2 * REACH - LAT_REACH))

    def load(c):
        lanes = lanes_of(c)
        lat = below_and_above([v[:edge, :, lanes] for v in turns])
        lon = ordered(lon_odd, in_chip([v[:rows, :, lanes] for v in turns]), lon_b[:, :, lanes])
        inner = slice(REACH, rows - REACH)
        blank = jnp.zeros((REACH, CELLS, LANES), F32)
        for side in range(2):
            at = slice(side * (rows + REACH), side * (rows + REACH) + REACH)
            field[c, at, CELLS : CELLS + cells] = lat[side].reshape(REACH, cells, LANES)
            own = slice(side * (rows - REACH), side * (rows - REACH) + REACH)
            at = slice(own.start + REACH, own.stop + REACH)
            field[c, at, CELLS : CELLS + cells] = x_ref[own, :, lanes].astype(F32)
            own = slice(side * (cells - TILE), side * (cells - TILE) + TILE)
            at = slice(own.start + CELLS, own.stop + CELLS)
            field[c, 2 * REACH : rows, at] = x_ref[inner, own, lanes].astype(F32)
            span = slice(side * (CELLS + cells), side * (CELLS + cells) + CELLS)
            field[c, REACH : REACH + rows, span] = lon[side]
            for end in range(2):
                at = slice(end * (rows + REACH), end * (rows + REACH) + REACH)
                field[c, at, span] = blank
                hidden[c, end * rows : end * rows + REACH, side * cells : side * cells + CELLS] = blank
        span = cells - CELLS
        for i, at in enumerate((REACH, rows - REACH)):
            part = rows_in[i * REACH : (i + 1) * REACH, :, lanes].astype(F32)
            hidden[c, at : at + REACH, CELLS : CELLS + span] = part[:, :span]
        part = cells_in[:, :, lanes].astype(F32)
        at = slice(2 * REACH, rows - REACH)
        hidden[c, at, CELLS : 2 * CELLS] = part[:, :CELLS]
        hidden[c, at, cells - CELLS : cells] = part[:, CELLS:]

    def rims(ref, c, span):
        last = ref.shape[1] - 2 * REACH
        return jnp.concatenate([ref[c, : 2 * REACH, span], ref[c, last:, span]], 0)

    def first_rows(items):
        tall = [rims(field, c, slice(w * CELLS, w * CELLS + WINDOW)) for c, w in items]
        values = product(rim_toeplitz, 0, 2 * REACH, tall, [one[c] for c, w in items])
        for (c, w), value in zip(items, values):
            value = erf_gelu(value)
            hidden[c, :REACH, w * CELLS : (w + 1) * CELLS] = value[:REACH]
            hidden[c, rows:, w * CELLS : (w + 1) * CELLS] = value[REACH:]

    def first_sides(c, start):
        low, high = max(start, LAT_REACH), min(start + block, rows - LAT_REACH)
        at = slice(start + LAT_REACH, start + LAT_REACH + block + REACH)
        tall = [field[c, at, s : s + WINDOW] for s in (0, cells)]
        values = product(toeplitz, low, high, tall, [one[c]] * 2)
        for s, value in zip((0, cells), values):
            hidden[c, low + LAT_REACH : high + LAT_REACH, s : s + CELLS] = erf_gelu(value)

    def second_rows(c, pair):
        tall = [rims(hidden, c, slice(w * CELLS, w * CELLS + WINDOW)) for w in pair]
        values = product(wide_toeplitz, 0, 2 * REACH, tall, [two[c]] * 2)
        blank = jnp.zeros((2 * REACH, CELLS, LANES), F32)
        if pair == [1, columns - 3]:
            rim_out[:, :TILE, lanes_of(c)] = jnp.concatenate([blank, values[0]], 1).astype(BF16)
            rim_out[:, cells - TILE :, lanes_of(c)] = jnp.concatenate([values[1], blank], 1).astype(BF16)
        else:
            rim_out[:, pair[0] * CELLS : (pair[0] + 2) * CELLS, lanes_of(c)] = jnp.concatenate(values, 1).astype(BF16)

    def second_sides(c, start):
        low, high = max(start, REACH), min(start + block, rows - REACH)
        tall = [hidden[c, start : start + block + REACH, s : s + WINDOW] for s in (0, cells - CELLS)]
        values = product(toeplitz, low, high, tall, [two[c]] * 2)
        at = slice(low - REACH, high - REACH)
        inner = sides_in[at, :, lanes_of(c)].astype(F32)
        side_out[0, at, :, lanes_of(c)] = jnp.concatenate([values[0], inner[:, :CELLS]], 1).astype(BF16)
        side_out[1, at, :, lanes_of(c)] = jnp.concatenate([inner[:, CELLS:], values[1]], 1).astype(BF16)

    def export(c):
        for side in range(2):
            span = slice(side * (cells - CELLS), side * (cells - CELLS) + WINDOW)
            ends[side, :, :, lanes_of(c)] = rims(hidden, c, span).astype(BF16)

    part = functools.partial
    steps = [([part(load, c)], []) for c in range(chunks)]
    items = [(c, w) for c in range(chunks) for w in range(1, columns - 1)]
    for pair in pairs_of(items):
        steps[pair[-1][0]][0].append(part(first_rows, pair))
    for c in range(chunks - 1, 0, -1):
        if c * (columns - 2) % 2:
            steps[c - 1][0].extend([steps[c][0].pop(0), steps[c][0].pop(0)])
    starts = range(0, rows, block)
    for c, (first, second) in enumerate(steps):
        first.extend(part(first_sides, c, start) for start in starts)
        second.extend(
            part(second_rows, c, pair) for pair in [[1, columns - 3]] + pairs_of(list(range(2, columns - 3)))
        )
        second.extend(part(second_sides, c, start) for start in starts)
        second.append(part(export, c))
    run_mixed(steps)


def corner_kernel(
    x_ref, turn_0, turn_1, turn_2, lon_b, corner_b, corner_a, ends, rim_toeplitz, wide_toeplitz, one_ref, two_ref,
    side_out, rim_out, begun_ref, out_ref, corner_out, sems,
):
    del begun_ref
    rows, cells, channels = x_ref.shape
    chunks = channels // LANES
    edge = REACH * (cells // CELLS)
    inner = pl.ds(REACH, rows - 2 * REACH)
    ends_at = (pl.ds(0, REACH), pl.ds(rows - REACH, REACH))
    sides_at = (pl.ds(0, TILE), pl.ds(cells - TILE, TILE))
    span = pl.ds(TILE, cells - 2 * TILE)
    moves = []
    for i in range(2):
        moves.append((side_out.at[i], out_ref.at[inner, sides_at[i]]))
        moves.append((rim_out.at[pl.ds(i * REACH, REACH), span], out_ref.at[ends_at[i], span]))
    copies = [pltpu.make_async_copy(source, target, sems.at[i]) for i, (source, target) in enumerate(moves)]
    for copy in copies:
        copy.start()
    turns, lon_odd = (turn_0, turn_1, turn_2), lax.axis_index("lon") % 2 == 1
    one, two = lane_weights(one_ref, 0.5), lane_weights(two_ref)

    def first(c):
        lanes = lanes_of(c)
        lat = below_and_above([v[:edge, :, lanes] for v in turns])
        lon = ordered(lon_odd, in_chip([v[:rows, :, lanes] for v in turns]), lon_b[:, :, lanes])
        corner = ordered(lon_odd, corner_a[:, lanes], corner_b[:, lanes])
        tall = []
        for side in range(2):
            own = slice(side * (cells - CELLS), side * (cells - CELLS) + CELLS)
            above = [v.reshape(REACH, cells, LANES)[:, own] for v in lat]
            tiles = slice(side * (cells - TILE), side * (cells - TILE) + TILE)
            half = slice(side * (TILE - CELLS), side * (TILE - CELLS) + CELLS)
            mine = [x_ref[r : r + REACH, tiles, lanes].astype(F32)[:, half] for r in (0, rows - REACH)]
            near = lon[side]
            far = corner[side].reshape(2, REACH, CELLS, LANES)
            own = jnp.concatenate([above[0], mine[0], mine[1], above[1]], 0)
            other = jnp.concatenate([far[0], near[:REACH], near[rows - REACH :], far[1]], 0)
            tall.append(jnp.concatenate([own, other] if side else [other, own], 1))
        return [erf_gelu(v) for v in product(rim_toeplitz, 0, 2 * REACH, tall, [one[c]] * 2)]

    def second(c, blocks):
        lanes = lanes_of(c)
        tall = []
        for side in range(2):
            near = ends[side, :, :, lanes].astype(F32)
            own = near[:, side * CELLS : side * CELLS + CELLS]
            own = jnp.concatenate([blocks[side][:REACH], own[REACH : 3 * REACH], blocks[side][REACH:]], 0)
            tall.append(jnp.concatenate([near[:, :CELLS], own] if side else [own, near[:, CELLS:]], 1))
        values = product(wide_toeplitz, 0, 2 * REACH, tall, [two[c]] * 2)
        for side in range(2):
            tiles = slice(side * (cells - TILE), side * (cells - TILE) + TILE)
            near = rim_out[:, tiles, lanes].astype(F32)
            near = near[:, : TILE - CELLS] if side else near[:, CELLS:]
            whole = [near, values[side]] if side else [values[side], near]
            corner_out[side, :, :, lanes] = jnp.concatenate(whole, 1).astype(BF16)

    def leave(begin, end):
        lanes = pl.ds(begin * LANES, (end - begin) * LANES)
        for side in range(2):
            for row in range(2):
                source = corner_out.at[side, pl.ds(row * REACH, REACH), :, lanes]
                target = out_ref.at[ends_at[row], sides_at[side], lanes]
                copies.append(pltpu.make_async_copy(source, target, sems.at[len(copies)]))
                copies[-1].start()

    hidden = [first(c) for c in range(chunks)]
    early = max(chunks - 2, 1)
    for c in range(early):
        second(c, hidden[c])
    leave(0, early)
    for c in range(early, chunks):
        second(c, hidden[c])
    if early < chunks:
        leave(early, chunks)
    for copy in copies:
        copy.wait()


def per_device(state_field, filters, band_edges, basis_mask, weights_one, weights_two):
    rows, cells, channels = state_field.shape
    bases = filters.shape[1]
    group = bases * CELLS
    chunks = channels // LANES
    block = max(b for b in range(2, rows + 1, 2) if rows % b == 0 and (b + REACH) * WINDOW <= DEPTH)
    lat_peers, lon_peers = lax.axis_size("lat"), lax.axis_size("lon")
    turn, lon = lax.axis_index("lat") % TURNS, lax.axis_index("lon")

    anywhere = pl.BlockSpec(memory_space=pl.ANY)
    vmem = pl.BlockSpec(memory_space=pltpu.VMEM)
    params = pltpu.CompilerParams(vmem_limit_bytes=VMEM_BYTES)
    dma = pltpu.SemaphoreType.DMA

    def array(*shape, dtype=BF16):
        return jax.ShapeDtypeStruct(shape, dtype)

    def scratch(*shape, dtype=BF16):
        return pltpu.VMEM(shape, dtype)

    across = cells // CELLS
    edge = REACH * across
    filter_args = (filters.transpose(1, 3, 2, 0), band_edges.T, basis_mask.T)
    *turns, lon_b, lines = pl.pallas_call(
        prep_kernel,
        out_shape=(array(edge + 1, CELLS, channels),) * TURNS
        + (array(rows, CELLS, channels), scratch(bases, rows, LANES, dtype=F32)),
        in_specs=[anywhere] * 5,
        out_specs=(anywhere,) * (TURNS + 1) + (vmem,),
        scratch_shapes=[
            scratch(bases, filters.shape[3], BANDS, rows, dtype=F32),
            scratch(2, rows, dtype=jnp.int32), scratch(bases, rows, dtype=jnp.int32),
            scratch(TURNS, edge + 1, CELLS, channels), scratch(rows, CELLS, channels),
            scratch(bases, LANES, LANES, dtype=F32), scratch(2, CELLS, channels, dtype=F32),
            dma((7,)), dma((2 * TURNS + 1,)),
        ],
        compiler_params=pltpu.CompilerParams(vmem_limit_bytes=60 * 1024 * 1024),
        cost_estimate=pl.CostEstimate(flops=0, bytes_accessed=8 * REACH * cells * channels, transcendentals=0),
        name="prep",
    )(
        state_field.reshape(rows * across, CELLS, channels), state_field.reshape(rows, across, CELLS, channels),
        *filter_args,
    )
    both = ("lat", "lon")
    turns = [lax.ppermute(v, both, turn_swaps(lat_peers, lon_peers, j)) for j, v in enumerate(turns)]
    lon_b = lax.ppermute(lon_b, "lon", swaps(lon_peers, True))

    middle = rows - 2 * REACH
    flops = 2 * (2 * rows - 3 * REACH) * (cells - 2 * CELLS) * bases * DEPTH * channels
    cost = pl.CostEstimate(flops=flops, bytes_accessed=4 * state_field.size, transcendentals=0)
    toeplitz, known, wide, edge_rows, edge_cells, sides, begun = pl.pallas_call(
        functools.partial(inner_kernel, block),
        out_shape=(
            array(rows * group, DEPTH), array(2 * REACH * group, DEPTH), array(2 * REACH * group, DEPTH),
            array(2 * REACH, cells, channels), array(middle - REACH, TILE, channels),
            array(middle, TILE, channels), array(rows, cells, channels),
        ),
        in_specs=[vmem] * 4,
        out_specs=(vmem,) * 6 + (anywhere,),
        scratch_shapes=[
            scratch(middle, cells - 2 * TILE, channels),
            scratch(chunks, rows + REACH, cells, LANES, dtype=F32),
            scratch(chunks, rows + REACH, cells - CELLS, LANES, dtype=F32),
            scratch(chunks, middle, TILE, LANES, dtype=F32), dma((1,)),
        ],
        compiler_params=params,
        cost_estimate=cost,
        name="inner",
    )(state_field, lines, weights_one, weights_two)

    *turns, sides = lax.optimization_barrier((*turns, sides))

    def corner_send(leading, second):
        parts = [jnp.where(leading, v[:edge:across], v[across - 1 : edge : across]) for v in turns]
        below = jnp.where(turn == 1, parts[0], jnp.where(turn == 2, parts[1], parts[2]))
        above = jnp.where(turn == 0, parts[0], jnp.where(turn == 1, parts[1], parts[2]))
        sent = jnp.concatenate([below, above], 0).reshape(2 * REACH * CELLS, channels)
        return lax.ppermute(sent, "lon", swaps(lon_peers, second))

    corner_b = corner_send(lon % 2 == 0, True)
    corner_a = corner_send(lon % 2 == 1, False)
    rim_toeplitz, rim_out, side_out, ends = pl.pallas_call(
        functools.partial(rim_kernel, block),
        out_shape=(
            array(2 * REACH * group, DEPTH), array(2 * REACH, cells, channels), array(2, middle, TILE, channels),
            array(2, 4 * REACH, WINDOW, channels),
        ),
        in_specs=[vmem] * 13,
        out_specs=(vmem,) * 4,
        scratch_shapes=[
            scratch(chunks, rows + 2 * REACH, cells + 2 * CELLS, LANES, dtype=F32),
            scratch(chunks, rows + REACH, cells + CELLS, LANES, dtype=F32),
        ],
        compiler_params=params,
        cost_estimate=cost,
        name="rim",
    )(
        state_field, *turns, lon_b, edge_rows, edge_cells, sides,
        toeplitz, known, wide, weights_one, weights_two,
    )
    return pl.pallas_call(
        corner_kernel,
        out_shape=array(rows, cells, channels),
        in_specs=[vmem] * 14 + [anywhere],
        out_specs=anywhere,
        input_output_aliases={14: 0},
        scratch_shapes=[scratch(2, 2 * REACH, TILE, channels), dma((12,))],
        compiler_params=params,
        cost_estimate=cost,
        name="corner",
    )(
        state_field, *turns, lon_b, corner_b, corner_a, ends, rim_toeplitz, wide,
        weights_one, weights_two, side_out, rim_out, begun,
    )


def solution(mesh):
    placed = (
        P("lat", "lon", None),
        P("lat", None, None, None),
        P("lat", None),
        P("lat", None),
        P(),
        P(),
    )
    return jax.shard_map(
        per_device, mesh=mesh, in_specs=placed, out_specs=P("lat", "lon", None), check_vma=False
    )
```

```python
import functools

import jax
import jax.numpy as jnp
from jax import lax
from jax.experimental import pallas as pl
from jax.experimental.pallas import tpu as pltpu
from jax.sharding import PartitionSpec as P

LAT_REACH = 2
LON_REACH = 4
REACH = 2 * LAT_REACH
BANDS = 2 * LAT_REACH + 1
CELLS = 8
WINDOW = CELLS + 2 * LON_REACH
LANES = 128
DEPTH = 2 * LANES
TILE = 16
VMEM_BYTES = 20 * 1024 * 1024
TURNS = 3
PIECE = 4
F32, BF16 = jnp.float32, jnp.bfloat16

ERF_SERIES = (
    1.5956562720156744,
    0.2917503271976864,
    -0.003995570947534282,
    -0.003914369984884403,
    0.0005729703632347449,
)


def erf_gelu(half):
    square = half * half
    series = ERF_SERIES[-1] * square + ERF_SERIES[-2]
    for term in ERF_SERIES[-3::-1]:
        series = series * square + term
    return half + half * jnp.tanh(half * series)


def swaps(peers, second):
    pairs = [(i, i + 1) for i in range(1 if second else 0, peers - 1, 2)]
    if second:
        pairs.append((peers - 1, 0))
    return pairs + [(j, i) for i, j in pairs]


def turn_swaps(peers, width, turn):
    pairs = [(i, i + 1) for i in range(peers - 1) if i % TURNS == turn]
    pairs += [(j, i) for i, j in pairs]
    alone = set(range(peers)) - {i for i, _ in pairs}
    result = [(i * width + k, j * width + k) for i, j in pairs for k in range(width)]
    return result + [(i * width + k, i * width + (k ^ 1)) for i in sorted(alone) for k in range(width)]


def pairs_of(items):
    return [items[i : i + 2] for i in range(0, len(items), 2)]


def lanes_of(chunk):
    return slice(chunk * LANES, (chunk + 1) * LANES)


def fill_toeplitz(toeplitz, line_of, rows, bases, place_of, pairs=None):
    group = bases * CELLS
    blank = jnp.zeros((CELLS, DEPTH - LANES), F32)
    for row in pairs or range(0, rows, 2):
        parts = []
        for r in (row, row + 1):
            for basis in range(bases):
                line = jnp.broadcast_to(line_of(r, basis), (CELLS, LANES))
                line = jnp.concatenate([line, blank], 1)
                parts.append(pltpu.roll(line, place_of(r) * WINDOW, 1, stride=1, stride_axis=0))
        toeplitz[row * group : (row + 2) * group, :] = jnp.concatenate(parts, 0).astype(BF16)


def lane_weights(ref, scale=1.0):
    bases, channels = ref.shape
    return [[ref[k : k + 1, lanes_of(c)] * scale for k in range(bases)] for c in range(channels // LANES)]


def product(matrix, low, high, windows, weights):
    wide = [w.astype(BF16).reshape(DEPTH, LANES) for w in windows]
    wide = jnp.concatenate(wide, 1)
    bases = len(weights[0])
    group = bases * CELLS
    scales = [jnp.concatenate([w[k] for w in weights], 1) for k in range(bases)]
    pieces = []
    for at in range(low, high, PIECE):
        to = min(at + PIECE, high)
        result = jnp.dot(matrix[at * group : to * group, :], wide, preferred_element_type=F32)
        result = result.reshape(to - at, bases, CELLS, len(windows) * LANES)
        total = result[:, 0] * scales[0]
        for k in range(1, bases):
            total = total + result[:, k] * scales[k]
        pieces.append(total)
    total = jnp.concatenate(pieces, 0) if len(pieces) > 1 else pieces[0]
    return [total[:, :, i * LANES : (i + 1) * LANES] for i in range(len(windows))]


def run_mixed(steps):
    waiting = []
    for first, second in steps:
        total, done = len(waiting), 0
        for i, unit in enumerate(first):
            unit()
            while done * len(first) < total * (i + 1):
                waiting.pop(0)()
                done += 1
        for unit in waiting:
            unit()
        waiting = list(second)
    for unit in waiting:
        unit()


def line_choice(lags):
    at = lax.broadcasted_iota(jnp.int32, (LANES, LANES), 0)
    lane = lax.broadcasted_iota(jnp.int32, (LANES, LANES), 1)
    chosen = (at // 8 == lane % WINDOW) & (at % 8 == lane // WINDOW) & (at % 8 < BANDS) & (at // 8 < lags)
    return jnp.where(chosen, 1.0, 0.0).astype(BF16)


def filter_lines(filter_ref, edge_ref, mask_ref, padded, chosen):
    bases, lags, bands, rows = filter_ref.shape
    source = lax.axis_index("lat") * rows + lax.broadcasted_iota(jnp.int32, (bands, rows), 1) - LAT_REACH
    source = source + lax.broadcasted_iota(jnp.int32, (bands, rows), 0)
    inside = (source >= edge_ref[0:1, :]) & (source < edge_ref[1:2, :])
    for k in range(bases):
        keep = inside & (mask_ref[k : k + 1, :] != 0)
        for m in range(lags):
            padded[k, m * 8 : m * 8 + bands, :rows] = jnp.where(keep, filter_ref[k, m], 0.0)
    return [jnp.dot(padded[k].T.astype(BF16), chosen, preferred_element_type=F32) for k in range(bases)]


def prep_kernel(
    flat_ref, groups_ref, filter_in, edge_in, mask_in, turn_0, turn_1, turn_2, lon_b, lines_ref,
    filter_ref, edge_ref, mask_ref, payloads, far, padded, tags, sems, out_sems,
):
    bases, lags, bands, rows = filter_in.shape
    across = groups_ref.shape[1]
    edge = REACH * across
    turn, lon_odd = lax.axis_index("lat") % TURNS, lax.axis_index("lon") % 2
    small = [
        pltpu.make_async_copy(filter_in, filter_ref, sems.at[0]),
        pltpu.make_async_copy(edge_in, edge_ref, sems.at[1]),
        pltpu.make_async_copy(mask_in, mask_ref, sems.at[2]),
    ]
    last, first = pl.ds((rows - REACH) * across, edge), pl.ds(0, edge)
    near_at, far_at = (1 - lon_odd) * (across - 1), lon_odd * (across - 1)
    copies = [
        pltpu.make_async_copy(flat_ref.at[last], payloads.at[0, pl.ds(0, edge)], sems.at[3]),
        pltpu.make_async_copy(flat_ref.at[first], payloads.at[1, pl.ds(0, edge)], sems.at[4]),
        pltpu.make_async_copy(groups_ref.at[:, near_at], payloads.at[2, pl.ds(0, rows)], sems.at[5]),
        pltpu.make_async_copy(groups_ref.at[:, far_at], far, sems.at[6]),
    ]
    for copy in copies + small:
        copy.start()
    padded[...] = jnp.zeros_like(padded)
    tags[...] = jnp.zeros_like(tags)
    payloads[2, rows:] = jnp.zeros((edge + 1 - rows,) + payloads.shape[2:], BF16)
    chosen = line_choice(lags)
    pending = []

    def send(source, target):
        pending.append(pltpu.make_async_copy(source, target, out_sems.at[len(pending)]))
        pending[-1].start()

    outs = [(out, (turn + TURNS - j) % TURNS) for j, out in enumerate((turn_0, turn_1, turn_2))]
    for copy in copies[:3]:
        copy.wait()
    for out, role in outs:
        send(payloads.at[role, pl.ds(0, edge)], out.at[pl.ds(0, edge)])
    copies[3].wait()
    send(far, lon_b)
    for copy in small:
        copy.wait()
    for k, line in enumerate(filter_lines(filter_ref, edge_ref, mask_ref, padded, chosen)):
        lines_ref[k] = line[:rows]
        tags[0, :LAT_REACH, lanes_of(k)] = line[rows - LAT_REACH : rows]
        tags[1, :LAT_REACH, lanes_of(k)] = line[:LAT_REACH]
    payloads[0, edge] = tags[0].astype(BF16)
    payloads[1, edge] = tags[1].astype(BF16)
    for out, role in outs:
        send(payloads.at[role, edge], out.at[edge])
    for copy in pending:
        copy.wait()


def place_of(r):
    return r if r < REACH else REACH + r


def inner_kernel(
    block, x_ref, lines_ref, one_ref, two_ref,
    toeplitz, rim_toeplitz, wide_toeplitz, edge_rows, edge_cells, sides, out_ref,
    middle, field, hidden, ends, sems,
):
    rows, cells, channels = x_ref.shape
    bases = one_ref.shape[0]
    chunks = channels // LANES
    lines = [lines_ref[k] for k in range(bases)]
    fill_toeplitz(toeplitz, lambda r, k: lines[k][r : r + 1, :], rows, bases, lambda r: r % block)
    kept = list(range(REACH)) + list(range(rows - REACH, rows))
    fill_toeplitz(wide_toeplitz, lambda r, k: lines[k][kept[r] : kept[r] + 1, :], 2 * REACH, bases, place_of)
    shifted = [r - LAT_REACH for r in range(REACH)] + [rows - LAT_REACH + r for r in range(REACH)]
    own = range(LAT_REACH, 2 * REACH - LAT_REACH, 2)
    rim_toeplitz[...] = jnp.zeros_like(rim_toeplitz)
    fill_toeplitz(
        rim_toeplitz, lambda r, k: lines[k][shifted[r] : shifted[r] + 1, :], 2 * REACH, bases, place_of, own
    )
    one, two = lane_weights(one_ref, 0.5), lane_weights(two_ref)
    starts = range(0, rows, block)
    windows = (cells - WINDOW) // CELLS + 1
    span = windows * CELLS

    def load(c):
        blank = jnp.zeros((LAT_REACH, cells, LANES), F32)
        field[c, :LAT_REACH] = blank
        field[c, LAT_REACH : LAT_REACH + rows] = x_ref[:, :, lanes_of(c)].astype(F32)
        field[c, LAT_REACH + rows :] = blank
        blank = jnp.zeros((REACH, span, LANES), F32)
        hidden[c, :REACH] = blank
        hidden[c, rows:] = blank

    def first(items, start):
        low, high = max(start, LAT_REACH), min(start + block, rows - LAT_REACH)
        tall = [field[c, start : start + block + REACH, w * CELLS : w * CELLS + WINDOW] for c, w in items]
        values = product(toeplitz, low, high, tall, [one[c] for c, w in items])
        for (c, w), value in zip(items, values):
            hidden[c, low + LAT_REACH : high + LAT_REACH, w * CELLS : (w + 1) * CELLS] = erf_gelu(value)

    def second(c, start, pair):
        low, high = max(start, REACH), min(start + block, rows - REACH)
        tall = [hidden[c, start : start + block + REACH, w * CELLS : w * CELLS + WINDOW] for w in pair]
        values = product(toeplitz, low, high, tall, [two[c]] * len(pair))
        at = slice(low - REACH, high - REACH)
        for w, value in zip(pair, values):
            if w in (0, windows - 2):
                ends[c, at, (w > 0) * CELLS : (w > 0) * CELLS + CELLS] = value
        if len(pair) == 2 and pair[0] > 0:
            span = slice((pair[0] - 1) * CELLS, (pair[0] + 1) * CELLS)
            middle[at, span, lanes_of(c)] = jnp.concatenate(values, 1).astype(BF16)

    def export(c):
        for i, row in enumerate((REACH, rows - REACH)):
            part = jnp.concatenate([hidden[c, row : row + REACH], jnp.zeros((REACH, cells - span, LANES), F32)], 1)
            edge_rows[i * REACH : (i + 1) * REACH, :, lanes_of(c)] = part.astype(BF16)
        part = hidden[c, 2 * REACH : rows - REACH]
        edge_cells[:, :, lanes_of(c)] = jnp.concatenate([part[:, :CELLS], part[:, span - CELLS :]], 1).astype(BF16)
        sides[:, :, lanes_of(c)] = ends[c].astype(BF16)

    part = functools.partial
    steps = [([part(load, c)], []) for c in range(chunks)]
    for items in pairs_of([(c, w) for c in range(chunks) for w in range(windows)]):
        steps[items[-1][0]][0].extend(part(first, items, start) for start in starts)
    for c in range(chunks):
        pairs = [[0, windows - 2]] + pairs_of(list(range(1, windows - 2)))
        steps[c][1].extend(part(second, c, start, pair) for start in starts for pair in pairs)
        steps[c][1].append(part(export, c))
    for c in range(chunks - 1, 0, -1):
        if c * windows % 2:
            straddle = steps[c][0][1 : 1 + len(starts)]
            steps[c][0][1 : 1 + len(starts)] = []
            steps[c - 1][0].extend([steps[c][0].pop(0)] + straddle)
    run_mixed(steps)
    target = out_ref.at[pl.ds(REACH, rows - 2 * REACH), pl.ds(TILE, cells - 2 * TILE)]
    copy = pltpu.make_async_copy(middle, target, sems.at[0])
    copy.start()
    copy.wait()


def ordered(odd, a, b):
    return jnp.where(odd, a, b).astype(F32), jnp.where(odd, b, a).astype(F32)


def pick(received, turn):
    value = received[-1]
    for j in range(TURNS - 1):
        value = jnp.where(turn == j, received[j], value)
    return value


def below_and_above(received):
    turn = lax.axis_index("lat") % TURNS
    return pick(received, (turn + TURNS - 1) % TURNS).astype(F32), pick(received, turn).astype(F32)


def in_chip(received):
    return pick(received, (lax.axis_index("lat") + 1) % TURNS)


def rim_kernel(
    block, x_ref, turn_0, turn_1, turn_2, lon_b, rows_in, cells_in, sides_in,
    toeplitz, known_toeplitz, wide_toeplitz, one_ref, two_ref,
    rim_toeplitz, rim_out, side_out, ends, field, hidden,
):
    rows, cells, channels = x_ref.shape
    bases = one_ref.shape[0]
    chunks = channels // LANES
    group = bases * CELLS
    edge = REACH * (cells // CELLS)
    columns = cells // CELLS + 1
    turns, lon_odd = (turn_0, turn_1, turn_2), lax.axis_index("lon") % 2 == 1
    one, two = lane_weights(one_ref, 0.5), lane_weights(two_ref)
    tags = below_and_above([v[edge] for v in turns])

    def tag_line(r, k):
        at = r % LAT_REACH
        return tags[0 if r < REACH else 1][at : at + 1, lanes_of(k)]

    own = slice(LAT_REACH * group, (2 * REACH - LAT_REACH) * group)
    rim_toeplitz[own, :] = known_toeplitz[own, :]
    fill_toeplitz(rim_toeplitz, tag_line, 2 * REACH, bases, place_of, (0, 2 * REACH - LAT_REACH))

    def load(c):
        lanes = lanes_of(c)
        lat = below_and_above([v[:edge, :, lanes] for v in turns])
        lon = ordered(lon_odd, in_chip([v[:rows, :, lanes] for v in turns]), lon_b[:, :, lanes])
        inner = slice(REACH, rows - REACH)
        blank = jnp.zeros((REACH, CELLS, LANES), F32)
        for side in range(2):
            at = slice(side * (rows + REACH), side * (rows + REACH) + REACH)
            field[c, at, CELLS : CELLS + cells] = lat[side].reshape(REACH, cells, LANES)
            own = slice(side * (rows - REACH), side * (rows - REACH) + REACH)
            at = slice(own.start + REACH, own.stop + REACH)
            field[c, at, CELLS : CELLS + cells] = x_ref[own, :, lanes].astype(F32)
            own = slice(side * (cells - TILE), side * (cells - TILE) + TILE)
            at = slice(own.start + CELLS, own.stop + CELLS)
            field[c, 2 * REACH : rows, at] = x_ref[inner, own, lanes].astype(F32)
            span = slice(side * (CELLS + cells), side * (CELLS + cells) + CELLS)
            field[c, REACH : REACH + rows, span] = lon[side]
            for end in range(2):
                at = slice(end * (rows + REACH), end * (rows + REACH) + REACH)
                field[c, at, span] = blank
                hidden[c, end * rows : end * rows + REACH, side * cells : side * cells + CELLS] = blank
        span = cells - CELLS
        for i, at in enumerate((REACH, rows - REACH)):
            part = rows_in[i * REACH : (i + 1) * REACH, :, lanes].astype(F32)
            hidden[c, at : at + REACH, CELLS : CELLS + span] = part[:, :span]
        part = cells_in[:, :, lanes].astype(F32)
        at = slice(2 * REACH, rows - REACH)
        hidden[c, at, CELLS : 2 * CELLS] = part[:, :CELLS]
        hidden[c, at, cells - CELLS : cells] = part[:, CELLS:]

    def rims(ref, c, span):
        last = ref.shape[1] - 2 * REACH
        return jnp.concatenate([ref[c, : 2 * REACH, span], ref[c, last:, span]], 0)

    def first_rows(items):
        tall = [rims(field, c, slice(w * CELLS, w * CELLS + WINDOW)) for c, w in items]
        values = product(rim_toeplitz, 0, 2 * REACH, tall, [one[c] for c, w in items])
        for (c, w), value in zip(items, values):
            value = erf_gelu(value)
            hidden[c, :REACH, w * CELLS : (w + 1) * CELLS] = value[:REACH]
            hidden[c, rows:, w * CELLS : (w + 1) * CELLS] = value[REACH:]

    def first_sides(c, start):
        low, high = max(start, LAT_REACH), min(start + block, rows - LAT_REACH)
        at = slice(start + LAT_REACH, start + LAT_REACH + block + REACH)
        tall = [field[c, at, s : s + WINDOW] for s in (0, cells)]
        values = product(toeplitz, low, high, tall, [one[c]] * 2)
        for s, value in zip((0, cells), values):
            hidden[c, low + LAT_REACH : high + LAT_REACH, s : s + CELLS] = erf_gelu(value)

    def second_rows(c, pair):
        tall = [rims(hidden, c, slice(w * CELLS, w * CELLS + WINDOW)) for w in pair]
        values = product(wide_toeplitz, 0, 2 * REACH, tall, [two[c]] * 2)
        blank = jnp.zeros((2 * REACH, CELLS, LANES), F32)
        if pair == [1, columns - 3]:
            rim_out[:, :TILE, lanes_of(c)] = jnp.concatenate([blank, values[0]], 1).astype(BF16)
            rim_out[:, cells - TILE :, lanes_of(c)] = jnp.concatenate([values[1], blank], 1).astype(BF16)
        else:
            rim_out[:, pair[0] * CELLS : (pair[0] + 2) * CELLS, lanes_of(c)] = jnp.concatenate(values, 1).astype(BF16)

    def second_sides(c, start):
        low, high = max(start, REACH), min(start + block, rows - REACH)
        tall = [hidden[c, start : start + block + REACH, s : s + WINDOW] for s in (0, cells - CELLS)]
        values = product(toeplitz, low, high, tall, [two[c]] * 2)
        at = slice(low - REACH, high - REACH)
        inner = sides_in[at, :, lanes_of(c)].astype(F32)
        side_out[0, at, :, lanes_of(c)] = jnp.concatenate([values[0], inner[:, :CELLS]], 1).astype(BF16)
        side_out[1, at, :, lanes_of(c)] = jnp.concatenate([inner[:, CELLS:], values[1]], 1).astype(BF16)

    def export(c):
        for side in range(2):
            span = slice(side * (cells - CELLS), side * (cells - CELLS) + WINDOW)
            ends[side, :, :, lanes_of(c)] = rims(hidden, c, span).astype(BF16)

    part = functools.partial
    steps = [([part(load, c)], []) for c in range(chunks)]
    items = [(c, w) for c in range(chunks) for w in range(1, columns - 1)]
    for pair in pairs_of(items):
        steps[pair[-1][0]][0].append(part(first_rows, pair))
    for c in range(chunks - 1, 0, -1):
        if c * (columns - 2) % 2:
            steps[c - 1][0].extend([steps[c][0].pop(0), steps[c][0].pop(0)])
    starts = range(0, rows, block)
    for c, (first, second) in enumerate(steps):
        first.extend(part(first_sides, c, start) for start in starts)
        second.extend(
            part(second_rows, c, pair) for pair in [[1, columns - 3]] + pairs_of(list(range(2, columns - 3)))
        )
        second.extend(part(second_sides, c, start) for start in starts)
        second.append(part(export, c))
    run_mixed(steps)


def corner_kernel(
    x_ref, turn_0, turn_1, turn_2, lon_b, corner_b, corner_a, ends, rim_toeplitz, wide_toeplitz, one_ref, two_ref,
    side_out, rim_out, begun_ref, out_ref, corner_out, sems,
):
    del begun_ref
    rows, cells, channels = x_ref.shape
    chunks = channels // LANES
    edge = REACH * (cells // CELLS)
    inner = pl.ds(REACH, rows - 2 * REACH)
    ends_at = (pl.ds(0, REACH), pl.ds(rows - REACH, REACH))
    sides_at = (pl.ds(0, TILE), pl.ds(cells - TILE, TILE))
    span = pl.ds(TILE, cells - 2 * TILE)
    moves = []
    for i in range(2):
        moves.append((side_out.at[i], out_ref.at[inner, sides_at[i]]))
        moves.append((rim_out.at[pl.ds(i * REACH, REACH), span], out_ref.at[ends_at[i], span]))
    copies = [pltpu.make_async_copy(source, target, sems.at[i]) for i, (source, target) in enumerate(moves)]
    for copy in copies:
        copy.start()
    turns, lon_odd = (turn_0, turn_1, turn_2), lax.axis_index("lon") % 2 == 1
    one, two = lane_weights(one_ref, 0.5), lane_weights(two_ref)

    def first(c):
        lanes = lanes_of(c)
        lat = below_and_above([v[:edge, :, lanes] for v in turns])
        lon = ordered(lon_odd, in_chip([v[:rows, :, lanes] for v in turns]), lon_b[:, :, lanes])
        corner = ordered(lon_odd, corner_a[:, lanes], corner_b[:, lanes])
        tall = []
        for side in range(2):
            own = slice(side * (cells - CELLS), side * (cells - CELLS) + CELLS)
            above = [v.reshape(REACH, cells, LANES)[:, own] for v in lat]
            tiles = slice(side * (cells - TILE), side * (cells - TILE) + TILE)
            half = slice(side * (TILE - CELLS), side * (TILE - CELLS) + CELLS)
            mine = [x_ref[r : r + REACH, tiles, lanes].astype(F32)[:, half] for r in (0, rows - REACH)]
            near = lon[side]
            far = corner[side].reshape(2, REACH, CELLS, LANES)
            own = jnp.concatenate([above[0], mine[0], mine[1], above[1]], 0)
            other = jnp.concatenate([far[0], near[:REACH], near[rows - REACH :], far[1]], 0)
            tall.append(jnp.concatenate([own, other] if side else [other, own], 1))
        return [erf_gelu(v) for v in product(rim_toeplitz, 0, 2 * REACH, tall, [one[c]] * 2)]

    def second(c, blocks):
        lanes = lanes_of(c)
        tall = []
        for side in range(2):
            near = ends[side, :, :, lanes].astype(F32)
            own = near[:, side * CELLS : side * CELLS + CELLS]
            own = jnp.concatenate([blocks[side][:REACH], own[REACH : 3 * REACH], blocks[side][REACH:]], 0)
            tall.append(jnp.concatenate([near[:, :CELLS], own] if side else [own, near[:, CELLS:]], 1))
        values = product(wide_toeplitz, 0, 2 * REACH, tall, [two[c]] * 2)
        for side in range(2):
            tiles = slice(side * (cells - TILE), side * (cells - TILE) + TILE)
            near = rim_out[:, tiles, lanes].astype(F32)
            near = near[:, : TILE - CELLS] if side else near[:, CELLS:]
            whole = [near, values[side]] if side else [values[side], near]
            corner_out[side, :, :, lanes] = jnp.concatenate(whole, 1).astype(BF16)

    def leave(begin, end):
        lanes = pl.ds(begin * LANES, (end - begin) * LANES)
        for side in range(2):
            for row in range(2):
                source = corner_out.at[side, pl.ds(row * REACH, REACH), :, lanes]
                target = out_ref.at[ends_at[row], sides_at[side], lanes]
                copies.append(pltpu.make_async_copy(source, target, sems.at[len(copies)]))
                copies[-1].start()

    hidden = [first(c) for c in range(chunks)]
    early = max(chunks - 2, 1)
    for c in range(early):
        second(c, hidden[c])
    leave(0, early)
    for c in range(early, chunks):
        second(c, hidden[c])
    if early < chunks:
        leave(early, chunks)
    for copy in copies:
        copy.wait()


def per_device(state_field, filters, band_edges, basis_mask, weights_one, weights_two):
    rows, cells, channels = state_field.shape
    bases = filters.shape[1]
    group = bases * CELLS
    chunks = channels // LANES
    block = max(b for b in range(2, rows + 1, 2) if rows % b == 0 and (b + REACH) * WINDOW <= DEPTH)
    lat_peers, lon_peers = lax.axis_size("lat"), lax.axis_size("lon")
    turn, lon = lax.axis_index("lat") % TURNS, lax.axis_index("lon")

    anywhere = pl.BlockSpec(memory_space=pl.ANY)
    vmem = pl.BlockSpec(memory_space=pltpu.VMEM)
    params = pltpu.CompilerParams(vmem_limit_bytes=VMEM_BYTES)
    dma = pltpu.SemaphoreType.DMA

    def array(*shape, dtype=BF16):
        return jax.ShapeDtypeStruct(shape, dtype)

    def scratch(*shape, dtype=BF16):
        return pltpu.VMEM(shape, dtype)

    across = cells // CELLS
    edge = REACH * across
    filter_args = (filters.transpose(1, 3, 2, 0), band_edges.T, basis_mask.T)
    *turns, lon_b, lines = pl.pallas_call(
        prep_kernel,
        out_shape=(array(edge + 1, CELLS, channels),) * TURNS
        + (array(rows, CELLS, channels), scratch(bases, rows, LANES, dtype=F32)),
        in_specs=[anywhere] * 5,
        out_specs=(anywhere,) * (TURNS + 1) + (vmem,),
        scratch_shapes=[
            scratch(bases, filters.shape[3], BANDS, rows, dtype=F32),
            scratch(2, rows, dtype=jnp.int32), scratch(bases, rows, dtype=jnp.int32),
            scratch(TURNS, edge + 1, CELLS, channels), scratch(rows, CELLS, channels),
            scratch(bases, LANES, LANES, dtype=F32), scratch(2, CELLS, channels, dtype=F32),
            dma((7,)), dma((2 * TURNS + 1,)),
        ],
        compiler_params=pltpu.CompilerParams(vmem_limit_bytes=60 * 1024 * 1024),
        cost_estimate=pl.CostEstimate(flops=0, bytes_accessed=8 * REACH * cells * channels, transcendentals=0),
        name="prep",
    )(
        state_field.reshape(rows * across, CELLS, channels), state_field.reshape(rows, across, CELLS, channels),
        *filter_args,
    )
    both = ("lat", "lon")
    turns = [lax.ppermute(v, both, turn_swaps(lat_peers, lon_peers, j)) for j, v in enumerate(turns)]
    lon_b = lax.ppermute(lon_b, "lon", swaps(lon_peers, True))

    middle = rows - 2 * REACH
    flops = 2 * (2 * rows - 3 * REACH) * (cells - 2 * CELLS) * bases * DEPTH * channels
    cost = pl.CostEstimate(flops=flops, bytes_accessed=4 * state_field.size, transcendentals=0)
    toeplitz, known, wide, edge_rows, edge_cells, sides, begun = pl.pallas_call(
        functools.partial(inner_kernel, block),
        out_shape=(
            array(rows * group, DEPTH), array(2 * REACH * group, DEPTH), array(2 * REACH * group, DEPTH),
            array(2 * REACH, cells, channels), array(middle - REACH, TILE, channels),
            array(middle, TILE, channels), array(rows, cells, channels),
        ),
        in_specs=[vmem] * 4,
        out_specs=(vmem,) * 6 + (anywhere,),
        scratch_shapes=[
            scratch(middle, cells - 2 * TILE, channels),
            scratch(chunks, rows + REACH, cells, LANES, dtype=F32),
            scratch(chunks, rows + REACH, cells - CELLS, LANES, dtype=F32),
            scratch(chunks, middle, TILE, LANES, dtype=F32), dma((1,)),
        ],
        compiler_params=params,
        cost_estimate=cost,
        name="inner",
    )(state_field, lines, weights_one, weights_two)

    *turns, sides = lax.optimization_barrier((*turns, sides))

    def corner_send(leading, second):
        parts = [jnp.where(leading, v[:edge:across], v[across - 1 : edge : across]) for v in turns]
        below = jnp.where(turn == 1, parts[0], jnp.where(turn == 2, parts[1], parts[2]))
        above = jnp.where(turn == 0, parts[0], jnp.where(turn == 1, parts[1], parts[2]))
        sent = jnp.concatenate([below, above], 0).reshape(2 * REACH * CELLS, channels)
        return lax.ppermute(sent, "lon", swaps(lon_peers, second))

    corner_b = corner_send(lon % 2 == 0, True)
    corner_a = corner_send(lon % 2 == 1, False)
    rim_toeplitz, rim_out, side_out, ends = pl.pallas_call(
        functools.partial(rim_kernel, block),
        out_shape=(
            array(2 * REACH * group, DEPTH), array(2 * REACH, cells, channels), array(2, middle, TILE, channels),
            array(2, 4 * REACH, WINDOW, channels),
        ),
        in_specs=[vmem] * 13,
        out_specs=(vmem,) * 4,
        scratch_shapes=[
            scratch(chunks, rows + 2 * REACH, cells + 2 * CELLS, LANES, dtype=F32),
            scratch(chunks, rows + REACH, cells + CELLS, LANES, dtype=F32),
        ],
        compiler_params=params,
        cost_estimate=cost,
        name="rim",
    )(
        state_field, *turns, lon_b, edge_rows, edge_cells, sides,
        toeplitz, known, wide, weights_one, weights_two,
    )
    return pl.pallas_call(
        corner_kernel,
        out_shape=array(rows, cells, channels),
        in_specs=[vmem] * 14 + [anywhere],
        out_specs=anywhere,
        input_output_aliases={14: 0},
        scratch_shapes=[scratch(2, 2 * REACH, TILE, channels), dma((12,))],
        compiler_params=params,
        cost_estimate=cost,
        name="corner",
    )(
        state_field, *turns, lon_b, corner_b, corner_a, ends, rim_toeplitz, wide,
        weights_one, weights_two, side_out, rim_out, begun,
    )


def solution(mesh):
    placed = (
        P("lat", "lon", None),
        P("lat", None, None, None),
        P("lat", None),
        P("lat", None),
        P(),
        P(),
    )
    return jax.shard_map(
        per_device, mesh=mesh, in_specs=placed, out_specs=P("lat", "lon", None), check_vma=False
    )
```
